128 devices in a mesh: gx: 4 (over x), gy: 32 (over z, y, core).
Axes of the slice: x: 4, y: 4, z: 4, core: 2. Of those that a mesh axis runs over, the one named last changes fastest.
Arguments:
- a_tiles: float32 [6144, 3, 128, 128], P(('gx', 'gy')), may hold values from -0.5 to 0.5
- a_cols: int32 [6144, 3], P(('gx', 'gy')), may hold values from 0 to 6143, as said below
- a_len: int32 [6144], P(('gx', 'gy')), may hold values from 1 to 3, as said below
- p_tiles: float32 [6144, 2, 128, 128], P(('gx', 'gy')), may hold values from -1 to 1
- aggregate: int32 [6144], replicated, may hold values from 0 to 2047, as said below
- owner: int32 [2048], replicated, may hold values from 0 to 127, as said below
Outputs:
- coarse_operator: float32 [2048, 7, 128, 128], P(('gx', 'gy'))
The draws below stay inside these ranges and needn't reach their ends.
Inputs may be any that keep to these rules, and one draw needn't show every extreme that they name: For k < a_len[i] the a_cols[i, k] are distinct among i - 1, i, i + 1 modulo 6144, the first being i; the later slots hold the remaining ones of these and belong to no operator. a_len[i] = 3 where i mod 48 is 0 or 47. aggregate[i] is i // 3 or i // 3 - 1, modulo 2048. The owner of row r of the 16 coarse rows of the device at (x, y) is the device at ((x + u[r]) mod 4, (v[y] + t[r]) mod 32), where u takes each value 16 // 4 times, v is a permutation and t takes no value more than 1 times, that many in every draw; each device owns exactly 16 coarse rows.
All inputs are finite; a program needn't handle non-finite values.
Results may differ from the reference program's by a relative error of at most 0.0003.
Values sent between devices are 32-bit elements; how exact they have to be, the bound alone decides.
No kernel may reach another device: no remote copies, remote signals or barrier semaphores. Data moves between devices by JAX's collectives and lax.ppermute only.
A program may use at most 192 MiB of HBM per device.

```python
import jax
import jax.numpy as jnp
from jax import lax

B = 128
RB = 48
KA = 3
RA = 1
KP = 2
AWIN = 5
CWIN = 7
CB = 16
S = 1
NB = 6144
NC = 2048
N_GX = 4
N_GY = 32


def fine_pattern(key):
    length_key, order_key = jax.random.split(key)
    lengths = jax.random.randint(length_key, (NB,), 1, KA + 1)
    within = jnp.arange(NB) % RB
    lengths = jnp.where((within == 0) | (within == RB - 1), KA, lengths)
    scores = jax.random.randint(order_key, (NB, KA), 0, 1 << 20) * KA + jnp.arange(KA)
    scores = jnp.where(jnp.arange(KA)[None, :] == RA, -1, scores)
    ordered = jnp.argsort(scores, axis=1, stable=True)
    columns = (jnp.arange(NB)[:, None] + ordered - RA) % NB
    return (lengths.astype(jnp.int32), columns.astype(jnp.int32))


def draw_a_cols(key, part):
    return fine_pattern(key)[1]


def draw_a_len(key, part):
    return fine_pattern(key)[0]


def draw_aggregate(key, part):
    key = jax.random.fold_in(key, 5)
    rows = jnp.arange(NB)
    return ((rows // 3 + jax.random.randint(key, (NB,), -1, 1)) % NC).astype(jnp.int32)


def draw_owner(key, part):
    key = jax.random.fold_in(key, 7)
    slab_key, column_key, spread_key = jax.random.split(key, 3)
    shift_x = jax.random.permutation(slab_key, CB) % N_GX
    shift_y = jax.random.permutation(spread_key, N_GY * S)[:CB] % N_GY
    mixing = jax.random.permutation(column_key, N_GY)
    rows = jnp.arange(NC)
    device = rows // CB
    local = rows % CB
    place_x = (device // N_GY + shift_x[local]) % N_GX
    place_y = (mixing[device % N_GY] + shift_y[local]) % N_GY
    return (place_x * N_GY + place_y).astype(jnp.int32)


def shard_levels(own_key, dims, shards, low, largest):
    loudness = 1.0
    for dim, blocks in shards:
        steps = jax.random.uniform(jax.random.fold_in(jax.random.fold_in(own_key, 6), dim), (blocks,), jnp.float32, low / len(shards), largest / len(shards))
        loudness = loudness * jnp.repeat(jnp.exp(steps), dims[dim] // blocks).reshape((-1,) + (1,) * (len(dims) - 1 - dim))
    return loudness


def centred(stream_key, shape, width, most, shards=(), kind=jnp.bfloat16):
    values = jax.random.normal(stream_key, shape, jnp.float32) * width
    if len(shards) > 0:
        values = shard_levels(stream_key, shape, shards, -0.22, 0.18) * values
    return jnp.clip(values, min=-most, max=most).astype(kind)


def setup_inputs(seed: int = 0) -> dict:
    splits = jax.random.split(jax.random.key(seed), 7)
    return {
        "a_tiles": centred(splits[0], (NB, KA, B, B), B ** -0.5, 0.5, ((0, 128),), jnp.float32),
        "a_cols": draw_a_cols(jax.random.fold_in(splits[6], 71), 0),
        "a_len": draw_a_len(jax.random.fold_in(splits[6], 71), 0),
        "p_tiles": centred(splits[3], (NB, KP, B, B), (B // 4) ** -0.5, 1.0, ((0, 128),), jnp.float32),
        "aggregate": draw_aggregate(jax.random.fold_in(splits[6], 71), 0),
        "owner": draw_owner(jax.random.fold_in(splits[6], 71), 0),
    }


highest = lax.Precision.HIGHEST


def reference(a_tiles, a_cols, a_len, p_tiles, aggregate, owner):
    p_cols = (aggregate[:, None] + jnp.arange(KP)[None, :]) % NC
    center = jnp.arange(NB) // 3
    active = jnp.arange(KA)[None, :] < a_len[:, None]

    def block(coarse, index):
        first = index * RB
        a_block = lax.dynamic_slice_in_dim(a_tiles, first, RB, 0)
        col_block = lax.dynamic_slice_in_dim(a_cols, first, RB, 0)
        act_block = lax.dynamic_slice_in_dim(active, first, RB, 0)
        cen_block = lax.dynamic_slice_in_dim(center, first, RB, 0)
        pc_block = lax.dynamic_slice_in_dim(p_cols, first, RB, 0)
        p_block = lax.dynamic_slice_in_dim(p_tiles, first, RB, 0)
        chosen = p_tiles[col_block]
        slots = (p_cols[col_block] - cen_block[:, None, None] + 2) % NC
        selector = ((slots[..., None] == jnp.arange(AWIN)) & act_block[:, :, None, None]).astype(jnp.float32)
        pieces = jnp.einsum("rkab,rkmbc->rkmac", a_block, chosen, precision=highest)
        applied = jnp.einsum("rkms,rkmac->rsac", selector, pieces, precision=highest)
        paired = jnp.einsum("rmba,rsbc->rmsac", p_block, applied, precision=highest)
        target_row = jnp.broadcast_to(pc_block[:, :, None], paired.shape[:3])
        target_col = (cen_block[:, None, None] + jnp.arange(AWIN) - 2 - pc_block[:, :, None] + 3) % NC
        return coarse.at[target_row, target_col].add(paired), None

    start = jnp.zeros((NC, CWIN, B, B), jnp.float32)
    coarse, unused = lax.scan(block, start, jnp.arange(NB // RB))
    return coarse[jnp.argsort(owner, stable=True)]
```

```python
import functools

import jax
import jax.numpy as jnp
from jax import lax
from jax.experimental import pallas as pl
from jax.experimental.pallas import tpu as pltpu
from jax.sharding import PartitionSpec as P

B = 128
KP = 2
CWIN = 7
W = 6
HALF = B // 2
BF = jnp.bfloat16
F32 = jnp.float32
SMEM = pltpu.SMEM
VMEM = pltpu.VMEM


def split(x):
    high = x.astype(BF)
    return high, (x - high.astype(F32)).astype(BF)


def left_operand(x):
    high, low = split(x)
    return jnp.concatenate([high, low, high], axis=1)


def right_operand(x):
    high, low = split(x)
    return jnp.concatenate([high, high, low], axis=0)


def matmul(left, right):
    return jnp.dot(left, right, preferred_element_type=F32)


def spread(total, flag, base, pair, slots):
    first, second = pair
    values = {
        base - 1: jnp.where(flag, first, 0.0),
        base: jnp.where(flag, second, first),
        base + 1: jnp.where(flag, 0.0, second),
    }
    for s, value in values.items():
        if s in slots:
            total[s] = value if total.get(s) is None else total[s] + value


def row_product(p_pair, tiles):
    turned = jnp.concatenate([p_pair[0].T, p_pair[1].T], axis=0)
    return matmul(left_operand(turned), right_operand(jnp.concatenate(tiles, axis=1)))


SLOTS = {0: (0, 1, 2, 3), 1: (1, 2, 3), 2: (1, 2, 3, 4)}


def main_kernel(
    flag_ref, left_ref, right_ref, lon_ref, ron_ref, slot_a, slot_b,
    a_ref, p_ref, before_ref, after_ref,
    out_a, out_b,
    stage, carry, sems,
):
    step = pl.program_id(0)
    steps = pl.num_programs(0) - 1
    buf = lax.rem(step, 2)

    def copies(at, which, row):
        c = 2 * at - 1 + row
        return (
            pltpu.make_async_copy(
                stage.at[which, row, :, pl.ds(0, HALF)], out_a.at[slot_a[c]], sems.at[which, row, 0]
            ),
            pltpu.make_async_copy(
                stage.at[which, row, :, pl.ds(HALF, HALF)], out_b.at[slot_b[c]], sems.at[which, row, 1]
            ),
        )

    def drain(at):
        which = lax.rem(at, 2)
        for row in range(2):
            @pl.when((2 * at - 1 + row >= 0) & (2 * at - 1 + row < 2 * steps))
            def _():
                for copy in copies(at, which, row):
                    copy.wait()

    @pl.when(step >= 2)
    def _():
        drain(step - 2)

    @pl.when(step == 0)
    def _():
        carry[...] = jnp.zeros_like(carry)

    stage[buf, 0] = carry[0]
    stage[buf, 1] = carry[1]

    @pl.when(step < steps)
    def _():
        carry[...] = jnp.zeros_like(carry)
        first = step * W
        flags = {q: flag_ref[first + q + 1] > 0 for q in range(-1, W + 1)}

        def p_tile(q, m):
            if q < 0:
                return before_ref[0, m]
            if q >= W:
                return after_ref[0, m]
            return p_ref[q, m]

        lefts = {}
        for r in range(W):
            tiles = {
                0: jnp.where(lon_ref[first + r] > 0, a_ref[r, left_ref[first + r]], 0.0),
                1: a_ref[r, 0],
                2: jnp.where(ron_ref[first + r] > 0, a_ref[r, right_ref[first + r]], 0.0),
            }
            for k in range(3):
                lefts[r, r + k - 1] = left_operand(tiles[k])
        total = {r: {} for r in range(W)}
        for q in range(-1, W + 1):
            rows = [r for r in (q - 1, q, q + 1) if 0 <= r < W]
            right = right_operand(jnp.concatenate([p_tile(q, 0), p_tile(q, 1)], axis=1))
            product = matmul(jnp.concatenate([lefts[r, q] for r in rows], axis=0), right)
            for n, r in enumerate(rows):
                pair = (product[n * B : (n + 1) * B, :B], product[n * B : (n + 1) * B, B:])
                spread(total[r], flags[q], q // 3 - r // 3 + 2, pair, SLOTS[r % 3])
        for r in range(W):
            slots = SLOTS[r % 3]
            product = row_product((p_ref[r, 0], p_ref[r, 1]), [total[r][s] for s in slots])
            g = r // 3
            for n, s in enumerate(slots):
                one = product[:B, n * B : (n + 1) * B]
                two = product[B:, n * B : (n + 1) * B]
                for delta, value in (
                    (-1, jnp.where(flags[r], one, 0.0)),
                    (0, jnp.where(flags[r], two, one)),
                    (1, jnp.where(flags[r], 0.0, two)),
                ):
                    place = g + delta + 1
                    if place < 2:
                        stage[buf, place, s + 1 - delta] += value
                    else:
                        carry[place - 2, s + 1 - delta] += value

    for row in range(2):
        @pl.when((2 * step - 1 + row >= 0) & (2 * step - 1 + row < 2 * steps))
        def _():
            for copy in copies(step, buf, row):
                copy.start()

    @pl.when(step == steps)
    def _():
        drain(step - 1)
        drain(step)


def main_product(meta, slot_a, slot_b, a_tiles, p_tiles, count_b):
    rows = a_tiles.shape[0]
    steps = rows // W
    coarse = rows // 3
    last = steps - 1

    def spec(shape, index):
        return pl.BlockSpec(shape, index)

    half = (CWIN, HALF, B)
    return pl.pallas_call(
        main_kernel,
        grid_spec=pltpu.PrefetchScalarGridSpec(
            num_scalar_prefetch=7,
            grid=(steps + 1,),
            in_specs=[
                spec((W, 3, B, B), lambda s, *_: (jnp.minimum(s, last), 0, 0, 0)),
                spec((W, KP, B, B), lambda s, *_: (jnp.minimum(s, last), 0, 0, 0)),
                spec((1, KP, B, B), lambda s, *_: (jnp.maximum(jnp.minimum(s, last) * W - 1, 0), 0, 0, 0)),
                spec((1, KP, B, B), lambda s, *_: (jnp.minimum(s * W + W, rows - 1), 0, 0, 0)),
            ],
            out_specs=[pl.BlockSpec(memory_space=pl.ANY)] * 2,
            scratch_shapes=[
                VMEM((2, 2, CWIN, B, B), F32),
                VMEM((2, CWIN, B, B), F32),
                pltpu.SemaphoreType.DMA((2, 2, 2)),
            ],
        ),
        out_shape=[
            jax.ShapeDtypeStruct((coarse,) + half, F32),
            jax.ShapeDtypeStruct((count_b,) + half, F32),
        ],
        compiler_params=pltpu.CompilerParams(
            dimension_semantics=("arbitrary",), vmem_limit_bytes=56 << 20
        ),
        cost_estimate=pl.CostEstimate(
            flops=16_000_000_000, bytes_accessed=24_000_000, transcendentals=0
        ),
        name="triple_product",
    )(*meta, slot_a, slot_b, a_tiles, p_tiles, p_tiles, p_tiles)


def edge_kernel(
    flag_ref, slot_a, slot_b,
    a_before, a_after, p_before, p_after, a_edge, p_first, p_last, in_a, in_b,
    out_a, out_b,
    rows_ref, sems,
):
    coarse = slot_a.shape[0]
    held = (0, 1, coarse - 2, coarse - 1)

    def copies(n, back):
        c = held[n]
        pairs = (
            (out_a.at[slot_a[c]], rows_ref.at[n, :, pl.ds(0, HALF)], sems.at[n, 0]),
            (out_b.at[slot_b[c]], rows_ref.at[n, :, pl.ds(HALF, HALF)], sems.at[n, 1]),
        )
        return [
            pltpu.make_async_copy(here, there, sem) if back else pltpu.make_async_copy(there, here, sem)
            for there, here, sem in pairs
        ]

    for n in range(4):
        for copy in copies(n, False):
            copy.start()

    sums = []
    for side in range(2):
        a_ref, p_ref = ((a_before, p_before), (a_after, p_after))[side]
        own_p = (p_first, p_last)[side]
        own_flag = flag_ref[(4, 5)[side]] > 0
        flags, tiles, p_at = {}, {}, {}
        for n in range(4):
            q = n - 1 if side == 0 else n
            flags[q] = flag_ref[(0, 6)[side] + n] > 0
            p_at[q] = (p_ref[n, 0], p_ref[n, 1])
        near = 3 if side == 0 else -1
        flags[near] = own_flag
        p_at[near] = (own_p[0, 0], own_p[0, 1])
        total = {r: {} for r in range(3)}
        total[near] = {}
        for q in range(-1, 4):
            rows = [r for r in (q - 1, q, q + 1) if 0 <= r < 3]
            lefts = [left_operand(a_ref[r, q - r + 1]) for r in rows]
            if q == (2 if side == 0 else 0):
                rows.append(near)
                lefts.append(left_operand(a_edge[side]))
            right = right_operand(jnp.concatenate(p_at[q], axis=1))
            product = matmul(jnp.concatenate(lefts, axis=0), right)
            for n, r in enumerate(rows):
                pair = (product[n * B : (n + 1) * B, :B], product[n * B : (n + 1) * B, B:])
                base = q // 3 - r // 3 + 2
                slots = SLOTS[r % 3] if r != near else (base - 1, base, base + 1)
                spread(total[r], flags[q], base, pair, slots)
        outer, inner = {}, {}

        def put(target, w, value):
            target[w] = value if w not in target else target[w] + value

        for r in range(3):
            slots = sorted(total[r])
            pick = 1 if side == 0 else 0
            turned = left_operand(p_at[r][pick].T)
            product = matmul(turned, right_operand(jnp.concatenate([total[r][s] for s in slots], axis=1)))
            for n, s in enumerate(slots):
                value = product[:, n * B : (n + 1) * B]
                if side == 0:
                    put(outer, s, jnp.where(flags[r], 0.0, value))
                else:
                    put(outer, s + 2, jnp.where(flags[r], value, 0.0))
        slots = sorted(total[near])
        product = row_product(p_at[near], [total[near][s] for s in slots])
        for n, s in enumerate(slots):
            one = product[:B, n * B : (n + 1) * B]
            two = product[B:, n * B : (n + 1) * B]
            put(outer, s + 1, jnp.where(own_flag, two, one))
            if side == 0:
                put(inner, s, jnp.where(own_flag, 0.0, two))
            else:
                put(inner, s + 2, jnp.where(own_flag, one, 0.0))
        sums.append((outer, inner))

    for n in range(4):
        for copy in copies(n, False):
            copy.wait()
    for n, target in ((0, sums[0][0]), (1, sums[0][1]), (2, sums[1][1]), (3, sums[1][0])):
        for w, value in target.items():
            rows_ref[n, w] += value
    for n in range(4):
        for copy in copies(n, True):
            copy.start()
    for n in range(4):
        for copy in copies(n, True):
            copy.wait()


def edge_product(flags, slot_a, slot_b, a_before, a_after, p_before, p_after, a_edge, p_tiles, out_a, out_b):
    rows = p_tiles.shape[0]

    def whole(x):
        return pl.BlockSpec(x.shape, lambda *_: (0,) * x.ndim)

    anywhere = pl.BlockSpec(memory_space=pl.ANY)
    return pl.pallas_call(
        edge_kernel,
        grid_spec=pltpu.PrefetchScalarGridSpec(
            num_scalar_prefetch=3,
            grid=(1,),
            in_specs=[whole(x) for x in (a_before, a_after, p_before, p_after, a_edge)]
            + [
                pl.BlockSpec((1, KP, B, B), lambda *_: (0, 0, 0, 0)),
                pl.BlockSpec((1, KP, B, B), lambda *_: (rows - 1, 0, 0, 0)),
                anywhere,
                anywhere,
            ],
            out_specs=[anywhere, anywhere],
            scratch_shapes=[VMEM((4, CWIN, B, B), F32), pltpu.SemaphoreType.DMA((4, 2))],
        ),
        out_shape=[jax.ShapeDtypeStruct(x.shape, x.dtype) for x in (out_a, out_b)],
        input_output_aliases={10: 0, 11: 1},
        compiler_params=pltpu.CompilerParams(
            dimension_semantics=("arbitrary",), vmem_limit_bytes=56 << 20
        ),
        cost_estimate=pl.CostEstimate(flops=2_000_000_000, bytes_accessed=10_000_000, transcendentals=0),
        name="edge_rows",
    )(flags, slot_a, slot_b, a_before, a_after, p_before, p_after, a_edge, p_tiles, p_tiles, out_a, out_b)


def relay(pairs, sems_in, sems_out):
    inward = [pltpu.make_async_copy(x, y, sems_in.at[k]) for k, (x, y, z) in enumerate(pairs)]
    outward = [pltpu.make_async_copy(y, z, sems_out.at[k]) for k, (x, y, z) in enumerate(pairs)]
    for copy in inward:
        copy.start()
    for come, go in zip(inward, outward):
        come.wait()
        go.start()
    for copy in outward:
        copy.wait()


def move_kernel(source_ref, target_ref, rows_in, rows_out, stage, sems_in, sems_out):
    relay(
        [(rows_in.at[source_ref[k]], stage.at[k], rows_out.at[target_ref[k]]) for k in range(stage.shape[0])],
        sems_in,
        sems_out,
    )


def move_rows(source, target, rows, places):
    count = source.shape[0]
    anywhere = pl.BlockSpec(memory_space=pl.ANY)
    return pl.pallas_call(
        move_kernel,
        grid_spec=pltpu.PrefetchScalarGridSpec(
            num_scalar_prefetch=2,
            grid=(1,),
            in_specs=[anywhere],
            out_specs=anywhere,
            scratch_shapes=[
                VMEM((count,) + rows.shape[1:], F32),
                pltpu.SemaphoreType.DMA((count,)),
                pltpu.SemaphoreType.DMA((count,)),
            ],
        ),
        out_shape=jax.ShapeDtypeStruct((places,) + rows.shape[1:], F32),
        compiler_params=pltpu.CompilerParams(vmem_limit_bytes=56 << 20),
        cost_estimate=pl.CostEstimate(flops=0, bytes_accessed=8_000_000, transcendentals=0),
        name="move_rows",
    )(source, target, rows)


def join_kernel(source_a, source_b, rows_a, rows_b, out, stage, sems_in, sems_out):
    pairs = []
    for k in range(stage.shape[0]):
        for rows, source, first in ((rows_a, source_a, 0), (rows_b, source_b, HALF)):
            part = pl.ds(first, HALF)
            pairs.append((rows.at[source[k]], stage.at[k, :, part], out.at[k, :, part]))
    relay(pairs, sems_in, sems_out)


def join_rows(source_a, source_b, rows_a, rows_b):
    count = source_a.shape[0]
    anywhere = pl.BlockSpec(memory_space=pl.ANY)
    return pl.pallas_call(
        join_kernel,
        grid_spec=pltpu.PrefetchScalarGridSpec(
            num_scalar_prefetch=2,
            grid=(1,),
            in_specs=[anywhere, anywhere],
            out_specs=anywhere,
            scratch_shapes=[
                VMEM((count, CWIN, B, B), F32),
                pltpu.SemaphoreType.DMA((2 * count,)),
                pltpu.SemaphoreType.DMA((2 * count,)),
            ],
        ),
        out_shape=jax.ShapeDtypeStruct((count, CWIN, B, B), F32),
        compiler_params=pltpu.CompilerParams(vmem_limit_bytes=56 << 20),
        cost_estimate=pl.CostEstimate(flops=0, bytes_accessed=16_000_000, transcendentals=0),
        name="join_rows",
    )(source_a, source_b, rows_a, rows_b)


def shards(a_tiles, a_cols, a_len, p_tiles, aggregate, owner):
    count_x = lax.axis_size("gx")
    count_y = lax.axis_size("gy")
    index_x = lax.axis_index("gx")
    index_y = lax.axis_index("gy")
    device = index_x * count_y + index_y
    fine = a_tiles.shape[0]
    coarse = fine // 3
    fine_total = fine * count_x * count_y
    devices = count_x * count_y
    first_row = device * fine

    rows = jnp.arange(fine)
    here = first_row + rows
    second = a_cols[:, 1] == (here + fine_total - 1) % fine_total
    left_at = jnp.where(second, 1, 2).astype(jnp.int32)
    right_at = 3 - left_at
    left_on = (a_len > left_at).astype(jnp.int32)
    right_on = (a_len > right_at).astype(jnp.int32)
    wrapped = jnp.concatenate([aggregate[-4:], aggregate, aggregate[:4]])
    window = lax.dynamic_slice_in_dim(wrapped, first_row, fine + 8)
    around = (first_row - 4 + jnp.arange(fine + 8)) % fine_total
    flags = (window != around // 3).astype(jnp.int32)

    def normal(at):
        part = a_tiles[at : at + 3]
        chosen = jnp.stack([left_at[at : at + 3], jnp.zeros(3, jnp.int32), right_at[at : at + 3]], axis=1)
        on = jnp.stack([left_on[at : at + 3], jnp.ones(3, jnp.int32), right_on[at : at + 3]], axis=1)
        tiles = jnp.where(
            (chosen == 1)[:, :, None, None],
            part[:, 1:2],
            jnp.where((chosen == 2)[:, :, None, None], part[:, 2:3], part[:, :1]),
        )
        return jnp.where((on > 0)[:, :, None, None], tiles, 0.0)

    a_first, a_last = normal(0), normal(fine - 3)
    a_edge = jnp.stack([a_first[0, 0], a_last[2, 2]])
    up = [(i, (i + 1) % devices) for i in range(devices)]
    down = [(j, i) for i, j in up]
    axes = ("gx", "gy")
    a_before = lax.ppermute(a_last, axes, up)
    p_before = lax.ppermute(p_tiles[fine - 4 :], axes, up)
    a_after = lax.ppermute(a_first, axes, down)
    p_after = lax.ppermute(p_tiles[:4], axes, down)

    table = owner.reshape(devices, coarse)
    order = jnp.arange(coarse)
    shift = table[0] // count_y
    same = shift[None, :] == shift[:, None]
    rank = jnp.sum((same & (order[None, :] < order[:, None])).astype(jnp.int32), axis=1)
    depth = coarse // count_x
    mine = lax.dynamic_slice_in_dim(table, device, 1)[0]
    slot_a = (shift * depth + rank).astype(jnp.int32)
    slot_b = (mine % count_y).astype(jnp.int32)
    from_x = (index_x - shift) % count_x
    column = table.reshape(count_x, count_y, coarse)[:, index_y]
    mid_a_target = jnp.sum(
        jnp.where(jnp.arange(count_x)[:, None] == from_x[None, :], column % count_y, 0), axis=0
    ).astype(jnp.int32)
    mid_a_source = (shift * depth + rank).astype(jnp.int32)
    slab = lax.dynamic_slice_in_dim(table.reshape(count_x, count_y, coarse), index_x, 1)[0]
    hit = (slab % count_y) == index_y
    mid_b_source = jnp.sum(jnp.where(hit, jnp.arange(count_y)[:, None], 0), axis=0).astype(jnp.int32)
    mid_b_target = (shift * depth + rank).astype(jnp.int32)
    found = table == device
    sender = jnp.sum(jnp.where(found, jnp.arange(devices)[:, None], 0), axis=0)
    ids = sender * coarse + order
    place = jnp.sum((ids[None, :] < ids[:, None]).astype(jnp.int32), axis=1)
    at = place[None, :] == order[:, None]
    last_a = jnp.sum(jnp.where(at, (sender % count_y)[None, :], 0), axis=1).astype(jnp.int32)
    last_b = jnp.sum(
        jnp.where(at, (shift * depth + rank)[None, :], 0), axis=1
    ).astype(jnp.int32)

    outer_left = left_on * (rows > 0)
    outer_right = right_on * (rows < fine - 1)
    meta = (flags[3 : fine + 5], left_at, right_at, outer_left, outer_right)
    rows_a, rows_b = main_product(meta, slot_a, slot_b, a_tiles, p_tiles, count_y)
    edge_flags = jnp.concatenate([flags[0:5], flags[fine + 3 : fine + 8]])
    rows_a, rows_b = edge_product(
        edge_flags, slot_a, slot_b, a_before, a_after, p_before, p_after, a_edge, p_tiles, rows_a, rows_b
    )

    def over(x, axis):
        return lax.all_to_all(x, axis, split_axis=0, concat_axis=0, tiled=True)

    def along_x(x):
        parts = [x[:depth]]
        for k in range(1, count_x):
            pairs = [(i, (i + k) % count_x) for i in range(count_x)]
            parts.append(lax.ppermute(x[k * depth : (k + 1) * depth], "gx", pairs))
        return jnp.concatenate(parts, axis=0)

    got_b = over(rows_b, "gy")
    got_a = along_x(rows_a)
    next_a = move_rows(mid_a_source, mid_a_target, got_a, count_y)
    next_b = move_rows(mid_b_source, mid_b_target, got_b, coarse)
    end_a = over(next_a, "gy")
    end_b = along_x(next_b)
    return join_rows(last_a, last_b, end_a, end_b)


def solution(mesh):
    in_specs = (
        P(("gx", "gy"), None, None, None),
        P(("gx", "gy"), None),
        P(("gx", "gy")),
        P(("gx", "gy"), None, None, None),
        P(),
        P(),
    )
    out_specs = P(("gx", "gy"), None, None, None)
    return jax.shard_map(shards, mesh=mesh, in_specs=in_specs, out_specs=out_specs, check_vma=False)
```

```python
import functools

import jax
import jax.numpy as jnp
from jax import lax
from jax.experimental import pallas as pl
from jax.experimental.pallas import tpu as pltpu
from jax.sharding import PartitionSpec as P

B = 128
KP = 2
LANES = 128
CWIN = 7
W = 6
BF = jnp.bfloat16
F32 = jnp.float32
SMEM = pltpu.SMEM
ANYWHERE = pl.BlockSpec(memory_space=pl.ANY)
VMEM = pltpu.VMEM


LEFT, OUT_LEFT, OUT_RIGHT, CODE, PLAN = 64, 128, 192, 256, 384


def split(x):
    high = x.astype(BF)
    return high, (x - high.astype(F32)).astype(BF)


def left_operand(x):
    high, low = split(x)
    return jnp.concatenate([high, low, high], axis=1)


def right_operand(x):
    high, low = split(x)
    return jnp.concatenate([high, high, low], axis=0)


def matmul(left, right):
    return jnp.dot(left, right, preferred_element_type=F32)


def spread(total, flag, base, pair, slots):
    first, second = pair
    values = {
        base - 1: jnp.where(flag, first, 0.0),
        base: jnp.where(flag, second, first),
        base + 1: jnp.where(flag, 0.0, second),
    }
    for s, value in values.items():
        if s in slots:
            total[s] = value if total.get(s) is None else total[s] + value


def row_product(p_pair, tiles):
    turned = jnp.concatenate([p_pair[0].T, p_pair[1].T], axis=0)
    return matmul(left_operand(turned), right_operand(jnp.concatenate(tiles, axis=1)))


SLOTS = {0: (0, 1, 2, 3), 1: (1, 2, 3), 2: (1, 2, 3, 4)}


def main_kernel(
    plan,
    a_ref, p_ref, before_ref, after_ref,
    out,
    stage, carry, sems,
):
    step = pl.program_id(0)
    steps = pl.num_programs(0) - 1
    buf = lax.rem(step, 2)

    def copy_out(at, which, row):
        c = 2 * at - 1 + row
        return pltpu.make_async_copy(stage.at[which, row], out.at[c], sems.at[which, row])

    def drain(at):
        which = lax.rem(at, 2)
        for row in range(2):
            @pl.when((2 * at - 1 + row >= 0) & (2 * at - 1 + row < 2 * steps))
            def _():
                copy_out(at, which, row).wait()

    @pl.when(step >= 2)
    def _():
        drain(step - 2)

    @pl.when(step == 0)
    def _():
        carry[...] = jnp.zeros_like(carry)

    stage[buf, 0] = carry[0]
    stage[buf, 1] = carry[1]

    @pl.when(step < steps)
    def _():
        carry[...] = jnp.zeros_like(carry)
        first = step * W
        flags = {q: plan[first + q + 4] > 0 for q in range(-1, W + 1)}

        def p_tile(q, m):
            if q < 0:
                return before_ref[0, m]
            if q >= W:
                return after_ref[0, m]
            return p_ref[q, m]

        lefts = {}
        for r in range(W):
            tiles = {
                0: jnp.where(plan[OUT_LEFT + first + r] > 0, a_ref[r, plan[LEFT + first + r]], 0.0),
                1: a_ref[r, 0],
                2: jnp.where(plan[OUT_RIGHT + first + r] > 0, a_ref[r, 3 - plan[LEFT + first + r]], 0.0),
            }
            for k in range(3):
                lefts[r, r + k - 1] = left_operand(tiles[k])
        total = {r: {} for r in range(W)}
        for q in range(-1, W + 1):
            rows = [r for r in (q - 1, q, q + 1) if 0 <= r < W]
            right = right_operand(jnp.concatenate([p_tile(q, 0), p_tile(q, 1)], axis=1))
            product = matmul(jnp.concatenate([lefts[r, q] for r in rows], axis=0), right)
            for n, r in enumerate(rows):
                pair = (product[n * B : (n + 1) * B, :B], product[n * B : (n + 1) * B, B:])
                spread(total[r], flags[q], q // 3 - r // 3 + 2, pair, SLOTS[r % 3])
        for r in range(W):
            slots = SLOTS[r % 3]
            product = row_product((p_ref[r, 0], p_ref[r, 1]), [total[r][s] for s in slots])
            g = r // 3
            for n, s in enumerate(slots):
                one = product[:B, n * B : (n + 1) * B]
                two = product[B:, n * B : (n + 1) * B]
                for delta, value in (
                    (-1, jnp.where(flags[r], one, 0.0)),
                    (0, jnp.where(flags[r], two, one)),
                    (1, jnp.where(flags[r], 0.0, two)),
                ):
                    place = g + delta + 1
                    if place < 2:
                        stage[buf, place, s + 1 - delta] += value
                    else:
                        carry[place - 2, s + 1 - delta] += value

    for row in range(2):
        @pl.when((2 * step - 1 + row >= 0) & (2 * step - 1 + row < 2 * steps))
        def _():
            copy_out(step, buf, row).start()

    @pl.when(step == steps)
    def _():
        drain(step - 1)
        drain(step)


def main_product(plan, a_tiles, p_tiles):
    rows = a_tiles.shape[0]
    steps = rows // W
    coarse = rows // 3
    last = steps - 1

    def spec(shape, index):
        return pl.BlockSpec(shape, index)

    return pl.pallas_call(
        main_kernel,
        grid_spec=pltpu.PrefetchScalarGridSpec(
            num_scalar_prefetch=1,
            grid=(steps + 1,),
            in_specs=[
                spec((W, 3, B, B), lambda s, *_: (jnp.minimum(s, last), 0, 0, 0)),
                spec((W, KP, B, B), lambda s, *_: (jnp.minimum(s, last), 0, 0, 0)),
                spec((1, KP, B, B), lambda s, *_: (jnp.maximum(jnp.minimum(s, last) * W - 1, 0), 0, 0, 0)),
                spec((1, KP, B, B), lambda s, *_: (jnp.minimum(s * W + W, rows - 1), 0, 0, 0)),
            ],
            out_specs=pl.BlockSpec(memory_space=pl.ANY),
            scratch_shapes=[
                VMEM((2, 2, CWIN, B, B), F32),
                VMEM((2, CWIN, B, B), F32),
                pltpu.SemaphoreType.DMA((2, 2)),
            ],
        ),
        out_shape=jax.ShapeDtypeStruct((coarse, CWIN, B, B), F32),
        compiler_params=pltpu.CompilerParams(
            dimension_semantics=("arbitrary",), vmem_limit_bytes=56 << 20
        ),
        cost_estimate=pl.CostEstimate(
            flops=16_000_000_000, bytes_accessed=24_000_000, transcendentals=0
        ),
        name="triple_product",
    )(plan, a_tiles, p_tiles, p_tiles, p_tiles)


def edge_kernel(
    plan,
    before, after, a_first, a_last, p_first, p_last, in_rows,
    out_rows,
    rows_ref, sems,
):
    coarse = out_rows.shape[0]
    held = (0, 1, coarse - 2, coarse - 1)

    def copy(n, back):
        there, here = out_rows.at[held[n]], rows_ref.at[n]
        if back:
            return pltpu.make_async_copy(here, there, sems.at[n])
        return pltpu.make_async_copy(there, here, sems.at[n])

    for n in range(4):
        copy(n, False).start()

    sums = []
    for side in range(2):
        halo = (before, after)[side]
        a_edge = (a_first, a_last)[side]
        own_p = (p_first, p_last)[side]
        own_flag = plan[(4, 3 * coarse + 3)[side]] > 0
        flags, tiles, p_at = {}, {}, {}
        for n in range(4):
            q = n - 1 if side == 0 else n
            flags[q] = plan[(0, 3 * coarse + 4)[side] + n] > 0
            p_at[q] = (halo[9 + 2 * n], halo[10 + 2 * n])
        near = 3 if side == 0 else -1
        flags[near] = own_flag
        p_at[near] = (own_p[0, 0], own_p[0, 1])
        total = {r: {} for r in range(3)}
        total[near] = {}
        for q in range(-1, 4):
            rows = [r for r in (q - 1, q, q + 1) if 0 <= r < 3]
            lefts = [left_operand(halo[3 * r + q - r + 1]) for r in rows]
            if q == (2 if side == 0 else 0):
                rows.append(near)
                lefts.append(left_operand(a_edge[0]))
            right = right_operand(jnp.concatenate(p_at[q], axis=1))
            product = matmul(jnp.concatenate(lefts, axis=0), right)
            for n, r in enumerate(rows):
                pair = (product[n * B : (n + 1) * B, :B], product[n * B : (n + 1) * B, B:])
                base = q // 3 - r // 3 + 2
                slots = SLOTS[r % 3] if r != near else (base - 1, base, base + 1)
                spread(total[r], flags[q], base, pair, slots)
        outer, inner = {}, {}

        def put(target, w, value):
            target[w] = value if w not in target else target[w] + value

        for r in range(3):
            slots = sorted(total[r])
            pick = 1 if side == 0 else 0
            turned = left_operand(p_at[r][pick].T)
            product = matmul(turned, right_operand(jnp.concatenate([total[r][s] for s in slots], axis=1)))
            for n, s in enumerate(slots):
                value = product[:, n * B : (n + 1) * B]
                if side == 0:
                    put(outer, s, jnp.where(flags[r], 0.0, value))
                else:
                    put(outer, s + 2, jnp.where(flags[r], value, 0.0))
        slots = sorted(total[near])
        product = row_product(p_at[near], [total[near][s] for s in slots])
        for n, s in enumerate(slots):
            one = product[:B, n * B : (n + 1) * B]
            two = product[B:, n * B : (n + 1) * B]
            put(outer, s + 1, jnp.where(own_flag, two, one))
            if side == 0:
                put(inner, s, jnp.where(own_flag, 0.0, two))
            else:
                put(inner, s + 2, jnp.where(own_flag, one, 0.0))
        sums.append((outer, inner))

    for n in range(4):
        copy(n, False).wait()
    for n, target in ((0, sums[0][0]), (1, sums[0][1]), (2, sums[1][1]), (3, sums[1][0])):
        for w, value in target.items():
            rows_ref[n, w] += value
    for n in range(4):
        copy(n, True).start()
    for n in range(4):
        copy(n, True).wait()


def edge_product(plan, before, after, up, down, p_tiles, out_rows):
    rows = p_tiles.shape[0]

    def whole(x):
        return pl.BlockSpec(x.shape, lambda *_: (0,) * x.ndim)

    anywhere = pl.BlockSpec(memory_space=pl.ANY)
    return pl.pallas_call(
        edge_kernel,
        grid_spec=pltpu.PrefetchScalarGridSpec(
            num_scalar_prefetch=1,
            grid=(1,),
            in_specs=[whole(before), whole(after)]
            + [
                pl.BlockSpec((1, B, B), lambda *_: (0, 0, 0)),
                pl.BlockSpec((1, B, B), lambda *_: (8, 0, 0)),
                pl.BlockSpec((1, KP, B, B), lambda *_: (0, 0, 0, 0)),
                pl.BlockSpec((1, KP, B, B), lambda *_: (rows - 1, 0, 0, 0)),
                anywhere,
            ],
            out_specs=anywhere,
            scratch_shapes=[VMEM((4, CWIN, B, B), F32), pltpu.SemaphoreType.DMA((4,))],
        ),
        out_shape=jax.ShapeDtypeStruct(out_rows.shape, F32),
        input_output_aliases={7: 0},
        compiler_params=pltpu.CompilerParams(
            dimension_semantics=("arbitrary",), vmem_limit_bytes=56 << 20
        ),
        cost_estimate=pl.CostEstimate(flops=2_000_000_000, bytes_accessed=10_000_000, transcendentals=0),
        name="edge_rows",
    )(plan, before, after, down, up, p_tiles, p_tiles, out_rows)


def plan_kernel(place, cols, length, aggregate, owner, a_tiles, p_tiles, owners, plan, counts, up, down, low, high, sem):
    fine, coarse = length.shape[0], owners.shape[1] // 8
    fine_total, coarse_total = aggregate.shape[0], owner.shape[0]
    first = place[0] * fine

    def entry(i):
        before = first + i - 1
        before = jnp.where(before < 0, fine_total - 1, before)
        left = jnp.where(cols[3 * i + 1] == before, 1, 2)
        return left, length[i] > left, length[i] > 3 - left

    sends = []
    for out, row, p_row in ((up, fine - 3, fine - 4), (down, 0, 0)):
        for r in range(3):
            left, on_left, on_right = entry(row + r)
            for k, slot, on in ((0, left, on_left), (2, 3 - left, on_right)):
                sends.append((a_tiles.at[row + r, slot], out.at[3 * r + k], on))
            sends.append((a_tiles.at[row + r, 0], out.at[3 * r + 1], None))
        for n in range(4):
            for m in range(KP):
                sends.append((p_tiles.at[p_row + n, m], out.at[9 + 2 * n + m], None))
    for k, (here, there, on) in enumerate(sends):
        if on is None:
            pltpu.make_async_copy(here, there, sem.at[k]).start()
        else:

            @pl.when(on)
            def _():
                pltpu.make_async_copy(here, there, sem.at[k]).start()

            @pl.when(jnp.logical_not(on))
            def _():
                there[...] = jnp.zeros(there.shape, F32)

    def flag(k, carry):
        row = first + k - 4
        row = jnp.where(row < 0, row + fine_total, jnp.where(row >= fine_total, row - fine_total, row))
        plan[k] = jnp.where(aggregate[row] != lax.div(row, 3), 1, 0)
        return carry

    lax.fori_loop(0, fine + 8, flag, 0)

    def bounds(k, mod, on_left, on_right):
        here = 2 - plan[k + 1]
        left = jnp.where(on_left, (1 if mod == 0 else 2) - plan[k], here)
        right = jnp.where(on_right, (3 if mod == 2 else 2) - plan[k + 2], here)
        low[k] = jnp.minimum(here, jnp.minimum(left, right))
        high[k] = 1 + jnp.maximum(here, jnp.maximum(left, right))

    for mod in range(3):
        bounds(mod, mod, True, True)
        bounds(fine + 3 + mod, mod, True, True)

    def group(g, carry):
        for mod in range(3):
            i = 3 * g + mod
            left, on_left, on_right = entry(i)
            plan[LEFT + i] = left
            plan[OUT_LEFT + i] = jnp.where(on_left & (i > 0), 1, 0)
            plan[OUT_RIGHT + i] = jnp.where(on_right & (i < fine - 1), 1, 0)
            bounds(i + 3, mod, on_left, on_right)
        return carry

    lax.fori_loop(0, coarse, group, 0)
    ids = lax.broadcasted_iota(jnp.int32, owners.shape, 0) * LANES + lax.broadcasted_iota(
        jnp.int32, owners.shape, 1
    )
    mine_at = lax.broadcasted_iota(jnp.int32, counts.shape, 1) == place[0]
    row_at = lax.broadcasted_iota(jnp.int32, counts.shape, 0)

    def code(c, carry):
        least, most = jnp.int32(9), jnp.int32(-9)
        for mod in range(3):
            at = 3 * c + mod
            past, next_ = plan[at + 1] == 0, plan[at + 7] == 1
            least = jnp.minimum(least, low[at + 3] + 1)
            most = jnp.maximum(most, high[at + 3] + 1)
            least = jnp.minimum(least, jnp.where(past, low[at], 9))
            most = jnp.maximum(most, jnp.where(past, high[at], -9))
            least = jnp.minimum(least, jnp.where(next_, low[at + 6] + 2, 9))
            most = jnp.maximum(most, jnp.where(next_, high[at + 6] + 2, -9))
        row = place[0] * coarse + c
        mine = owner[row]
        spot = jnp.sum(jnp.where((owners[...] == mine) & (ids < row), 1, 0))
        tiles = most - least + 1
        plan[CODE + c] = mine * 1024 + spot * 64 + least * 8 + tiles
        return jnp.where(mine_at & (row_at == c), tiles, carry)

    tiles = lax.fori_loop(0, coarse, code, jnp.zeros(counts.shape, jnp.int32))
    counts[...] = tiles.astype(F32)
    for k, (here, there, on) in enumerate(sends):
        if on is None:
            pltpu.make_async_copy(here, there, sem.at[k]).wait()
        else:

            @pl.when(on)
            def _():
                pltpu.make_async_copy(here, there, sem.at[k]).wait()


def make_plan(place, a_cols, a_len, aggregate, owner, a_tiles, p_tiles):
    fine = a_len.shape[0]
    coarse = fine // 3
    owners = owner.reshape(-1, LANES)

    def whole(shape):
        return pl.BlockSpec(shape, lambda *_: (0,) * len(shape))

    halo = (9 + 4 * KP, B, B)
    return pl.pallas_call(
        plan_kernel,
        grid_spec=pltpu.PrefetchScalarGridSpec(
            num_scalar_prefetch=5,
            grid=(1,),
            in_specs=[ANYWHERE, ANYWHERE, whole(owners.shape)],
            out_specs=[
                pl.BlockSpec(memory_space=SMEM),
                whole((coarse, LANES)),
                whole(halo),
                whole(halo),
            ],
            scratch_shapes=[
                SMEM((fine + 6,), jnp.int32),
                SMEM((fine + 6,), jnp.int32),
                pltpu.SemaphoreType.DMA((2 * halo[0],)),
            ],
        ),
        out_shape=[
            jax.ShapeDtypeStruct((PLAN,), jnp.int32),
            jax.ShapeDtypeStruct((coarse, LANES), F32),
            jax.ShapeDtypeStruct(halo, F32),
            jax.ShapeDtypeStruct(halo, F32),
        ],
        compiler_params=pltpu.CompilerParams(vmem_limit_bytes=32 << 20),
        cost_estimate=pl.CostEstimate(flops=0, bytes_accessed=5_000_000, transcendentals=0),
        name="plan",
    )(place, a_cols.reshape(-1), a_len, aggregate, owner, a_tiles, p_tiles, owners)


PARTS = (
    (0, 48, "xyz", ((36, 14, 48), (44, 20, 48), (49, 24, 48))),
    (48, 40, "yzx", ((44, 22, 48), (50, 22, 48), (50, 22, 48))),
    (88, 40, "zxy", ((43, 24, 48), (60, 30, 60), (50, 22, 48))),
)
SWAP = 64
SHIFT = {"x": 5, "z": 3, "y": 1}
FRONTS, BACKS = LANES - 2, LANES - 1
TABLE = pl.ds(8, 16)


def fields(code):
    return code >> 10, (code >> 6) & 15, (code >> 3) & 7, code & 7


def start_tiles(count, source, target, sem):
    for size in (4, 2, 1):
        first = count & (8 - 2 * size)

        @pl.when((count & size) != 0)
        def _():
            pltpu.make_async_copy(source(first, size), target(first, size), sem).start()


def wait_tiles(count, one, sem):
    def step(_, carry):
        pltpu.make_async_copy(one, one, sem).wait()
        return carry

    lax.fori_loop(0, count, step, 0)


class Rows:
    def __init__(self, codes, ref, first, height):
        self.codes, self.ref, self.first, self.height = codes, ref, first, height

    def walk(self, body):
        def step(k, carry):
            code = self.codes[CODE + k]
            tile = fields(code)[2]
            part = pl.ds(self.first, self.height)
            body(code, lambda at, size: self.ref.at[k, pl.ds(tile + at, size), part])
            return carry

        lax.fori_loop(0, self.ref.shape[0], step, 0)


class Slots:
    def __init__(self, header, ref, back):
        self.header, self.ref, self.back = header, ref, back

    def walk(self, body):
        def step(k, at):
            lane = FRONTS - 1 - k if self.back else k
            code = self.header[0, lane].astype(jnp.int32)
            count = code & 7
            slot = at - count if self.back else at
            body(code, lambda first, size: self.ref.at[pl.ds(slot + first, size)])
            return slot if self.back else slot + count

        entries = self.header[0, BACKS if self.back else FRONTS].astype(jnp.int32)
        lax.fori_loop(0, entries, step, self.ref.shape[0] if self.back else 1)


def read_headers(pairs, sem):
    copies = [pltpu.make_async_copy(ref.at[0, pl.ds(0, 1)], header, sem.at[k]) for k, (ref, header) in enumerate(pairs)]
    for copy in copies:
        copy.start()
    for copy in copies:
        copy.wait()


def read_table(arrivals, table_in, sem):
    copies = [pltpu.make_async_copy(x.at[0, TABLE], table_in.at[k], sem.at[k]) for k, x in enumerate(arrivals)]
    for copy in copies:
        copy.start()
    for copy in copies:
        copy.wait()
    table = table_in[0]
    for k in range(1, len(copies)):
        table = jnp.maximum(table, table_in[k])
    return table


def route_kernel(stage, plan, place, *refs):
    refs = list(refs)
    parts = len(PARTS)
    if stage == 0:
        arrivals = [[refs.pop(0)]] * parts
        counts = refs.pop(0)
    else:
        arrivals = [[refs.pop(0) for _ in range(5)] for _ in range(parts)]
    outs_of = [[refs.pop(0) for _ in range(3)] for _ in range(parts)]
    bufs = [refs.pop(0) for _ in range(parts)]
    state, copy_sem, head_sem, out_sem, table_in, table_out = [refs.pop(0) for _ in range(6)]
    heads = [[refs.pop(0) for _ in range(3)] for _ in range(parts)]
    odd = (place[0] & 1) == 1
    if stage > 0:
        came = [[refs.pop(0) for _ in range(5)] for _ in range(parts)]
        read_headers([(arrivals[p][k], came[p][k]) for p in range(parts) for k in range(5)], head_sem)
        table_out[...] = read_table(arrivals[0], table_in, head_sem)
    else:
        load = pltpu.make_async_copy(counts, table_out, head_sem.at[0])
        load.start()
        load.wait()
    tables = [
        pltpu.make_async_copy(table_out, outs_of[0][way].at[0, TABLE], out_sem.at[9 * parts + way]) for way in range(3)
    ]
    for table in tables:
        table.start()

    for p, (first_row, height, order, sizes) in enumerate(PARTS):
        send, on, stay = sizes[stage]
        shift = SHIFT[order[stage]]
        buf, sem, head, zero = bufs[p], copy_sem.at[p], heads[p], 16 * p
        if stage == 0:
            sources = [Rows(plan, arrivals[p][0], first_row, height)]
        else:
            sources = [
                Slots(h, g, back)
                for h, g, back in zip(came[p], arrivals[p], (False, True, True, False, False))
            ]
        mine = (place[0] >> shift) & 3
        base = (0, send + 1, 2 * (send + 1))

        def turn(code):
            by = (code >> (10 + shift)) - mine
            return jnp.where(odd, -by, by) & 3

        for k in range(4):
            state[zero + k] = 0

        def count(code, source):
            where = turn(code)
            state[zero + where] = state[zero + where] + (code & 7)

        for source in sources:
            source.walk(count)
        ahead, behind, across = state[zero + 1], state[zero + 3], state[zero + 2]
        big, small = jnp.maximum(ahead, behind), jnp.minimum(ahead, behind)
        lesser = jnp.minimum(jnp.minimum(across, (across + big - small + 1) >> 1), on)
        forward = jnp.where(ahead <= behind, lesser, across - lesser)
        for k, value in ((4, 1), (5, 1), (6, 1), (7, send + 1), (8, send + 1), (14, forward)):
            state[zero + k] = value
        for k in (9, 10, 11, 12, 13, 15):
            state[zero + k] = 0

        def put(code, source, skip, tiles, slot):
            start_tiles(
                tiles,
                lambda at, size: source(skip + at, size),
                lambda at, size: buf.at[pl.ds(slot + at, size)],
                sem,
            )
            state[zero + 15] = state[zero + 15] + tiles

        def front(way, code, source, skip, tiles, limit):
            slot = state[zero + 4 + way]
            fits = slot + tiles <= limit
            if way < 2:
                fits = fits & (slot + tiles <= state[zero + 7 + way])

            @pl.when((tiles > 0) & fits)
            def _():
                state[zero + 4 + way] = slot + tiles
                entry = state[zero + 9 + way]
                state[zero + 9 + way] = entry + 1
                sent = (code & ~63) | ((((code >> 3) & 7) + skip) << 3) | tiles
                head[way][0, entry] = sent.astype(F32)
                put(code, source, skip, tiles, base[way] + slot)

        def back(way, code, source):
            tiles = code & 7
            slot = state[zero + 7 + way] - tiles

            @pl.when(slot >= state[zero + 4 + way])
            def _():
                state[zero + 7 + way] = slot
                entry = state[zero + 12 + way]
                state[zero + 12 + way] = entry + 1
                head[way][0, FRONTS - 1 - entry] = code.astype(F32)
                put(code, source, 0, tiles, base[way] + slot)

        def assign(code, source):
            where = turn(code)
            tiles = code & 7

            @pl.when(where == 0)
            def _():
                front(2, code, source, 0, tiles, stay + 1)

            @pl.when(where == 1)
            def _():
                back(0, code, source)

            @pl.when(where == 3)
            def _():
                back(1, code, source)

            @pl.when(where == 2)
            def _():
                take = jnp.minimum(tiles, state[zero + 14])
                state[zero + 14] = state[zero + 14] - take
                front(0, code, source, 0, take, on + 1)
                front(1, code, source, take, tiles - take, on + 1)

        for source in sources:
            source.walk(assign)
        for way in range(3):
            head[way][0, FRONTS] = state[zero + 9 + way].astype(F32)
            head[way][0, BACKS] = (state[zero + 12 + way] if way < 2 else jnp.int32(0)).astype(F32)

    writes, kept = [], []
    for p, (_, _, _, sizes) in enumerate(PARTS):
        send, _, stay = sizes[stage]
        buf, head, outs, zero = bufs[p], heads[p], outs_of[p], 16 * p
        wait_tiles(state[zero + 15], buf.at[0], copy_sem.at[p])
        fresh = [
            pltpu.make_async_copy(head[way], outs[way].at[0, pl.ds(0, 1)], out_sem.at[9 * p + way]) for way in range(3)
        ]
        for way in range(2):
            fresh.append(
                pltpu.make_async_copy(
                    buf.at[pl.ds(way * (send + 1) + 1, send)],
                    outs[way].at[pl.ds(1, send)],
                    out_sem.at[9 * p + 3 + way],
                )
            )
        for write in fresh:
            write.start()
        writes += fresh
        chunk = stay // 4
        for k in range(4):
            first = 1 + k * chunk
            write = pltpu.make_async_copy(
                buf.at[pl.ds(2 * (send + 1) + first, chunk)], outs[2].at[pl.ds(first, chunk)], out_sem.at[9 * p + 5 + k]
            )
            used = state[zero + 6] > first
            pl.when(used)(write.start)
            kept.append((used, write))
    for used, write in kept:
        pl.when(used)(write.wait)
    for write in writes + tables:
        write.wait()


def table_scratch():
    return [VMEM((5, 16, LANES), F32), VMEM((16, LANES), F32)]


def head_scratch(count):
    return [SMEM((1, LANES), F32)] * count


def route(stage, plan, place, got):
    parts = len(PARTS)
    sizes = [(size[stage], height) for _, height, _, size in PARTS]
    result = pl.pallas_call(
        functools.partial(route_kernel, stage),
        grid_spec=pltpu.PrefetchScalarGridSpec(
            num_scalar_prefetch=2,
            grid=(1,),
            in_specs=[ANYWHERE] * len(got),
            out_specs=[ANYWHERE] * (3 * parts),
            scratch_shapes=[VMEM((2 * (send + 1) + stay + 1, height, LANES), F32) for (send, _, stay), height in sizes]
            + [
                SMEM((16 * parts,), jnp.int32),
                pltpu.SemaphoreType.DMA((parts,)),
                pltpu.SemaphoreType.DMA((5 * parts,)),
                pltpu.SemaphoreType.DMA((9 * parts + 3,)),
            ]
            + table_scratch()
            + head_scratch(3 * parts)
            + ([] if stage == 0 else head_scratch(5 * parts)),
        ),
        out_shape=[
            jax.ShapeDtypeStruct((size + 1, height, LANES), F32)
            for (send, _, stay), height in sizes
            for size in (send, send, stay)
        ],
        compiler_params=pltpu.CompilerParams(vmem_limit_bytes=48 << 20),
        cost_estimate=pl.CostEstimate(flops=0, bytes_accessed=24_000_000, transcendentals=0),
        name="route",
    )(plan, place, *got)
    return [result[3 * p : 3 * p + 3] for p in range(parts)]


def swap_kernel(first_part, place, *refs):
    refs = list(refs)
    got = [refs.pop(0) for _ in range(5)]
    out, buf, state, copy_sem, head_sem, out_sem, table_in, table_out, head = [refs.pop(0) for _ in range(9)]
    read_headers(list(zip(got, refs)), head_sem)
    writes = []
    if first_part:
        table_out[...] = read_table(got, table_in, head_sem)
        writes.append(pltpu.make_async_copy(table_out, out.at[0, TABLE], out_sem.at[2]))
    core, sem = place[0] & 1, copy_sem.at[0]
    for k, value in ((0, 1), (1, 0), (2, 0)):
        state[k] = value

    def assign(code, source):
        tiles = code & 7
        slot = state[0]

        @pl.when((((code >> 10) & 1) != core) & (slot + tiles <= SWAP + 1))
        def _():
            state[0] = slot + tiles
            entry = state[1]
            state[1] = entry + 1
            head[0, entry] = code.astype(F32)
            start_tiles(tiles, source, lambda at, size: buf.at[pl.ds(slot + at, size)], sem)
            state[2] = state[2] + tiles

    for h, g, back in zip(refs, got, (False, True, True, False, False)):
        Slots(h, g, back).walk(assign)
    head[0, FRONTS] = state[1].astype(F32)
    wait_tiles(state[2], buf.at[0], sem)
    writes += [
        pltpu.make_async_copy(buf.at[pl.ds(1, SWAP)], out.at[pl.ds(1, SWAP)], out_sem.at[0]),
        pltpu.make_async_copy(head, out.at[0, pl.ds(0, 1)], out_sem.at[1]),
    ]
    for write in writes:
        write.start()
    for write in writes:
        write.wait()


def swap_out(part, place, got):
    height = PARTS[part][1]
    return pl.pallas_call(
        functools.partial(swap_kernel, part == 0),
        grid_spec=pltpu.PrefetchScalarGridSpec(
            num_scalar_prefetch=1,
            grid=(1,),
            in_specs=[ANYWHERE] * len(got),
            out_specs=ANYWHERE,
            scratch_shapes=[
                VMEM((SWAP + 1, height, LANES), F32),
                SMEM((4,), jnp.int32),
                pltpu.SemaphoreType.DMA((1,)),
                pltpu.SemaphoreType.DMA((5,)),
                pltpu.SemaphoreType.DMA((3,)),
            ]
            + table_scratch()
            + head_scratch(6),
        ),
        out_shape=jax.ShapeDtypeStruct((SWAP + 1, height, LANES), F32),
        compiler_params=pltpu.CompilerParams(vmem_limit_bytes=32 << 20),
        cost_estimate=pl.CostEstimate(flops=0, bytes_accessed=6_000_000, transcendentals=0),
        name="swap_out",
    )(place, *got)


def gather_kernel(firsts, heights, place, *refs):
    refs = list(refs)
    parts = len(heights)
    got = [[refs.pop(0) for _ in range(6)] for _ in range(parts)]
    out, state, copy_sem, head_sem = [refs.pop(0) for _ in range(4)]
    heads = [[refs.pop(0) for _ in range(6)] for _ in range(parts)]
    copies = [
        pltpu.make_async_copy(got[p][k].at[0, pl.ds(0, 1)], heads[p][k], head_sem.at[6 * p + k])
        for p in range(parts)
        for k in range(6)
    ]
    for copy in copies:
        copy.start()

    def clear(k, carry):
        out[k] = jnp.zeros(out.shape[1:], F32)
        return carry

    lax.fori_loop(0, out.shape[0], clear, 0)
    for copy in copies:
        copy.wait()
    core = place[0] & 1
    for p in range(parts):
        sem = copy_sem.at[p]
        part = pl.ds(firsts[p], heights[p])
        state[p] = 0

        def assign(code, source):
            owner, row, tile, tiles = fields(code)

            @pl.when((owner & 1) == core)
            def _():
                start_tiles(tiles, source, lambda at, size: out.at[row, pl.ds(tile + at, size), part], sem)
                state[p] = state[p] + tiles

        for k, back in enumerate((False, True, True, False, False, False)):
            Slots(heads[p][k], got[p][k], back).walk(assign)
    for p in range(parts):
        wait_tiles(state[p], out.at[0, 0, pl.ds(firsts[p], heights[p])], copy_sem.at[p])


def gather_rows(place, got, coarse):
    firsts = tuple(first for first, _, _, _ in PARTS)
    heights = tuple(height for _, height, _, _ in PARTS)
    parts = len(PARTS)
    inputs = [x for part in got for x in part]
    return pl.pallas_call(
        functools.partial(gather_kernel, firsts, heights),
        grid_spec=pltpu.PrefetchScalarGridSpec(
            num_scalar_prefetch=1,
            grid=(1,),
            in_specs=[ANYWHERE] * len(inputs),
            out_specs=pl.BlockSpec((coarse, CWIN, B, B), lambda *_: (0, 0, 0, 0)),
            scratch_shapes=[
                SMEM((4,), jnp.int32),
                pltpu.SemaphoreType.DMA((parts,)),
                pltpu.SemaphoreType.DMA((6 * parts,)),
            ]
            + head_scratch(6 * parts),
        ),
        out_shape=jax.ShapeDtypeStruct((coarse, CWIN, B, B), F32),
        compiler_params=pltpu.CompilerParams(vmem_limit_bytes=56 << 20),
        cost_estimate=pl.CostEstimate(flops=0, bytes_accessed=16_000_000, transcendentals=0),
        name="gather_rows",
    )(place, *inputs)


def fits_kernel(owner_ref, one_ref, two_ref, out_ref):
    units = owner_ref.shape[1]
    devices = LANES
    owner = owner_ref[...]
    turned = jnp.maximum(one_ref[0, TABLE], two_ref[0, TABLE])
    tiles = jnp.concatenate([turned[r : r + 1] for r in range(units // devices)], axis=1)
    source = lax.broadcasted_iota(jnp.int32, (1, units), 1) & (devices - 1)
    index = lax.broadcasted_iota(jnp.int32, (devices, units), 0)
    kinds = lax.broadcasted_iota(jnp.int32, (8, units), 0)

    def tally(holder, kind):
        left = jnp.where(holder == index, 1.0, 0.0).astype(BF)
        right = jnp.where(kinds == kind, tiles, 0.0).astype(BF)
        return lax.dot_general(left, right, (((1,), (1,)), ((), ())), preferred_element_type=F32)

    def step(holder, shift):
        return holder + ((((owner >> shift) & 3) - ((holder >> shift) & 3)) << shift)

    excess = jnp.full((devices, 1), -1.0, F32)
    holder = source
    for _, _, order, sizes in PARTS:
        holder = source
        for axis, (send, on, stay) in zip(order, sizes):
            shift = SHIFT[axis]
            table = tally(holder, ((owner >> shift) - (holder >> shift)) & 3)
            here, ahead, across, behind = (table[:, k : k + 1] for k in range(4))
            big, small = jnp.maximum(ahead, behind), jnp.minimum(ahead, behind)
            lesser = jnp.minimum(jnp.minimum(across, jnp.floor((across + big - small + 1.0) * 0.5)), float(on))
            greater = across - lesser
            for value, limit in ((small + lesser, send), (big + greater, send), (greater, on), (here, stay)):
                excess = jnp.maximum(excess, value - float(limit))
            holder = step(holder, shift)
    table = tally(holder, (owner ^ holder) & 1)
    excess = jnp.maximum(excess, table[:, 1:2] - float(SWAP))
    out_ref[...] = jnp.broadcast_to(jnp.max(excess, axis=0, keepdims=True), out_ref.shape)


def ring_fits(owner, one, two):
    turned = owner.reshape(LANES, -1).T.reshape(1, -1)
    head = pl.BlockSpec((1,) + one.shape[1:], lambda *_: (0, 0, 0))
    return pl.pallas_call(
        fits_kernel,
        grid=(1,),
        in_specs=[pl.BlockSpec(turned.shape, lambda *_: (0, 0)), head, head],
        out_specs=pl.BlockSpec((8, LANES), lambda *_: (0, 0)),
        out_shape=jax.ShapeDtypeStruct((8, LANES), F32),
        compiler_params=pltpu.CompilerParams(vmem_limit_bytes=32 << 20),
        cost_estimate=pl.CostEstimate(flops=100_000_000, bytes_accessed=100_000, transcendentals=0),
        name="ring_fits",
    )(turned, one, two)[0, 0] <= 0.0


AXES = ("gx", "gy")


def neighbours(axis, way):
    shift, size = SHIFT[axis], lax.axis_size(AXES)
    pairs = []
    for i in range(size):
        by = way if i % 2 == 0 else -way
        pairs.append((i, (i & ~(3 << shift)) | ((((i >> shift) + by) & 3) << shift)))
    return pairs


def by_ring(plan, place, rows, counts):
    got = [[rows, counts]]
    for stage in range(3):
        sent = route(stage, plan, place, [x for part in got for x in part])
        got = []
        for (one, two, stay), (_, _, order, sizes) in zip(sent, PARTS):
            on = sizes[stage][1] + 1
            ways = neighbours(order[stage], 1), neighbours(order[stage], -1)
            came = [lax.ppermute(x, AXES, way) for x, way in zip((one, two), ways)]
            came += [lax.ppermute(x[:on], AXES, way) for x, way in zip(came, ways)]
            got.append([stay] + came)
    size = lax.axis_size(AXES)
    pairs = [(i, i ^ 1) for i in range(size)]
    other = [swap_out(part, place, got[part]) for part in range(len(PARTS))]
    swapped = [lax.ppermute(x, AXES, pairs) for x in other]
    return [part + [x] for part, x in zip(got, swapped)], other[0], swapped[0]


def shards(a_tiles, a_cols, a_len, p_tiles, aggregate, owner):
    device = lax.axis_index(AXES)
    size = lax.axis_size(AXES)
    coarse = a_tiles.shape[0] // 3
    place = jnp.reshape(device, (1,)).astype(jnp.int32)
    plan, counts, up, down = make_plan(place, a_cols, a_len, aggregate, owner, a_tiles, p_tiles)
    before = lax.ppermute(up, AXES, [(i, (i + 1) % size) for i in range(size)])
    behind = lax.ppermute(down, AXES, [((i + 1) % size, i) for i in range(size)])
    coarse_rows = main_product(plan, a_tiles, p_tiles)
    coarse_rows = edge_product(plan, before, behind, up, down, p_tiles, coarse_rows)
    got, one, two = by_ring(plan, place, coarse_rows, counts)
    fits = ring_fits(owner, one, two)
    return lax.cond(
        fits,
        lambda kept, parts: gather_rows(place, parts, coarse),
        lambda kept, parts: by_slots(kept, owner, device),
        coarse_rows,
        got,
    )


def by_slots(complete, owner, device):
    count_x, count_y = lax.axis_size("gx"), lax.axis_size("gy")
    index_x, index_y = device // count_y, device % count_y
    coarse = complete.shape[0]
    depth = coarse // count_x
    table = owner.reshape(count_x, count_y, coarse)
    order = jnp.arange(coarse)
    shift = table[0, 0] // count_y
    same = shift[None, :] == shift[:, None]
    rank = jnp.sum((same & (order[None, :] < order[:, None])).astype(jnp.int32), axis=1)
    mine = table[index_x, index_y]
    slot = (mine // count_y) * depth + rank
    hits = slot[None, :] == order[:, None]
    packed = complete[jnp.sum(jnp.where(hits, order[None, :], 0), axis=1)]
    moved = lax.all_to_all(packed, "gx", split_axis=0, concat_axis=0, tiled=True)
    from_x = (index_x - shift) % count_x
    column = table[:, index_y] % count_y
    target = jnp.sum(jnp.where(jnp.arange(count_x)[:, None] == from_x[None, :], column, 0), axis=0)
    hits = target[None, :] == jnp.arange(count_y)[:, None]
    packed = moved[jnp.sum(jnp.where(hits, (from_x * depth + rank)[None, :], 0), axis=1)]
    moved = lax.all_to_all(packed, "gy", split_axis=0, concat_axis=0, tiled=True)
    found = table.reshape(-1, coarse) == device
    sender = jnp.sum(jnp.where(found, jnp.arange(count_x * count_y)[:, None], 0), axis=0)
    ids = sender * coarse + order
    spot = jnp.sum((ids[None, :] < ids[:, None]).astype(jnp.int32), axis=1)
    hits = spot[None, :] == order[:, None]
    return moved[jnp.sum(jnp.where(hits, (sender % count_y)[None, :], 0), axis=1)]


def solution(mesh):
    in_specs = (
        P(("gx", "gy"), None, None, None),
        P(("gx", "gy"), None),
        P(("gx", "gy")),
        P(("gx", "gy"), None, None, None),
        P(),
        P(),
    )
    out_specs = P(("gx", "gy"), None, None, None)
    return jax.shard_map(shards, mesh=mesh, in_specs=in_specs, out_specs=out_specs, check_vma=False)
```

```python
import functools

import jax
import jax.numpy as jnp
from jax import lax
from jax.experimental import pallas as pl
from jax.experimental.pallas import tpu as pltpu
from jax.sharding import PartitionSpec as P

B = 128
KP = 2
LANES = 128
CWIN = 7
W = 6
BF = jnp.bfloat16
F32 = jnp.float32
SMEM = pltpu.SMEM
ANYWHERE = pl.BlockSpec(memory_space=pl.ANY)
VMEM = pltpu.VMEM


LEFT, OUT_LEFT, OUT_RIGHT, CODE, PLAN = 64, 128, 192, 256, 384


def split(x):
    high = x.astype(BF)
    return high, (x - high.astype(F32)).astype(BF)


def left_operand(x):
    high, low = split(x)
    return jnp.concatenate([high, low, high], axis=1)


def right_operand(x):
    high, low = split(x)
    return jnp.concatenate([high, high, low], axis=0)


def matmul(left, right):
    return jnp.dot(left, right, preferred_element_type=F32)


def spread(total, flag, base, pair, slots):
    first, second = pair
    values = {
        base - 1: jnp.where(flag, first, 0.0),
        base: jnp.where(flag, second, first),
        base + 1: jnp.where(flag, 0.0, second),
    }
    for s, value in values.items():
        if s in slots:
            total[s] = value if total.get(s) is None else total[s] + value


def row_product(p_pair, tiles):
    turned = jnp.concatenate([p_pair[0].T, p_pair[1].T], axis=0)
    return matmul(left_operand(turned), right_operand(jnp.concatenate(tiles, axis=1)))


SLOTS = {0: (0, 1, 2, 3), 1: (1, 2, 3), 2: (1, 2, 3, 4)}


def main_kernel(
    plan,
    a_ref, p_ref, before_ref, after_ref,
    out,
    stage, carry, sems,
):
    step = pl.program_id(0)
    steps = pl.num_programs(0) - 1
    buf = lax.rem(step, 2)

    def copy_out(at, which, row):
        c = 2 * at - 1 + row
        return pltpu.make_async_copy(stage.at[which, row], out.at[c], sems.at[which, row])

    def drain(at):
        which = lax.rem(at, 2)
        for row in range(2):
            @pl.when((2 * at - 1 + row >= 0) & (2 * at - 1 + row < 2 * steps))
            def _():
                copy_out(at, which, row).wait()

    @pl.when(step >= 2)
    def _():
        drain(step - 2)

    @pl.when(step == 0)
    def _():
        carry[...] = jnp.zeros_like(carry)

    stage[buf, 0] = carry[0]
    stage[buf, 1] = carry[1]

    @pl.when(step < steps)
    def _():
        carry[...] = jnp.zeros_like(carry)
        first = step * W
        flags = {q: plan[first + q + 4] > 0 for q in range(-1, W + 1)}

        def p_tile(q, m):
            if q < 0:
                return before_ref[0, m]
            if q >= W:
                return after_ref[0, m]
            return p_ref[q, m]

        lefts = {}
        for r in range(W):
            tiles = {
                0: jnp.where(plan[OUT_LEFT + first + r] > 0, a_ref[r, plan[LEFT + first + r]], 0.0),
                1: a_ref[r, 0],
                2: jnp.where(plan[OUT_RIGHT + first + r] > 0, a_ref[r, 3 - plan[LEFT + first + r]], 0.0),
            }
            for k in range(3):
                lefts[r, r + k - 1] = left_operand(tiles[k])
        total = {r: {} for r in range(W)}
        for q in range(-1, W + 1):
            rows = [r for r in (q - 1, q, q + 1) if 0 <= r < W]
            right = right_operand(jnp.concatenate([p_tile(q, 0), p_tile(q, 1)], axis=1))
            product = matmul(jnp.concatenate([lefts[r, q] for r in rows], axis=0), right)
            for n, r in enumerate(rows):
                pair = (product[n * B : (n + 1) * B, :B], product[n * B : (n + 1) * B, B:])
                spread(total[r], flags[q], q // 3 - r // 3 + 2, pair, SLOTS[r % 3])
        for r in range(W):
            slots = SLOTS[r % 3]
            product = row_product((p_ref[r, 0], p_ref[r, 1]), [total[r][s] for s in slots])
            g = r // 3
            for n, s in enumerate(slots):
                one = product[:B, n * B : (n + 1) * B]
                two = product[B:, n * B : (n + 1) * B]
                for delta, value in (
                    (-1, jnp.where(flags[r], one, 0.0)),
                    (0, jnp.where(flags[r], two, one)),
                    (1, jnp.where(flags[r], 0.0, two)),
                ):
                    place = g + delta + 1
                    if place < 2:
                        stage[buf, place, s + 1 - delta] += value
                    else:
                        carry[place - 2, s + 1 - delta] += value

    for row in range(2):
        @pl.when((2 * step - 1 + row >= 0) & (2 * step - 1 + row < 2 * steps))
        def _():
            copy_out(step, buf, row).start()

    @pl.when(step == steps)
    def _():
        drain(step - 1)
        drain(step)


def main_product(plan, a_tiles, p_tiles):
    rows = a_tiles.shape[0]
    steps = rows // W
    coarse = rows // 3
    last = steps - 1

    def spec(shape, index):
        return pl.BlockSpec(shape, index)

    return pl.pallas_call(
        main_kernel,
        grid_spec=pltpu.PrefetchScalarGridSpec(
            num_scalar_prefetch=1,
            grid=(steps + 1,),
            in_specs=[
                spec((W, 3, B, B), lambda s, *_: (jnp.minimum(s, last), 0, 0, 0)),
                spec((W, KP, B, B), lambda s, *_: (jnp.minimum(s, last), 0, 0, 0)),
                spec((1, KP, B, B), lambda s, *_: (jnp.maximum(jnp.minimum(s, last) * W - 1, 0), 0, 0, 0)),
                spec((1, KP, B, B), lambda s, *_: (jnp.minimum(s * W + W, rows - 1), 0, 0, 0)),
            ],
            out_specs=pl.BlockSpec(memory_space=pl.ANY),
            scratch_shapes=[
                VMEM((2, 2, CWIN, B, B), F32),
                VMEM((2, CWIN, B, B), F32),
                pltpu.SemaphoreType.DMA((2, 2)),
            ],
        ),
        out_shape=jax.ShapeDtypeStruct((coarse, CWIN, B, B), F32),
        compiler_params=pltpu.CompilerParams(
            dimension_semantics=("arbitrary",), vmem_limit_bytes=56 << 20
        ),
        cost_estimate=pl.CostEstimate(
            flops=16_000_000_000, bytes_accessed=24_000_000, transcendentals=0
        ),
        name="triple_product",
    )(plan, a_tiles, p_tiles, p_tiles, p_tiles)


def edge_kernel(
    plan,
    before, after, a_first, a_last, p_first, p_last, in_rows,
    out_rows,
    rows_ref, sems,
):
    coarse = out_rows.shape[0]
    held = (0, 1, coarse - 2, coarse - 1)

    def copy(n, back):
        there, here = out_rows.at[held[n]], rows_ref.at[n]
        if back:
            return pltpu.make_async_copy(here, there, sems.at[n])
        return pltpu.make_async_copy(there, here, sems.at[n])

    for n in range(4):
        copy(n, False).start()

    sums = []
    for side in range(2):
        halo = (before, after)[side]
        a_edge = (a_first, a_last)[side]
        own_p = (p_first, p_last)[side]
        own_flag = plan[(4, 3 * coarse + 3)[side]] > 0
        flags, tiles, p_at = {}, {}, {}
        for n in range(4):
            q = n - 1 if side == 0 else n
            flags[q] = plan[(0, 3 * coarse + 4)[side] + n] > 0
            p_at[q] = (halo[9 + 2 * n], halo[10 + 2 * n])
        near = 3 if side == 0 else -1
        flags[near] = own_flag
        p_at[near] = (own_p[0, 0], own_p[0, 1])
        total = {r: {} for r in range(3)}
        total[near] = {}
        for q in range(-1, 4):
            rows = [r for r in (q - 1, q, q + 1) if 0 <= r < 3]
            lefts = [left_operand(halo[3 * r + q - r + 1]) for r in rows]
            if q == (2 if side == 0 else 0):
                rows.append(near)
                lefts.append(left_operand(a_edge[0]))
            right = right_operand(jnp.concatenate(p_at[q], axis=1))
            product = matmul(jnp.concatenate(lefts, axis=0), right)
            for n, r in enumerate(rows):
                pair = (product[n * B : (n + 1) * B, :B], product[n * B : (n + 1) * B, B:])
                base = q // 3 - r // 3 + 2
                slots = SLOTS[r % 3] if r != near else (base - 1, base, base + 1)
                spread(total[r], flags[q], base, pair, slots)
        outer, inner = {}, {}

        def put(target, w, value):
            target[w] = value if w not in target else target[w] + value

        for r in range(3):
            slots = sorted(total[r])
            pick = 1 if side == 0 else 0
            turned = left_operand(p_at[r][pick].T)
            product = matmul(turned, right_operand(jnp.concatenate([total[r][s] for s in slots], axis=1)))
            for n, s in enumerate(slots):
                value = product[:, n * B : (n + 1) * B]
                if side == 0:
                    put(outer, s, jnp.where(flags[r], 0.0, value))
                else:
                    put(outer, s + 2, jnp.where(flags[r], value, 0.0))
        slots = sorted(total[near])
        product = row_product(p_at[near], [total[near][s] for s in slots])
        for n, s in enumerate(slots):
            one = product[:B, n * B : (n + 1) * B]
            two = product[B:, n * B : (n + 1) * B]
            put(outer, s + 1, jnp.where(own_flag, two, one))
            if side == 0:
                put(inner, s, jnp.where(own_flag, 0.0, two))
            else:
                put(inner, s + 2, jnp.where(own_flag, one, 0.0))
        sums.append((outer, inner))

    for n in range(4):
        copy(n, False).wait()
    for n, target in ((0, sums[0][0]), (1, sums[0][1]), (2, sums[1][1]), (3, sums[1][0])):
        for w, value in target.items():
            rows_ref[n, w] += value
    for n in range(4):
        copy(n, True).start()
    for n in range(4):
        copy(n, True).wait()


def edge_product(plan, before, after, up, down, p_tiles, out_rows):
    rows = p_tiles.shape[0]

    def whole(x):
        return pl.BlockSpec(x.shape, lambda *_: (0,) * x.ndim)

    anywhere = pl.BlockSpec(memory_space=pl.ANY)
    return pl.pallas_call(
        edge_kernel,
        grid_spec=pltpu.PrefetchScalarGridSpec(
            num_scalar_prefetch=1,
            grid=(1,),
            in_specs=[whole(before), whole(after)]
            + [
                pl.BlockSpec((1, B, B), lambda *_: (0, 0, 0)),
                pl.BlockSpec((1, B, B), lambda *_: (8, 0, 0)),
                pl.BlockSpec((1, KP, B, B), lambda *_: (0, 0, 0, 0)),
                pl.BlockSpec((1, KP, B, B), lambda *_: (rows - 1, 0, 0, 0)),
                anywhere,
            ],
            out_specs=anywhere,
            scratch_shapes=[VMEM((4, CWIN, B, B), F32), pltpu.SemaphoreType.DMA((4,))],
        ),
        out_shape=jax.ShapeDtypeStruct(out_rows.shape, F32),
        input_output_aliases={7: 0},
        compiler_params=pltpu.CompilerParams(
            dimension_semantics=("arbitrary",), vmem_limit_bytes=56 << 20
        ),
        cost_estimate=pl.CostEstimate(flops=2_000_000_000, bytes_accessed=10_000_000, transcendentals=0),
        name="edge_rows",
    )(plan, before, after, down, up, p_tiles, p_tiles, out_rows)


def plan_kernel(place, cols, length, a_tiles, p_tiles, aggregate, owners, owners_all, plan, counts, up, down, low, high, near, mine_ref, sem):
    fine, coarse = length.shape[0], counts.shape[0]
    wide = aggregate.shape[0]
    fine_total = wide * LANES
    first = place[0] * fine
    line = jnp.where(first < 4, wide - 1, (first - 4) >> 7)
    begin = jnp.where(first < 4, LANES - 4, (first - 4) & (LANES - 1))
    lines = (line, jnp.where(line == wide - 1, 0, line + 1))
    index_loads = [
        pltpu.make_async_copy(aggregate.at[pl.ds(at, 1)], near.at[pl.ds(n, 1)], sem.at[n]) for n, at in enumerate(lines)
    ]
    index_loads.append(
        pltpu.make_async_copy(owners.at[pl.ds((place[0] * coarse) >> 7, 1)], mine_ref, sem.at[2])
    )
    for load in index_loads:
        load.start()

    def entry(i):
        before = first + i - 1
        before = jnp.where(before < 0, fine_total - 1, before)
        left = jnp.where(cols[1, i] == before, 1, 2)
        return left, length[i] > left, length[i] > 3 - left

    sends = []
    for out, row, p_row in ((up, fine - 3, fine - 4), (down, 0, 0)):
        for r in range(3):
            left, on_left, on_right = entry(row + r)
            for k, slot, on in ((0, left, on_left), (2, 3 - left, on_right)):
                sends.append((a_tiles.at[row + r, slot], out.at[3 * r + k], on))
            sends.append((a_tiles.at[row + r, 0], out.at[3 * r + 1], None))
        for n in range(4):
            for m in range(KP):
                sends.append((p_tiles.at[p_row + n, m], out.at[9 + 2 * n + m], None))
    for k, (here, there, on) in enumerate(sends):
        if on is None:
            pltpu.make_async_copy(here, there, sem.at[3 + k]).start()
        else:

            @pl.when(on)
            def _():
                pltpu.make_async_copy(here, there, sem.at[3 + k]).start()

            @pl.when(jnp.logical_not(on))
            def _():
                there[...] = jnp.zeros(there.shape, F32)

    def flag(k, carry):
        row = first + k - 4
        row = jnp.where(row < 0, row + fine_total, jnp.where(row >= fine_total, row - fine_total, row))
        at = begin + k
        plan[k] = jnp.where(near[at >> 7, at & (LANES - 1)] != lax.div(row, 3), 1, 0)
        return carry

    for load in index_loads:
        load.wait()
    lax.fori_loop(0, fine + 8, flag, 0, unroll=8)

    def bounds(k, mod, on_left, on_right):
        here = 2 - plan[k + 1]
        left = jnp.where(on_left, (1 if mod == 0 else 2) - plan[k], here)
        right = jnp.where(on_right, (3 if mod == 2 else 2) - plan[k + 2], here)
        low[k] = jnp.minimum(here, jnp.minimum(left, right))
        high[k] = 1 + jnp.maximum(here, jnp.maximum(left, right))

    for mod in range(3):
        bounds(mod, mod, True, True)
        bounds(fine + 3 + mod, mod, True, True)

    def group(g, carry):
        for mod in range(3):
            i = 3 * g + mod
            left, on_left, on_right = entry(i)
            plan[LEFT + i] = left
            plan[OUT_LEFT + i] = jnp.where(on_left & (i > 0), 1, 0)
            plan[OUT_RIGHT + i] = jnp.where(on_right & (i < fine - 1), 1, 0)
            bounds(i + 3, mod, on_left, on_right)
        return carry

    lax.fori_loop(0, coarse, group, 0, unroll=4)
    ids = lax.broadcasted_iota(jnp.int32, counts.shape, 0) * LANES + lax.broadcasted_iota(
        jnp.int32, counts.shape, 1
    )
    everyone = owners_all[...]

    def code(c, carry):
        least, most = jnp.int32(9), jnp.int32(-9)
        for mod in range(3):
            at = 3 * c + mod
            past, next_ = plan[at + 1] == 0, plan[at + 7] == 1
            least = jnp.minimum(least, low[at + 3] + 1)
            most = jnp.maximum(most, high[at + 3] + 1)
            least = jnp.minimum(least, jnp.where(past, low[at], 9))
            most = jnp.maximum(most, jnp.where(past, high[at], -9))
            least = jnp.minimum(least, jnp.where(next_, low[at + 6] + 2, 9))
            most = jnp.maximum(most, jnp.where(next_, high[at + 6] + 2, -9))
        row = place[0] * coarse + c
        mine = mine_ref[0, row & (LANES - 1)]
        spot = jnp.sum(jnp.where((everyone == mine) & (ids < row), 1, 0))
        tiles = most - least + 1
        plan[CODE + c] = mine * 1024 + spot * 64 + least * 8 + tiles
        return jnp.where(ids == row, tiles, carry)

    tiles = lax.fori_loop(0, coarse, code, jnp.zeros(counts.shape, jnp.int32), unroll=4)
    counts[...] = tiles.astype(F32)
    for k, (here, there, on) in enumerate(sends):
        if on is None:
            pltpu.make_async_copy(here, there, sem.at[3 + k]).wait()
        else:

            @pl.when(on)
            def _():
                pltpu.make_async_copy(here, there, sem.at[3 + k]).wait()


def make_plan(place, a_cols, a_len, aggregate, owner, a_tiles, p_tiles):
    fine = a_len.shape[0]
    coarse = fine // 3
    owners = owner.reshape(-1, LANES)

    def whole(shape):
        return pl.BlockSpec(shape, lambda *_: (0,) * len(shape))

    halo = (9 + 4 * KP, B, B)
    return pl.pallas_call(
        plan_kernel,
        grid_spec=pltpu.PrefetchScalarGridSpec(
            num_scalar_prefetch=3,
            grid=(1,),
            in_specs=[ANYWHERE] * 4 + [whole(owners.shape)],
            out_specs=[
                pl.BlockSpec(memory_space=SMEM),
                whole((coarse, LANES)),
                whole(halo),
                whole(halo),
            ],
            scratch_shapes=[
                SMEM((fine + 6,), jnp.int32),
                SMEM((fine + 6,), jnp.int32),
                SMEM((2, LANES), jnp.int32),
                SMEM((1, LANES), jnp.int32),
                pltpu.SemaphoreType.DMA((3 + 2 * halo[0],)),
            ],
        ),
        out_shape=[
            jax.ShapeDtypeStruct((PLAN,), jnp.int32),
            jax.ShapeDtypeStruct((coarse, LANES), F32),
            jax.ShapeDtypeStruct(halo, F32),
            jax.ShapeDtypeStruct(halo, F32),
        ],
        compiler_params=pltpu.CompilerParams(vmem_limit_bytes=32 << 20),
        cost_estimate=pl.CostEstimate(flops=0, bytes_accessed=5_000_000, transcendentals=0),
        name="plan",
    )(place, a_cols.T, a_len, a_tiles, p_tiles, aggregate.reshape(-1, LANES), owners, owners)


PARTS = (
    (0, 48, "xyz", ((37, 14, 48), (46, 24, 48), (54, 24, 48))),
    (48, 40, "yzx", ((49, 24, 48), (54, 24, 48), (50, 24, 48))),
    (88, 40, "zxy", ((47, 24, 48), (64, 32, 64), (53, 24, 48))),
)
SWAP = 67
SHIFT = {"x": 5, "z": 3, "y": 1}
FRONTS, BACKS = LANES - 2, LANES - 1
TABLE = pl.ds(8, 16)


def fields(code):
    return code >> 10, (code >> 6) & 15, (code >> 3) & 7, code & 7


def start_tiles(count, source, target, sem):
    for size in (4, 2, 1):
        first = count & (8 - 2 * size)

        @pl.when((count & size) != 0)
        def _():
            pltpu.make_async_copy(source(first, size), target(first, size), sem).start()


def wait_tiles(count, one, sem):
    def step(_, carry):
        pltpu.make_async_copy(one, one, sem).wait()
        return carry

    lax.fori_loop(0, count, step, 0)


class Rows:
    def __init__(self, codes, ref, first, height):
        self.codes, self.ref, self.first, self.height = codes, ref, first, height

    def walk(self, body):
        def step(k, carry):
            code = self.codes[CODE + k]
            tile = fields(code)[2]
            part = pl.ds(self.first, self.height)
            body(code, lambda at, size: self.ref.at[k, pl.ds(tile + at, size), part])
            return carry

        lax.fori_loop(0, self.ref.shape[0], step, 0)


class Slots:
    def __init__(self, header, ref, back):
        self.header, self.ref, self.back = header, ref, back

    def walk(self, body):
        def step(k, at):
            lane = FRONTS - 1 - k if self.back else k
            code = self.header[0, lane].astype(jnp.int32)
            count = code & 7
            slot = at - count if self.back else at
            body(code, lambda first, size: self.ref.at[pl.ds(slot + first, size)])
            return slot if self.back else slot + count

        entries = self.header[0, BACKS if self.back else FRONTS].astype(jnp.int32)
        lax.fori_loop(0, entries, step, self.ref.shape[0] if self.back else 1)


def read_headers(pairs, sem):
    copies = [pltpu.make_async_copy(ref.at[0, pl.ds(0, 1)], header, sem.at[k]) for k, (ref, header) in enumerate(pairs)]
    for copy in copies:
        copy.start()
    for copy in copies:
        copy.wait()


def read_table(arrivals, table_in, sem):
    copies = [pltpu.make_async_copy(x.at[0, TABLE], table_in.at[k], sem.at[k]) for k, x in enumerate(arrivals)]
    for copy in copies:
        copy.start()

    def finish():
        for copy in copies:
            copy.wait()
        table = table_in[0]
        for k in range(1, len(copies)):
            table = jnp.maximum(table, table_in[k])
        return table

    return finish


def route_kernel(stage, plan, place, *refs):
    refs = list(refs)
    parts = len(PARTS)
    if stage == 0:
        arrivals = [[refs.pop(0)]] * parts
        counts = refs.pop(0)
    else:
        arrivals = [[refs.pop(0) for _ in range(5)] for _ in range(parts)]
    outs_of = [[refs.pop(0) for _ in range(3)] for _ in range(parts)]
    bufs = [refs.pop(0) for _ in range(parts)]
    state, copy_sem, head_sem, out_sem, table_in, table_out, table_sem = [refs.pop(0) for _ in range(7)]
    heads = [[refs.pop(0) for _ in range(3)] for _ in range(parts)]
    odd = (place[0] & 1) == 1
    if stage > 0:
        came = [[refs.pop(0) for _ in range(5)] for _ in range(parts)]
        finish = read_table(arrivals[0], table_in, table_sem)
        read_headers([(arrivals[p][k], came[p][k]) for p in range(parts) for k in range(5)], head_sem)
        table_out[...] = finish()
    else:
        load = pltpu.make_async_copy(counts, table_out, head_sem.at[0])
        load.start()
        load.wait()
    tables = [
        pltpu.make_async_copy(table_out, outs_of[0][way].at[0, TABLE], out_sem.at[9 * parts + way]) for way in range(3)
    ]
    for table in tables:
        table.start()
    writes, kept = [], []

    def write_out(p):
        send, _, stay = PARTS[p][3][stage]
        buf, head, outs, zero = bufs[p], heads[p], outs_of[p], 16 * p
        wait_tiles(state[zero + 15], buf.at[0], copy_sem.at[p])
        fresh = [
            pltpu.make_async_copy(head[way], outs[way].at[0, pl.ds(0, 1)], out_sem.at[9 * p + way]) for way in range(3)
        ]
        for way in range(2):
            fresh.append(
                pltpu.make_async_copy(
                    buf.at[pl.ds(way * (send + 1) + 1, send)],
                    outs[way].at[pl.ds(1, send)],
                    out_sem.at[9 * p + 3 + way],
                )
            )
        for write in fresh:
            write.start()
        writes.extend(fresh)
        chunk = stay // 4
        for k in range(4):
            first = 1 + k * chunk
            write = pltpu.make_async_copy(
                buf.at[pl.ds(2 * (send + 1) + first, chunk)], outs[2].at[pl.ds(first, chunk)], out_sem.at[9 * p + 5 + k]
            )
            used = state[zero + 6] > first
            pl.when(used)(write.start)
            kept.append((used, write))

    for p, (first_row, height, order, sizes) in enumerate(PARTS):
        send, on, stay = sizes[stage]
        shift = SHIFT[order[stage]]
        buf, sem, head, zero = bufs[p], copy_sem.at[p], heads[p], 16 * p
        if stage == 0:
            sources = [Rows(plan, arrivals[p][0], first_row, height)]
        else:
            sources = [
                Slots(h, g, back)
                for h, g, back in zip(came[p], arrivals[p], (False, True, True, False, False))
            ]
        mine = (place[0] >> shift) & 3
        base = (0, send + 1, 2 * (send + 1))

        def turn(code):
            by = (code >> (10 + shift)) - mine
            return jnp.where(odd, -by, by) & 3

        for k in range(4):
            state[zero + k] = 0

        def count(code, source):
            where = turn(code)
            state[zero + where] = state[zero + where] + (code & 7)

        for source in sources:
            source.walk(count)
        ahead, behind, across = state[zero + 1], state[zero + 3], state[zero + 2]
        big, small = jnp.maximum(ahead, behind), jnp.minimum(ahead, behind)
        lesser = jnp.minimum(jnp.minimum(across, (across + big - small + 1) >> 1), on)
        forward = jnp.where(ahead <= behind, lesser, across - lesser)
        for k, value in ((4, 1), (5, 1), (6, 1), (7, send + 1), (8, send + 1), (14, forward)):
            state[zero + k] = value
        for k in (9, 10, 11, 12, 13, 15):
            state[zero + k] = 0

        def put(code, source, skip, tiles, slot):
            start_tiles(
                tiles,
                lambda at, size: source(skip + at, size),
                lambda at, size: buf.at[pl.ds(slot + at, size)],
                sem,
            )
            state[zero + 15] = state[zero + 15] + tiles

        def front(way, code, source, skip, tiles, limit):
            slot = state[zero + 4 + way]
            fits = slot + tiles <= limit
            if way < 2:
                fits = fits & (slot + tiles <= state[zero + 7 + way])

            @pl.when((tiles > 0) & fits)
            def _():
                state[zero + 4 + way] = slot + tiles
                entry = state[zero + 9 + way]
                state[zero + 9 + way] = entry + 1
                sent = (code & ~63) | ((((code >> 3) & 7) + skip) << 3) | tiles
                head[way][0, entry] = sent.astype(F32)
                put(code, source, skip, tiles, base[way] + slot)

        def back(way, code, source):
            tiles = code & 7
            slot = state[zero + 7 + way] - tiles

            @pl.when(slot >= state[zero + 4 + way])
            def _():
                state[zero + 7 + way] = slot
                entry = state[zero + 12 + way]
                state[zero + 12 + way] = entry + 1
                head[way][0, FRONTS - 1 - entry] = code.astype(F32)
                put(code, source, 0, tiles, base[way] + slot)

        def assign(code, source):
            where = turn(code)
            tiles = code & 7

            @pl.when(where == 0)
            def _():
                front(2, code, source, 0, tiles, stay + 1)

            @pl.when(where == 1)
            def _():
                back(0, code, source)

            @pl.when(where == 3)
            def _():
                back(1, code, source)

            @pl.when(where == 2)
            def _():
                take = jnp.minimum(tiles, state[zero + 14])
                state[zero + 14] = state[zero + 14] - take
                front(0, code, source, 0, take, on + 1)
                front(1, code, source, take, tiles - take, on + 1)

        for source in sources:
            source.walk(assign)
        for way in range(3):
            head[way][0, FRONTS] = state[zero + 9 + way].astype(F32)
            head[way][0, BACKS] = (state[zero + 12 + way] if way < 2 else jnp.int32(0)).astype(F32)
        if p > 0:
            write_out(p - 1)
    write_out(parts - 1)


    for used, write in kept:
        pl.when(used)(write.wait)
    for write in writes + tables:
        write.wait()


def table_scratch():
    return [VMEM((5, 16, LANES), F32), VMEM((16, LANES), F32), pltpu.SemaphoreType.DMA((5,))]


def head_scratch(count):
    return [SMEM((1, LANES), F32)] * count


def route(stage, plan, place, got):
    parts = len(PARTS)
    sizes = [(size[stage], height) for _, height, _, size in PARTS]
    result = pl.pallas_call(
        functools.partial(route_kernel, stage),
        grid_spec=pltpu.PrefetchScalarGridSpec(
            num_scalar_prefetch=2,
            grid=(1,),
            in_specs=[ANYWHERE] * len(got),
            out_specs=[ANYWHERE] * (3 * parts),
            scratch_shapes=[VMEM((2 * (send + 1) + stay + 1, height, LANES), F32) for (send, _, stay), height in sizes]
            + [
                SMEM((16 * parts,), jnp.int32),
                pltpu.SemaphoreType.DMA((parts,)),
                pltpu.SemaphoreType.DMA((5 * parts,)),
                pltpu.SemaphoreType.DMA((9 * parts + 3,)),
            ]
            + table_scratch()
            + head_scratch(3 * parts)
            + ([] if stage == 0 else head_scratch(5 * parts)),
        ),
        out_shape=[
            jax.ShapeDtypeStruct((size + 1, height, LANES), F32)
            for (send, _, stay), height in sizes
            for size in (send, send, stay)
        ],
        compiler_params=pltpu.CompilerParams(vmem_limit_bytes=48 << 20),
        cost_estimate=pl.CostEstimate(flops=0, bytes_accessed=24_000_000, transcendentals=0),
        name="route",
    )(plan, place, *got)
    return [result[3 * p : 3 * p + 3] for p in range(parts)]


def swap_kernel(place, *refs):
    refs = list(refs)
    parts = len(PARTS)
    got = [[refs.pop(0) for _ in range(5)] for _ in range(parts)]
    outs = [refs.pop(0) for _ in range(parts)]
    bufs = [refs.pop(0) for _ in range(parts)]
    state, copy_sem, head_sem, out_sem, table_in, table_out, table_sem = [refs.pop(0) for _ in range(7)]
    out_heads = [refs.pop(0) for _ in range(parts)]
    heads = [[refs.pop(0) for _ in range(5)] for _ in range(parts)]
    finish = read_table(got[0], table_in, table_sem)
    read_headers([(got[p][k], heads[p][k]) for p in range(parts) for k in range(5)], head_sem)
    core = place[0] & 1
    table_out[...] = finish()
    writes = [pltpu.make_async_copy(table_out, outs[0].at[0, TABLE], out_sem.at[2 * parts])]
    writes[0].start()

    def write_out(p):
        wait_tiles(state[4 * p + 2], bufs[p].at[0], copy_sem.at[p])
        fresh = [
            pltpu.make_async_copy(bufs[p].at[pl.ds(1, SWAP)], outs[p].at[pl.ds(1, SWAP)], out_sem.at[2 * p]),
            pltpu.make_async_copy(out_heads[p], outs[p].at[0, pl.ds(0, 1)], out_sem.at[2 * p + 1]),
        ]
        for write in fresh:
            write.start()
        writes.extend(fresh)

    for p in range(parts):
        buf, sem, head, zero = bufs[p], copy_sem.at[p], out_heads[p], 4 * p
        for k, value in ((0, 1), (1, 0), (2, 0)):
            state[zero + k] = value

        def assign(code, source):
            tiles = code & 7
            slot = state[zero]

            @pl.when((((code >> 10) & 1) != core) & (slot + tiles <= SWAP + 1))
            def _():
                state[zero] = slot + tiles
                entry = state[zero + 1]
                state[zero + 1] = entry + 1
                head[0, entry] = code.astype(F32)
                start_tiles(tiles, source, lambda at, size: buf.at[pl.ds(slot + at, size)], sem)
                state[zero + 2] = state[zero + 2] + tiles

        for h, g, back in zip(heads[p], got[p], (False, True, True, False, False)):
            Slots(h, g, back).walk(assign)
        head[0, FRONTS] = state[zero + 1].astype(F32)
        if p > 0:
            write_out(p - 1)
    write_out(parts - 1)
    for write in writes:
        write.wait()


def swap_out(place, got):
    parts = len(PARTS)
    heights = [height for _, height, _, _ in PARTS]
    inputs = [x for part in got for x in part]
    return pl.pallas_call(
        swap_kernel,
        grid_spec=pltpu.PrefetchScalarGridSpec(
            num_scalar_prefetch=1,
            grid=(1,),
            in_specs=[ANYWHERE] * len(inputs),
            out_specs=[ANYWHERE] * parts,
            scratch_shapes=[VMEM((SWAP + 1, height, LANES), F32) for height in heights]
            + [
                SMEM((4 * parts,), jnp.int32),
                pltpu.SemaphoreType.DMA((parts,)),
                pltpu.SemaphoreType.DMA((5 * parts,)),
                pltpu.SemaphoreType.DMA((2 * parts + 1,)),
            ]
            + table_scratch()
            + head_scratch(6 * parts),
        ),
        out_shape=[jax.ShapeDtypeStruct((SWAP + 1, height, LANES), F32) for height in heights],
        compiler_params=pltpu.CompilerParams(vmem_limit_bytes=48 << 20),
        cost_estimate=pl.CostEstimate(flops=0, bytes_accessed=16_000_000, transcendentals=0),
        name="swap_out",
    )(place, *inputs)


def gather_kernel(firsts, heights, place, *refs):
    refs = list(refs)
    parts = len(heights)
    got = [[refs.pop(0) for _ in range(6)] for _ in range(parts)]
    out, state, copy_sem, head_sem = [refs.pop(0) for _ in range(4)]
    heads = [[refs.pop(0) for _ in range(6)] for _ in range(parts)]
    copies = [
        pltpu.make_async_copy(got[p][k].at[0, pl.ds(0, 1)], heads[p][k], head_sem.at[6 * p + k])
        for p in range(parts)
        for k in range(6)
    ]
    for copy in copies:
        copy.start()

    def clear(k, carry):
        out[k] = jnp.zeros(out.shape[1:], F32)
        return carry

    lax.fori_loop(0, out.shape[0], clear, 0)
    for copy in copies:
        copy.wait()
    core = place[0] & 1
    for p in range(parts):
        sem = copy_sem.at[p]
        part = pl.ds(firsts[p], heights[p])
        state[p] = 0

        def assign(code, source):
            owner, row, tile, tiles = fields(code)

            @pl.when((owner & 1) == core)
            def _():
                start_tiles(tiles, source, lambda at, size: out.at[row, pl.ds(tile + at, size), part], sem)
                state[p] = state[p] + tiles

        for k, back in enumerate((False, True, True, False, False, False)):
            Slots(heads[p][k], got[p][k], back).walk(assign)
    for p in range(parts):
        wait_tiles(state[p], out.at[0, 0, pl.ds(firsts[p], heights[p])], copy_sem.at[p])


def gather_rows(place, got, coarse):
    firsts = tuple(first for first, _, _, _ in PARTS)
    heights = tuple(height for _, height, _, _ in PARTS)
    parts = len(PARTS)
    inputs = [x for part in got for x in part]
    return pl.pallas_call(
        functools.partial(gather_kernel, firsts, heights),
        grid_spec=pltpu.PrefetchScalarGridSpec(
            num_scalar_prefetch=1,
            grid=(1,),
            in_specs=[ANYWHERE] * len(inputs),
            out_specs=pl.BlockSpec((coarse, CWIN, B, B), lambda *_: (0, 0, 0, 0)),
            scratch_shapes=[
                SMEM((4,), jnp.int32),
                pltpu.SemaphoreType.DMA((parts,)),
                pltpu.SemaphoreType.DMA((6 * parts,)),
            ]
            + head_scratch(6 * parts),
        ),
        out_shape=jax.ShapeDtypeStruct((coarse, CWIN, B, B), F32),
        compiler_params=pltpu.CompilerParams(vmem_limit_bytes=56 << 20),
        cost_estimate=pl.CostEstimate(flops=0, bytes_accessed=16_000_000, transcendentals=0),
        name="gather_rows",
    )(place, *inputs)


def fits_kernel(owner_ref, one_ref, two_ref, out_ref):
    units = owner_ref.shape[1]
    devices = LANES
    owner = owner_ref[...]
    turned = jnp.maximum(one_ref[0, TABLE], two_ref[0, TABLE])
    tiles = jnp.concatenate([turned[r : r + 1] for r in range(units // devices)], axis=1)
    source = lax.broadcasted_iota(jnp.int32, (1, units), 1) // (units // devices)
    index = lax.broadcasted_iota(jnp.int32, (devices, units), 0)
    kinds = lax.broadcasted_iota(jnp.int32, (8, units), 0)

    def tally(holder, kind):
        left = jnp.where(holder == index, 1.0, 0.0).astype(BF)
        right = jnp.where(kinds == kind, tiles, 0.0).astype(BF)
        return lax.dot_general(left, right, (((1,), (1,)), ((), ())), preferred_element_type=F32)

    def step(holder, shift):
        return holder + ((((owner >> shift) & 3) - ((holder >> shift) & 3)) << shift)

    excess = jnp.full((devices, 1), -1.0, F32)
    holder = source
    for _, _, order, sizes in PARTS:
        holder = source
        for axis, (send, on, stay) in zip(order, sizes):
            shift = SHIFT[axis]
            table = tally(holder, ((owner >> shift) - (holder >> shift)) & 3)
            here, ahead, across, behind = (table[:, k : k + 1] for k in range(4))
            big, small = jnp.maximum(ahead, behind), jnp.minimum(ahead, behind)
            lesser = jnp.minimum(jnp.minimum(across, jnp.floor((across + big - small + 1.0) * 0.5)), float(on))
            greater = across - lesser
            for value, limit in ((small + lesser, send), (big + greater, send), (greater, on), (here, stay)):
                excess = jnp.maximum(excess, value - float(limit))
            holder = step(holder, shift)
    table = tally(holder, (owner ^ holder) & 1)
    excess = jnp.maximum(excess, table[:, 1:2] - float(SWAP))
    out_ref[...] = jnp.broadcast_to(jnp.max(excess, axis=0, keepdims=True), out_ref.shape)


def ring_fits(owner, one, two):
    turned = owner.reshape(1, -1)
    head = pl.BlockSpec((1,) + one.shape[1:], lambda *_: (0, 0, 0))
    return pl.pallas_call(
        fits_kernel,
        grid=(1,),
        in_specs=[pl.BlockSpec(turned.shape, lambda *_: (0, 0)), head, head],
        out_specs=pl.BlockSpec((8, LANES), lambda *_: (0, 0)),
        out_shape=jax.ShapeDtypeStruct((8, LANES), F32),
        compiler_params=pltpu.CompilerParams(vmem_limit_bytes=32 << 20),
        cost_estimate=pl.CostEstimate(flops=100_000_000, bytes_accessed=100_000, transcendentals=0),
        name="ring_fits",
    )(turned, one, two)[0, 0] <= 0.0


AXES = ("gx", "gy")


def neighbours(axis, way):
    shift, size = SHIFT[axis], lax.axis_size(AXES)
    pairs = []
    for i in range(size):
        by = way if i % 2 == 0 else -way
        pairs.append((i, (i & ~(3 << shift)) | ((((i >> shift) + by) & 3) << shift)))
    return pairs


def by_ring(plan, place, rows, counts):
    got = [[rows, counts]]
    for stage in range(3):
        sent = route(stage, plan, place, [x for part in got for x in part])
        got = []
        for (one, two, stay), (_, _, order, sizes) in zip(sent, PARTS):
            on = sizes[stage][1] + 1
            ways = neighbours(order[stage], 1), neighbours(order[stage], -1)
            came = [lax.ppermute(x, AXES, way) for x, way in zip((one, two), ways)]
            came += [lax.ppermute(x[:on], AXES, way) for x, way in zip(came, ways)]
            got.append([stay] + came)
    size = lax.axis_size(AXES)
    pairs = [(i, i ^ 1) for i in range(size)]
    other = swap_out(place, got)
    swapped = [lax.ppermute(x, AXES, pairs) for x in other]
    return [part + [x] for part, x in zip(got, swapped)], other[0], swapped[0]


def shards(a_tiles, a_cols, a_len, p_tiles, aggregate, owner):
    device = lax.axis_index(AXES)
    size = lax.axis_size(AXES)
    coarse = a_tiles.shape[0] // 3
    place = jnp.reshape(device, (1,)).astype(jnp.int32)
    plan, counts, up, down = make_plan(place, a_cols, a_len, aggregate, owner, a_tiles, p_tiles)
    before = lax.ppermute(up, AXES, [(i, (i + 1) % size) for i in range(size)])
    behind = lax.ppermute(down, AXES, [((i + 1) % size, i) for i in range(size)])
    coarse_rows = main_product(plan, a_tiles, p_tiles)
    coarse_rows = edge_product(plan, before, behind, up, down, p_tiles, coarse_rows)
    got, one, two = by_ring(plan, place, coarse_rows, counts)
    fits = ring_fits(owner, one, two)
    return lax.cond(
        fits,
        lambda kept, parts: gather_rows(place, parts, coarse),
        lambda kept, parts: by_slots(kept, owner, device),
        coarse_rows,
        got,
    )


def by_slots(complete, owner, device):
    count_x, count_y = lax.axis_size("gx"), lax.axis_size("gy")
    index_x, index_y = device // count_y, device % count_y
    coarse = complete.shape[0]
    depth = coarse // count_x
    table = owner.reshape(count_x, count_y, coarse)
    order = jnp.arange(coarse)
    shift = table[0, 0] // count_y
    same = shift[None, :] == shift[:, None]
    rank = jnp.sum((same & (order[None, :] < order[:, None])).astype(jnp.int32), axis=1)
    mine = table[index_x, index_y]
    slot = (mine // count_y) * depth + rank
    hits = slot[None, :] == order[:, None]
    packed = complete[jnp.sum(jnp.where(hits, order[None, :], 0), axis=1)]
    moved = lax.all_to_all(packed, "gx", split_axis=0, concat_axis=0, tiled=True)
    from_x = (index_x - shift) % count_x
    column = table[:, index_y] % count_y
    target = jnp.sum(jnp.where(jnp.arange(count_x)[:, None] == from_x[None, :], column, 0), axis=0)
    hits = target[None, :] == jnp.arange(count_y)[:, None]
    packed = moved[jnp.sum(jnp.where(hits, (from_x * depth + rank)[None, :], 0), axis=1)]
    moved = lax.all_to_all(packed, "gy", split_axis=0, concat_axis=0, tiled=True)
    found = table.reshape(-1, coarse) == device
    sender = jnp.sum(jnp.where(found, jnp.arange(count_x * count_y)[:, None], 0), axis=0)
    ids = sender * coarse + order
    spot = jnp.sum((ids[None, :] < ids[:, None]).astype(jnp.int32), axis=1)
    hits = spot[None, :] == order[:, None]
    return moved[jnp.sum(jnp.where(hits, (sender % count_y)[None, :], 0), axis=1)]


def solution(mesh):
    in_specs = (
        P(("gx", "gy"), None, None, None),
        P(("gx", "gy"), None),
        P(("gx", "gy")),
        P(("gx", "gy"), None, None, None),
        P(),
        P(),
    )
    out_specs = P(("gx", "gy"), None, None, None)
    return jax.shard_map(shards, mesh=mesh, in_specs=in_specs, out_specs=out_specs, check_vma=False)
```

```python
import functools

import jax
import jax.numpy as jnp
from jax import lax
from jax.experimental import pallas as pl
from jax.experimental.pallas import tpu as pltpu
from jax.sharding import PartitionSpec as P

B = 128
KP = 2
LANES = 128
CWIN = 7
W = 6
BF = jnp.bfloat16
F32 = jnp.float32
SMEM = pltpu.SMEM
ANYWHERE = pl.BlockSpec(memory_space=pl.ANY)
VMEM = pltpu.VMEM


LEFT, OUT_LEFT, OUT_RIGHT, CODE, SLOT_A, SLOT_B, PLAN = 64, 128, 192, 256, 320, 352, 384
HALF = B // 2
MIDDLE = pl.ds(1, CWIN - 2)


def split(x):
    high = x.astype(BF)
    return high, (x - high.astype(F32)).astype(BF)


def left_operand(x):
    high, low = split(x)
    return jnp.concatenate([high, low, high], axis=1)


def right_operand(x):
    high, low = split(x)
    return jnp.concatenate([high, high, low], axis=0)


def matmul(left, right):
    return jnp.dot(left, right, preferred_element_type=F32)


def spread(total, flag, base, pair, slots):
    first, second = pair
    values = {
        base - 1: jnp.where(flag, first, 0.0),
        base: jnp.where(flag, second, first),
        base + 1: jnp.where(flag, 0.0, second),
    }
    for s, value in values.items():
        if s in slots:
            total[s] = value if total.get(s) is None else total[s] + value


def row_product(p_pair, tiles):
    turned = jnp.concatenate([p_pair[0].T, p_pair[1].T], axis=0)
    return matmul(left_operand(turned), right_operand(jnp.concatenate(tiles, axis=1)))


SLOTS = {0: (0, 1, 2, 3), 1: (1, 2, 3), 2: (1, 2, 3, 4)}


def row_copies(plan, c, row, out_a, out_b, out_outer, sems, back=False):
    pairs = (
        (row.at[MIDDLE, pl.ds(0, HALF)], out_a.at[plan[SLOT_A + c]]),
        (row.at[MIDDLE, pl.ds(HALF, HALF)], out_b.at[plan[SLOT_B + c]]),
        (row.at[0], out_outer.at[2 * c]),
        (row.at[CWIN - 1], out_outer.at[2 * c + 1]),
    )
    return [
        pltpu.make_async_copy(*((there, here) if back else (here, there)), sems.at[k])
        for k, (here, there) in enumerate(pairs)
    ]


def main_kernel(
    plan,
    a_ref, p_ref, before_ref, after_ref,
    out_a, out_b, out_outer,
    stage, carry, sems,
):
    step = pl.program_id(0)
    steps = pl.num_programs(0) - 1
    buf = lax.rem(step, 2)

    def copies(at, which, row):
        c = 2 * at - 1 + row
        return row_copies(plan, c, stage.at[which, row], out_a, out_b, out_outer, sems.at[which, row])

    def drain(at):
        which = lax.rem(at, 2)
        for row in range(2):
            @pl.when((2 * at - 1 + row >= 0) & (2 * at - 1 + row < 2 * steps))
            def _():
                for copy in copies(at, which, row):
                    copy.wait()

    @pl.when(step >= 2)
    def _():
        drain(step - 2)

    @pl.when(step == 0)
    def _():
        carry[...] = jnp.zeros_like(carry)

    stage[buf, 0] = carry[0]
    stage[buf, 1] = carry[1]

    @pl.when(step < steps)
    def _():
        carry[...] = jnp.zeros_like(carry)
        first = step * W
        flags = {q: plan[first + q + 4] > 0 for q in range(-1, W + 1)}

        def p_tile(q, m):
            if q < 0:
                return before_ref[0, m]
            if q >= W:
                return after_ref[0, m]
            return p_ref[q, m]

        lefts = {}
        for r in range(W):
            tiles = {
                0: jnp.where(plan[OUT_LEFT + first + r] > 0, a_ref[r, plan[LEFT + first + r]], 0.0),
                1: a_ref[r, 0],
                2: jnp.where(plan[OUT_RIGHT + first + r] > 0, a_ref[r, 3 - plan[LEFT + first + r]], 0.0),
            }
            for k in range(3):
                lefts[r, r + k - 1] = left_operand(tiles[k])
        total = {r: {} for r in range(W)}
        for q in range(-1, W + 1):
            rows = [r for r in (q - 1, q, q + 1) if 0 <= r < W]
            right = right_operand(jnp.concatenate([p_tile(q, 0), p_tile(q, 1)], axis=1))
            product = matmul(jnp.concatenate([lefts[r, q] for r in rows], axis=0), right)
            for n, r in enumerate(rows):
                pair = (product[n * B : (n + 1) * B, :B], product[n * B : (n + 1) * B, B:])
                spread(total[r], flags[q], q // 3 - r // 3 + 2, pair, SLOTS[r % 3])
        for r in range(W):
            slots = SLOTS[r % 3]
            product = row_product((p_ref[r, 0], p_ref[r, 1]), [total[r][s] for s in slots])
            g = r // 3
            for n, s in enumerate(slots):
                one = product[:B, n * B : (n + 1) * B]
                two = product[B:, n * B : (n + 1) * B]
                for delta, value in (
                    (-1, jnp.where(flags[r], one, 0.0)),
                    (0, jnp.where(flags[r], two, one)),
                    (1, jnp.where(flags[r], 0.0, two)),
                ):
                    place = g + delta + 1
                    if place < 2:
                        stage[buf, place, s + 1 - delta] += value
                    else:
                        carry[place - 2, s + 1 - delta] += value

    for row in range(2):
        @pl.when((2 * step - 1 + row >= 0) & (2 * step - 1 + row < 2 * steps))
        def _():
            for copy in copies(step, buf, row):
                copy.start()

    @pl.when(step == steps)
    def _():
        drain(step - 1)
        drain(step)


def main_product(plan, a_tiles, p_tiles, count_y):
    rows = a_tiles.shape[0]
    steps = rows // W
    coarse = rows // 3
    last = steps - 1

    def spec(shape, index):
        return pl.BlockSpec(shape, index)

    return pl.pallas_call(
        main_kernel,
        grid_spec=pltpu.PrefetchScalarGridSpec(
            num_scalar_prefetch=1,
            grid=(steps + 1,),
            in_specs=[
                spec((W, 3, B, B), lambda s, *_: (jnp.minimum(s, last), 0, 0, 0)),
                spec((W, KP, B, B), lambda s, *_: (jnp.minimum(s, last), 0, 0, 0)),
                spec((1, KP, B, B), lambda s, *_: (jnp.maximum(jnp.minimum(s, last) * W - 1, 0), 0, 0, 0)),
                spec((1, KP, B, B), lambda s, *_: (jnp.minimum(s * W + W, rows - 1), 0, 0, 0)),
            ],
            out_specs=[ANYWHERE] * 3,
            scratch_shapes=[
                VMEM((2, 2, CWIN, B, B), F32),
                VMEM((2, CWIN, B, B), F32),
                pltpu.SemaphoreType.DMA((2, 2, 4)),
            ],
        ),
        out_shape=[
            jax.ShapeDtypeStruct((coarse, CWIN - 2, HALF, B), F32),
            jax.ShapeDtypeStruct((count_y, CWIN - 2, HALF, B), F32),
            jax.ShapeDtypeStruct((2 * coarse, B, B), F32),
        ],
        compiler_params=pltpu.CompilerParams(
            dimension_semantics=("arbitrary",), vmem_limit_bytes=56 << 20
        ),
        cost_estimate=pl.CostEstimate(
            flops=16_000_000_000, bytes_accessed=24_000_000, transcendentals=0
        ),
        name="triple_product",
    )(plan, a_tiles, p_tiles, p_tiles, p_tiles)


def edge_kernel(
    plan,
    before, after, a_first, a_last, p_first, p_last, in_a, in_b, in_outer,
    out_a, out_b, out_outer,
    rows_ref, sems,
):
    coarse = out_a.shape[0]
    held = (0, 1, coarse - 2, coarse - 1)

    def copies(n, back):
        return row_copies(plan, held[n], rows_ref.at[n], out_a, out_b, out_outer, sems.at[n], back)

    for n in range(4):
        for copy in copies(n, True):
            copy.start()

    sums = []
    for side in range(2):
        halo = (before, after)[side]
        a_edge = (a_first, a_last)[side]
        own_p = (p_first, p_last)[side]
        own_flag = plan[(4, 3 * coarse + 3)[side]] > 0
        flags, tiles, p_at = {}, {}, {}
        for n in range(4):
            q = n - 1 if side == 0 else n
            flags[q] = plan[(0, 3 * coarse + 4)[side] + n] > 0
            p_at[q] = (halo[9 + 2 * n], halo[10 + 2 * n])
        near = 3 if side == 0 else -1
        flags[near] = own_flag
        p_at[near] = (own_p[0, 0], own_p[0, 1])
        total = {r: {} for r in range(3)}
        total[near] = {}
        for q in range(-1, 4):
            rows = [r for r in (q - 1, q, q + 1) if 0 <= r < 3]
            lefts = [left_operand(halo[3 * r + q - r + 1]) for r in rows]
            if q == (2 if side == 0 else 0):
                rows.append(near)
                lefts.append(left_operand(a_edge[0]))
            right = right_operand(jnp.concatenate(p_at[q], axis=1))
            product = matmul(jnp.concatenate(lefts, axis=0), right)
            for n, r in enumerate(rows):
                pair = (product[n * B : (n + 1) * B, :B], product[n * B : (n + 1) * B, B:])
                base = q // 3 - r // 3 + 2
                slots = SLOTS[r % 3] if r != near else (base - 1, base, base + 1)
                spread(total[r], flags[q], base, pair, slots)
        outer, inner = {}, {}

        def put(target, w, value):
            target[w] = value if w not in target else target[w] + value

        for r in range(3):
            slots = sorted(total[r])
            pick = 1 if side == 0 else 0
            turned = left_operand(p_at[r][pick].T)
            product = matmul(turned, right_operand(jnp.concatenate([total[r][s] for s in slots], axis=1)))
            for n, s in enumerate(slots):
                value = product[:, n * B : (n + 1) * B]
                if side == 0:
                    put(outer, s, jnp.where(flags[r], 0.0, value))
                else:
                    put(outer, s + 2, jnp.where(flags[r], value, 0.0))
        slots = sorted(total[near])
        product = row_product(p_at[near], [total[near][s] for s in slots])
        for n, s in enumerate(slots):
            one = product[:B, n * B : (n + 1) * B]
            two = product[B:, n * B : (n + 1) * B]
            put(outer, s + 1, jnp.where(own_flag, two, one))
            if side == 0:
                put(inner, s, jnp.where(own_flag, 0.0, two))
            else:
                put(inner, s + 2, jnp.where(own_flag, one, 0.0))
        sums.append((outer, inner))

    for n in range(4):
        for copy in copies(n, True):
            copy.wait()
    for n, target in ((0, sums[0][0]), (1, sums[0][1]), (2, sums[1][1]), (3, sums[1][0])):
        for w, value in target.items():
            rows_ref[n, w] += value
    for n in range(4):
        for copy in copies(n, False):
            copy.start()
    for n in range(4):
        for copy in copies(n, False):
            copy.wait()


def edge_product(plan, before, after, up, down, p_tiles, pieces):
    rows = p_tiles.shape[0]

    def whole(x):
        return pl.BlockSpec(x.shape, lambda *_: (0,) * x.ndim)

    return pl.pallas_call(
        edge_kernel,
        grid_spec=pltpu.PrefetchScalarGridSpec(
            num_scalar_prefetch=1,
            grid=(1,),
            in_specs=[whole(before), whole(after)]
            + [
                pl.BlockSpec((1, B, B), lambda *_: (0, 0, 0)),
                pl.BlockSpec((1, B, B), lambda *_: (8, 0, 0)),
                pl.BlockSpec((1, KP, B, B), lambda *_: (0, 0, 0, 0)),
                pl.BlockSpec((1, KP, B, B), lambda *_: (rows - 1, 0, 0, 0)),
            ]
            + [ANYWHERE] * 3,
            out_specs=[ANYWHERE] * 3,
            scratch_shapes=[VMEM((4, CWIN, B, B), F32), pltpu.SemaphoreType.DMA((4, 4))],
        ),
        out_shape=[jax.ShapeDtypeStruct(x.shape, F32) for x in pieces],
        input_output_aliases={7: 0, 8: 1, 9: 2},
        compiler_params=pltpu.CompilerParams(
            dimension_semantics=("arbitrary",), vmem_limit_bytes=32 << 20
        ),
        cost_estimate=pl.CostEstimate(flops=2_000_000_000, bytes_accessed=10_000_000, transcendentals=0),
        name="edge_rows",
    )(plan, before, after, down, up, p_tiles, p_tiles, *pieces)


def plan_kernel(place, cols, length, a_tiles, p_tiles, aggregate, owners, owners_all, plan, counts, up, down, low, high, near, mine_ref, used, sem):
    fine, coarse = length.shape[0], counts.shape[0]
    wide = aggregate.shape[0]
    fine_total = wide * LANES
    first = place[0] * fine
    line = jnp.where(first < 4, wide - 1, (first - 4) >> 7)
    begin = jnp.where(first < 4, LANES - 4, (first - 4) & (LANES - 1))
    lines = (line, jnp.where(line == wide - 1, 0, line + 1))
    index_loads = [
        pltpu.make_async_copy(aggregate.at[pl.ds(at, 1)], near.at[pl.ds(n, 1)], sem.at[n]) for n, at in enumerate(lines)
    ]
    index_loads.append(
        pltpu.make_async_copy(owners.at[pl.ds((place[0] * coarse) >> 7, 1)], mine_ref, sem.at[2])
    )
    for load in index_loads:
        load.start()

    def entry(i):
        before = first + i - 1
        before = jnp.where(before < 0, fine_total - 1, before)
        left = jnp.where(cols[1, i] == before, 1, 2)
        return left, length[i] > left, length[i] > 3 - left

    sends = []
    for out, row, p_row in ((up, fine - 3, fine - 4), (down, 0, 0)):
        for r in range(3):
            left, on_left, on_right = entry(row + r)
            for k, slot, on in ((0, left, on_left), (2, 3 - left, on_right)):
                sends.append((a_tiles.at[row + r, slot], out.at[3 * r + k], on))
            sends.append((a_tiles.at[row + r, 0], out.at[3 * r + 1], None))
        for n in range(4):
            for m in range(KP):
                sends.append((p_tiles.at[p_row + n, m], out.at[9 + 2 * n + m], None))
    for k, (here, there, on) in enumerate(sends):
        if on is None:
            pltpu.make_async_copy(here, there, sem.at[3 + k]).start()
        else:

            @pl.when(on)
            def _():
                pltpu.make_async_copy(here, there, sem.at[3 + k]).start()

            @pl.when(jnp.logical_not(on))
            def _():
                there[...] = jnp.zeros(there.shape, F32)

    def flag(k, carry):
        row = first + k - 4
        row = jnp.where(row < 0, row + fine_total, jnp.where(row >= fine_total, row - fine_total, row))
        at = begin + k
        plan[k] = jnp.where(near[at >> 7, at & (LANES - 1)] != lax.div(row, 3), 1, 0)
        return carry

    for load in index_loads:
        load.wait()
    lax.fori_loop(0, fine + 8, flag, 0, unroll=8)

    def bounds(k, mod, on_left, on_right):
        here = 2 - plan[k + 1]
        left = jnp.where(on_left, (1 if mod == 0 else 2) - plan[k], here)
        right = jnp.where(on_right, (3 if mod == 2 else 2) - plan[k + 2], here)
        low[k] = jnp.minimum(here, jnp.minimum(left, right))
        high[k] = 1 + jnp.maximum(here, jnp.maximum(left, right))

    for mod in range(3):
        bounds(mod, mod, True, True)
        bounds(fine + 3 + mod, mod, True, True)

    def group(g, carry):
        for mod in range(3):
            i = 3 * g + mod
            left, on_left, on_right = entry(i)
            plan[LEFT + i] = left
            plan[OUT_LEFT + i] = jnp.where(on_left & (i > 0), 1, 0)
            plan[OUT_RIGHT + i] = jnp.where(on_right & (i < fine - 1), 1, 0)
            bounds(i + 3, mod, on_left, on_right)
        return carry

    lax.fori_loop(0, coarse, group, 0, unroll=4)
    ids = lax.broadcasted_iota(jnp.int32, counts.shape, 0) * LANES + lax.broadcasted_iota(
        jnp.int32, counts.shape, 1
    )
    everyone = owners_all[...]

    def code(c, carry):
        least, most = jnp.int32(9), jnp.int32(-9)
        for mod in range(3):
            at = 3 * c + mod
            past, next_ = plan[at + 1] == 0, plan[at + 7] == 1
            least = jnp.minimum(least, low[at + 3] + 1)
            most = jnp.maximum(most, high[at + 3] + 1)
            least = jnp.minimum(least, jnp.where(past, low[at], 9))
            most = jnp.maximum(most, jnp.where(past, high[at], -9))
            least = jnp.minimum(least, jnp.where(next_, low[at + 6] + 2, 9))
            most = jnp.maximum(most, jnp.where(next_, high[at + 6] + 2, -9))
        row = place[0] * coarse + c
        mine = mine_ref[0, row & (LANES - 1)]
        spot = jnp.sum(jnp.where((everyone == mine) & (ids < row), 1, 0))
        first_on, last_on = jnp.where(least == 0, 1, 0), jnp.where(most == CWIN - 1, 1, 0)
        whole = mine * 1024 + spot * 64
        plan[CODE + 2 * c] = whole + first_on
        plan[CODE + 2 * c + 1] = whole + (CWIN - 1) * 8 + last_on
        tiles = first_on + last_on
        shift = ((mine >> 5) - (place[0] >> 5)) & 3
        plan[SLOT_A + c] = shift * (coarse // 4) + used[shift]
        plan[SLOT_B + c] = mine & 31
        used[shift] = used[shift] + 1
        return jnp.where(ids == row, tiles, carry)

    for k in range(4):
        used[k] = 0
    tiles = lax.fori_loop(0, coarse, code, jnp.zeros(counts.shape, jnp.int32), unroll=4)
    counts[...] = tiles.astype(F32)
    for k, (here, there, on) in enumerate(sends):
        if on is None:
            pltpu.make_async_copy(here, there, sem.at[3 + k]).wait()
        else:

            @pl.when(on)
            def _():
                pltpu.make_async_copy(here, there, sem.at[3 + k]).wait()


def make_plan(place, a_cols, a_len, aggregate, owner, a_tiles, p_tiles):
    fine = a_len.shape[0]
    coarse = fine // 3
    owners = owner.reshape(-1, LANES)

    def whole(shape):
        return pl.BlockSpec(shape, lambda *_: (0,) * len(shape))

    halo = (9 + 4 * KP, B, B)
    return pl.pallas_call(
        plan_kernel,
        grid_spec=pltpu.PrefetchScalarGridSpec(
            num_scalar_prefetch=3,
            grid=(1,),
            in_specs=[ANYWHERE] * 4 + [whole(owners.shape)],
            out_specs=[
                pl.BlockSpec(memory_space=SMEM),
                whole((coarse, LANES)),
                whole(halo),
                whole(halo),
            ],
            scratch_shapes=[
                SMEM((fine + 6,), jnp.int32),
                SMEM((fine + 6,), jnp.int32),
                SMEM((2, LANES), jnp.int32),
                SMEM((1, LANES), jnp.int32),
                SMEM((4,), jnp.int32),
                pltpu.SemaphoreType.DMA((3 + 2 * halo[0],)),
            ],
        ),
        out_shape=[
            jax.ShapeDtypeStruct((PLAN,), jnp.int32),
            jax.ShapeDtypeStruct((coarse, LANES), F32),
            jax.ShapeDtypeStruct(halo, F32),
            jax.ShapeDtypeStruct(halo, F32),
        ],
        compiler_params=pltpu.CompilerParams(vmem_limit_bytes=60 << 20),
        cost_estimate=pl.CostEstimate(flops=0, bytes_accessed=5_000_000, transcendentals=0),
        name="plan",
    )(place, a_cols.T, a_len, a_tiles, p_tiles, aggregate.reshape(-1, LANES), owners, owners)


PARTS = ((0, 128, "xyz", ((8, 4, 12), (10, 5, 12), (9, 5, 12))),)
SWAP = 12
SHIFT = {"x": 5, "z": 3, "y": 1}
FRONTS, BACKS = LANES - 2, LANES - 1
TABLE = pl.ds(8, 16)


def fields(code):
    return code >> 10, (code >> 6) & 15, (code >> 3) & 7, code & 7


def start_tiles(count, source, target, sem):
    @pl.when(count > 0)
    def _():
        pltpu.make_async_copy(source(0, 1), target(0, 1), sem).start()


def wait_tiles(count, one, sem):
    def step(_, carry):
        pltpu.make_async_copy(one, one, sem).wait()
        return carry

    lax.fori_loop(0, count, step, 0)


class Outer:
    def __init__(self, codes, ref):
        self.codes, self.ref = codes, ref

    def walk(self, body):
        def step(k, carry):
            body(self.codes[CODE + k], lambda first, size: self.ref.at[pl.ds(k + first, size)])
            return carry

        lax.fori_loop(0, self.ref.shape[0], step, 0)


class Slots:
    def __init__(self, header, ref, back):
        self.header, self.ref, self.back = header, ref, back

    def walk(self, body):
        def step(k, at):
            lane = FRONTS - 1 - k if self.back else k
            code = self.header[0, lane].astype(jnp.int32)
            count = code & 7
            slot = at - count if self.back else at
            body(code, lambda first, size: self.ref.at[pl.ds(slot + first, size)])
            return slot if self.back else slot + count

        entries = self.header[0, BACKS if self.back else FRONTS].astype(jnp.int32)
        lax.fori_loop(0, entries, step, self.ref.shape[0] if self.back else 1)


def read_headers(pairs, sem):
    copies = [pltpu.make_async_copy(ref.at[0, pl.ds(0, 1)], header, sem.at[k]) for k, (ref, header) in enumerate(pairs)]
    for copy in copies:
        copy.start()
    for copy in copies:
        copy.wait()


def read_table(arrivals, table_in, sem):
    copies = [pltpu.make_async_copy(x.at[0, TABLE], table_in.at[k], sem.at[k]) for k, x in enumerate(arrivals)]
    for copy in copies:
        copy.start()

    def finish():
        for copy in copies:
            copy.wait()
        table = table_in[0]
        for k in range(1, len(copies)):
            table = jnp.maximum(table, table_in[k])
        return table

    return finish


def route_kernel(stage, behind, plan, place, *refs):
    refs = list(refs)
    parts = len(PARTS)
    if stage == 0:
        arrivals = [[refs.pop(0)]] * parts
        counts = refs.pop(0)
    else:
        arrivals = [[refs.pop(0) for _ in range(5)] for _ in range(parts)]
    del refs[:behind]
    outs_of = [[refs.pop(0) for _ in range(3)] for _ in range(parts)]
    bufs = [refs.pop(0) for _ in range(parts)]
    state, copy_sem, head_sem, out_sem, table_in, table_out, table_sem = [refs.pop(0) for _ in range(7)]
    heads = [[refs.pop(0) for _ in range(3)] for _ in range(parts)]
    odd = (place[0] & 1) == 1
    if stage > 0:
        came = [[refs.pop(0) for _ in range(5)] for _ in range(parts)]
        finish = read_table(arrivals[0], table_in, table_sem)
        read_headers([(arrivals[p][k], came[p][k]) for p in range(parts) for k in range(5)], head_sem)
        table_out[...] = finish()
    else:
        load = pltpu.make_async_copy(counts, table_out, head_sem.at[0])
        load.start()
        load.wait()
    tables = [
        pltpu.make_async_copy(table_out, outs_of[0][way].at[0, TABLE], out_sem.at[9 * parts + way]) for way in range(3)
    ]
    for table in tables:
        table.start()
    writes, kept = [], []

    def write_out(p):
        send, _, stay = PARTS[p][3][stage]
        buf, head, outs, zero = bufs[p], heads[p], outs_of[p], 16 * p
        wait_tiles(state[zero + 15], buf.at[0], copy_sem.at[p])
        fresh = [
            pltpu.make_async_copy(head[way], outs[way].at[0, pl.ds(0, 1)], out_sem.at[9 * p + way]) for way in range(3)
        ]
        for way in range(2):
            fresh.append(
                pltpu.make_async_copy(
                    buf.at[pl.ds(way * (send + 1) + 1, send)],
                    outs[way].at[pl.ds(1, send)],
                    out_sem.at[9 * p + 3 + way],
                )
            )
        for write in fresh:
            write.start()
        writes.extend(fresh)
        chunk = stay // 4
        for k in range(4):
            first = 1 + k * chunk
            write = pltpu.make_async_copy(
                buf.at[pl.ds(2 * (send + 1) + first, chunk)], outs[2].at[pl.ds(first, chunk)], out_sem.at[9 * p + 5 + k]
            )
            used = state[zero + 6] > first
            pl.when(used)(write.start)
            kept.append((used, write))

    for p, (first_row, height, order, sizes) in enumerate(PARTS):
        send, on, stay = sizes[stage]
        shift = SHIFT[order[stage]]
        buf, sem, head, zero = bufs[p], copy_sem.at[p], heads[p], 16 * p
        if stage == 0:
            sources = [Outer(plan, arrivals[p][0])]
        else:
            sources = [
                Slots(h, g, back)
                for h, g, back in zip(came[p], arrivals[p], (False, True, True, False, False))
            ]
        mine = (place[0] >> shift) & 3
        base = (0, send + 1, 2 * (send + 1))

        def turn(code):
            by = (code >> (10 + shift)) - mine
            return jnp.where(odd, -by, by) & 3

        for k in range(4):
            state[zero + k] = 0

        def count(code, source):
            where = turn(code)
            state[zero + where] = state[zero + where] + (code & 7)

        for source in sources:
            source.walk(count)
        ahead, behind, across = state[zero + 1], state[zero + 3], state[zero + 2]
        big, small = jnp.maximum(ahead, behind), jnp.minimum(ahead, behind)
        lesser = jnp.minimum(jnp.minimum(across, (across + big - small + 1) >> 1), on)
        forward = jnp.where(ahead <= behind, lesser, across - lesser)
        for k, value in ((4, 1), (5, 1), (6, 1), (7, send + 1), (8, send + 1), (14, forward)):
            state[zero + k] = value
        for k in (9, 10, 11, 12, 13, 15):
            state[zero + k] = 0

        def put(code, source, skip, tiles, slot):
            start_tiles(
                tiles,
                lambda at, size: source(skip + at, size),
                lambda at, size: buf.at[pl.ds(slot + at, size)],
                sem,
            )
            state[zero + 15] = state[zero + 15] + tiles

        def front(way, code, source, skip, tiles, limit):
            slot = state[zero + 4 + way]
            fits = slot + tiles <= limit
            if way < 2:
                fits = fits & (slot + tiles <= state[zero + 7 + way])

            @pl.when((tiles > 0) & fits)
            def _():
                state[zero + 4 + way] = slot + tiles
                entry = state[zero + 9 + way]
                state[zero + 9 + way] = entry + 1
                sent = (code & ~63) | ((((code >> 3) & 7) + skip) << 3) | tiles
                head[way][0, entry] = sent.astype(F32)
                put(code, source, skip, tiles, base[way] + slot)

        def back(way, code, source):
            tiles = code & 7
            slot = state[zero + 7 + way] - tiles

            @pl.when((tiles > 0) & (slot >= state[zero + 4 + way]))
            def _():
                state[zero + 7 + way] = slot
                entry = state[zero + 12 + way]
                state[zero + 12 + way] = entry + 1
                head[way][0, FRONTS - 1 - entry] = code.astype(F32)
                put(code, source, 0, tiles, base[way] + slot)

        def assign(code, source):
            where = turn(code)
            tiles = code & 7

            @pl.when(where == 0)
            def _():
                front(2, code, source, 0, tiles, stay + 1)

            @pl.when(where == 1)
            def _():
                back(0, code, source)

            @pl.when(where == 3)
            def _():
                back(1, code, source)

            @pl.when(where == 2)
            def _():
                take = jnp.minimum(tiles, state[zero + 14])
                state[zero + 14] = state[zero + 14] - take
                front(0, code, source, 0, take, on + 1)
                front(1, code, source, take, tiles - take, on + 1)

        for source in sources:
            source.walk(assign)
        for way in range(3):
            head[way][0, FRONTS] = state[zero + 9 + way].astype(F32)
            head[way][0, BACKS] = (state[zero + 12 + way] if way < 2 else jnp.int32(0)).astype(F32)
        if p > 0:
            write_out(p - 1)
    write_out(parts - 1)


    for used, write in kept:
        pl.when(used)(write.wait)
    for write in writes + tables:
        write.wait()


def table_scratch():
    return [VMEM((5, 16, LANES), F32), VMEM((16, LANES), F32), pltpu.SemaphoreType.DMA((5,))]


def head_scratch(count):
    return [SMEM((1, LANES), F32)] * count


def route(stage, plan, place, got, *behind):
    parts = len(PARTS)
    sizes = [(size[stage], height) for _, height, _, size in PARTS]
    result = pl.pallas_call(
        functools.partial(route_kernel, stage, len(behind)),
        grid_spec=pltpu.PrefetchScalarGridSpec(
            num_scalar_prefetch=2,
            grid=(1,),
            in_specs=[ANYWHERE] * (len(got) + len(behind)),
            out_specs=[ANYWHERE] * (3 * parts),
            scratch_shapes=[VMEM((2 * (send + 1) + stay + 1, height, LANES), F32) for (send, _, stay), height in sizes]
            + [
                SMEM((16 * parts,), jnp.int32),
                pltpu.SemaphoreType.DMA((parts,)),
                pltpu.SemaphoreType.DMA((5 * parts,)),
                pltpu.SemaphoreType.DMA((9 * parts + 3,)),
            ]
            + table_scratch()
            + head_scratch(3 * parts)
            + ([] if stage == 0 else head_scratch(5 * parts)),
        ),
        out_shape=[
            jax.ShapeDtypeStruct((size + 1, height, LANES), F32)
            for (send, _, stay), height in sizes
            for size in (send, send, stay)
        ],
        compiler_params=pltpu.CompilerParams(vmem_limit_bytes=48 << 20),
        cost_estimate=pl.CostEstimate(flops=0, bytes_accessed=24_000_000, transcendentals=0),
        name="route",
    )(plan, place, *got, *behind)
    return [result[3 * p : 3 * p + 3] for p in range(parts)]


def swap_kernel(place, *refs):
    refs = list(refs)
    parts = len(PARTS)
    got = [[refs.pop(0) for _ in range(5)] for _ in range(parts)]
    outs = [refs.pop(0) for _ in range(parts)]
    bufs = [refs.pop(0) for _ in range(parts)]
    state, copy_sem, head_sem, out_sem, table_in, table_out, table_sem = [refs.pop(0) for _ in range(7)]
    out_heads = [refs.pop(0) for _ in range(parts)]
    heads = [[refs.pop(0) for _ in range(5)] for _ in range(parts)]
    finish = read_table(got[0], table_in, table_sem)
    read_headers([(got[p][k], heads[p][k]) for p in range(parts) for k in range(5)], head_sem)
    core = place[0] & 1
    table_out[...] = finish()
    writes = [pltpu.make_async_copy(table_out, outs[0].at[0, TABLE], out_sem.at[2 * parts])]
    writes[0].start()

    def write_out(p):
        wait_tiles(state[4 * p + 2], bufs[p].at[0], copy_sem.at[p])
        fresh = [
            pltpu.make_async_copy(bufs[p].at[pl.ds(1, SWAP)], outs[p].at[pl.ds(1, SWAP)], out_sem.at[2 * p]),
            pltpu.make_async_copy(out_heads[p], outs[p].at[0, pl.ds(0, 1)], out_sem.at[2 * p + 1]),
        ]
        for write in fresh:
            write.start()
        writes.extend(fresh)

    for p in range(parts):
        buf, sem, head, zero = bufs[p], copy_sem.at[p], out_heads[p], 4 * p
        for k, value in ((0, 1), (1, 0), (2, 0)):
            state[zero + k] = value

        def assign(code, source):
            tiles = code & 7
            slot = state[zero]

            @pl.when((((code >> 10) & 1) != core) & (slot + tiles <= SWAP + 1))
            def _():
                state[zero] = slot + tiles
                entry = state[zero + 1]
                state[zero + 1] = entry + 1
                head[0, entry] = code.astype(F32)
                start_tiles(tiles, source, lambda at, size: buf.at[pl.ds(slot + at, size)], sem)
                state[zero + 2] = state[zero + 2] + tiles

        for h, g, back in zip(heads[p], got[p], (False, True, True, False, False)):
            Slots(h, g, back).walk(assign)
        head[0, FRONTS] = state[zero + 1].astype(F32)
        if p > 0:
            write_out(p - 1)
    write_out(parts - 1)
    for write in writes:
        write.wait()


def swap_out(place, got):
    parts = len(PARTS)
    heights = [height for _, height, _, _ in PARTS]
    inputs = [x for part in got for x in part]
    return pl.pallas_call(
        swap_kernel,
        grid_spec=pltpu.PrefetchScalarGridSpec(
            num_scalar_prefetch=1,
            grid=(1,),
            in_specs=[ANYWHERE] * len(inputs),
            out_specs=[ANYWHERE] * parts,
            scratch_shapes=[VMEM((SWAP + 1, height, LANES), F32) for height in heights]
            + [
                SMEM((4 * parts,), jnp.int32),
                pltpu.SemaphoreType.DMA((parts,)),
                pltpu.SemaphoreType.DMA((5 * parts,)),
                pltpu.SemaphoreType.DMA((2 * parts + 1,)),
            ]
            + table_scratch()
            + head_scratch(6 * parts),
        ),
        out_shape=[jax.ShapeDtypeStruct((SWAP + 1, height, LANES), F32) for height in heights],
        compiler_params=pltpu.CompilerParams(vmem_limit_bytes=48 << 20),
        cost_estimate=pl.CostEstimate(flops=0, bytes_accessed=16_000_000, transcendentals=0),
        name="swap_out",
    )(place, *inputs)


def relay(pairs, sems_in, sems_out):
    inward = [pltpu.make_async_copy(x, y, sems_in.at[k]) for k, (x, y, z) in enumerate(pairs)]
    outward = [pltpu.make_async_copy(y, z, sems_out.at[k]) for k, (x, y, z) in enumerate(pairs)]
    for copy in inward:
        copy.start()
    for come, go in zip(inward, outward):
        come.wait()
        go.start()
    for copy in outward:
        copy.wait()


def move_kernel(source_ref, target_ref, rows_in, rows_out, stage, sems_in, sems_out):
    relay(
        [(rows_in.at[source_ref[k]], stage.at[k], rows_out.at[target_ref[k]]) for k in range(stage.shape[0])],
        sems_in,
        sems_out,
    )


def move_rows(source, target, rows, places):
    count = source.shape[0]
    return pl.pallas_call(
        move_kernel,
        grid_spec=pltpu.PrefetchScalarGridSpec(
            num_scalar_prefetch=2,
            grid=(1,),
            in_specs=[ANYWHERE],
            out_specs=ANYWHERE,
            scratch_shapes=[
                VMEM((count,) + rows.shape[1:], F32),
                pltpu.SemaphoreType.DMA((count,)),
                pltpu.SemaphoreType.DMA((count,)),
            ],
        ),
        out_shape=jax.ShapeDtypeStruct((places,) + rows.shape[1:], F32),
        compiler_params=pltpu.CompilerParams(vmem_limit_bytes=56 << 20),
        cost_estimate=pl.CostEstimate(flops=0, bytes_accessed=8_000_000, transcendentals=0),
        name="move_rows",
    )(source, target, rows)


def join_kernel(source_a, source_b, place, rows_a, rows_b, *refs):
    got, refs = refs[:6], refs[6:]
    out, stage, copied, copy_sem, head_sem, sems_in, sems_out = refs[:7]
    heads = refs[7:]
    coarse = out.shape[0]
    inward, outward = [], []
    for k in range(coarse):
        for h, (rows, source) in enumerate(((rows_a, source_a), (rows_b, source_b))):
            inward.append(
                pltpu.make_async_copy(
                    rows.at[source[k]], stage.at[k, MIDDLE, pl.ds(h * HALF, HALF)], sems_in.at[2 * k + h]
                )
            )
        outward.append(pltpu.make_async_copy(stage.at[k], out.at[k], sems_out.at[k]))
    for copy in inward:
        copy.start()

    def clear(k, carry):
        stage[k, 0] = jnp.zeros((B, B), F32)
        stage[k, CWIN - 1] = jnp.zeros((B, B), F32)
        return carry

    lax.fori_loop(0, coarse, clear, 0)
    read_headers(list(zip(got, heads)), head_sem)
    core = place[0] & 1
    sem = copy_sem.at[0]
    copied[0] = 0

    def assign(code, source):
        owner, row, tile, tiles = fields(code)

        @pl.when((owner & 1) == core)
        def _():
            start_tiles(tiles, source, lambda at, size: stage.at[row, pl.ds(tile + at, size)], sem)
            copied[0] = copied[0] + tiles

    for head, ref, back in zip(heads, got, (False, True, True, False, False, False)):
        Slots(head, ref, back).walk(assign)
    wait_tiles(copied[0], stage.at[0, 0], sem)
    for k in range(coarse):
        inward[2 * k].wait()
        inward[2 * k + 1].wait()
        outward[k].start()
    for copy in outward:
        copy.wait()


def join_rows(source_a, source_b, place, rows_a, rows_b, got):
    coarse = source_a.shape[0]
    return pl.pallas_call(
        join_kernel,
        grid_spec=pltpu.PrefetchScalarGridSpec(
            num_scalar_prefetch=3,
            grid=(1,),
            in_specs=[ANYWHERE] * (2 + len(got)),
            out_specs=ANYWHERE,
            scratch_shapes=[
                VMEM((coarse, CWIN, B, B), F32),
                SMEM((1,), jnp.int32),
                pltpu.SemaphoreType.DMA((1,)),
                pltpu.SemaphoreType.DMA((len(got),)),
                pltpu.SemaphoreType.DMA((2 * coarse,)),
                pltpu.SemaphoreType.DMA((coarse,)),
            ]
            + head_scratch(len(got)),
        ),
        out_shape=jax.ShapeDtypeStruct((coarse, CWIN, B, B), F32),
        compiler_params=pltpu.CompilerParams(vmem_limit_bytes=56 << 20),
        cost_estimate=pl.CostEstimate(flops=0, bytes_accessed=16_000_000, transcendentals=0),
        name="join_rows",
    )(source_a, source_b, place, rows_a, rows_b, *got)


def fits_kernel(owner_ref, one_ref, two_ref, out_ref):
    units = owner_ref.shape[1]
    devices = LANES
    owner = owner_ref[...]
    turned = jnp.maximum(one_ref[0, TABLE], two_ref[0, TABLE])
    tiles = jnp.concatenate([turned[r : r + 1] for r in range(units // devices)], axis=1)
    source = lax.broadcasted_iota(jnp.int32, (1, units), 1) // (units // devices)
    index = lax.broadcasted_iota(jnp.int32, (devices, units), 0)
    kinds = lax.broadcasted_iota(jnp.int32, (8, units), 0)

    def tally(holder, kind):
        left = jnp.where(holder == index, 1.0, 0.0).astype(BF)
        right = jnp.where(kinds == kind, tiles, 0.0).astype(BF)
        return lax.dot_general(left, right, (((1,), (1,)), ((), ())), preferred_element_type=F32)

    def step(holder, shift):
        return holder + ((((owner >> shift) & 3) - ((holder >> shift) & 3)) << shift)

    excess = jnp.full((devices, 1), -1.0, F32)
    holder = source
    for _, _, order, sizes in PARTS:
        holder = source
        for axis, (send, on, stay) in zip(order, sizes):
            shift = SHIFT[axis]
            table = tally(holder, ((owner >> shift) - (holder >> shift)) & 3)
            here, ahead, across, behind = (table[:, k : k + 1] for k in range(4))
            big, small = jnp.maximum(ahead, behind), jnp.minimum(ahead, behind)
            lesser = jnp.minimum(jnp.minimum(across, jnp.floor((across + big - small + 1.0) * 0.5)), float(on))
            greater = across - lesser
            for value, limit in ((small + lesser, send), (big + greater, send), (greater, on), (here, stay)):
                excess = jnp.maximum(excess, value - float(limit))
            holder = step(holder, shift)
    table = tally(holder, (owner ^ holder) & 1)
    excess = jnp.maximum(excess, table[:, 1:2] - float(SWAP))
    out_ref[...] = jnp.broadcast_to(jnp.max(excess, axis=0, keepdims=True), out_ref.shape)


def ring_fits(owner, one, two):
    turned = owner.reshape(1, -1)
    head = pl.BlockSpec((1,) + one.shape[1:], lambda *_: (0, 0, 0))
    return pl.pallas_call(
        fits_kernel,
        grid=(1,),
        in_specs=[pl.BlockSpec(turned.shape, lambda *_: (0, 0)), head, head],
        out_specs=pl.BlockSpec((8, LANES), lambda *_: (0, 0)),
        out_shape=jax.ShapeDtypeStruct((8, LANES), F32),
        compiler_params=pltpu.CompilerParams(vmem_limit_bytes=32 << 20),
        cost_estimate=pl.CostEstimate(flops=100_000_000, bytes_accessed=100_000, transcendentals=0),
        name="ring_fits",
    )(turned, one, two)[0, 0] <= 0.0


AXES = ("gx", "gy")


def neighbours(axis, way):
    shift, size = SHIFT[axis], lax.axis_size(AXES)
    pairs = []
    for i in range(size):
        by = way if i % 2 == 0 else -way
        pairs.append((i, (i & ~(3 << shift)) | ((((i >> shift) + by) & 3) << shift)))
    return pairs


def by_ring(plan, place, outer, counts, waits):
    got = [[outer, counts]]
    for stage in range(3):
        sent = route(stage, plan, place, [x for part in got for x in part], *waits[stage])
        got = []
        for (one, two, stay), (_, _, order, sizes) in zip(sent, PARTS):
            on = sizes[stage][1] + 1
            ways = neighbours(order[stage], 1), neighbours(order[stage], -1)
            came = [lax.ppermute(x, AXES, way) for x, way in zip((one, two), ways)]
            came += [lax.ppermute(x[:on], AXES, way) for x, way in zip(came, ways)]
            got.append([stay] + came)
    size = lax.axis_size(AXES)
    pairs = [(i, i ^ 1) for i in range(size)]
    other = swap_out(place, got)
    swapped = [lax.ppermute(x, AXES, pairs) for x in other]
    return got[0] + [swapped[0]], other[0], swapped[0]


def shards(a_tiles, a_cols, a_len, p_tiles, aggregate, owner):
    count_x, count_y = lax.axis_size("gx"), lax.axis_size("gy")
    index_x, index_y = lax.axis_index("gx"), lax.axis_index("gy")
    size = count_x * count_y
    device = index_x * count_y + index_y
    coarse = a_tiles.shape[0] // 3
    depth = coarse // count_x
    place = jnp.reshape(device, (1,)).astype(jnp.int32)
    plan, counts, up, down = make_plan(place, a_cols, a_len, aggregate, owner, a_tiles, p_tiles)
    before = lax.ppermute(up, AXES, [(i, (i + 1) % size) for i in range(size)])
    behind = lax.ppermute(down, AXES, [((i + 1) % size, i) for i in range(size)])
    pieces = main_product(plan, a_tiles, p_tiles, count_y)
    rows_a, rows_b, outer = edge_product(plan, before, behind, up, down, p_tiles, pieces)

    table = owner.reshape(count_x, count_y, coarse)
    order = jnp.arange(coarse)
    shift = table[0, 0] // count_y
    same = shift[None, :] == shift[:, None]
    rank = jnp.sum((same & (order[None, :] < order[:, None])).astype(jnp.int32), axis=1)
    slot = (shift * depth + rank).astype(jnp.int32)
    from_x = (index_x - shift) % count_x
    column = table[:, index_y] % count_y
    mid_a_target = jnp.sum(
        jnp.where(jnp.arange(count_x)[:, None] == from_x[None, :], column, 0), axis=0
    ).astype(jnp.int32)
    hit = (table[index_x] % count_y) == index_y
    mid_b_source = jnp.sum(jnp.where(hit, jnp.arange(count_y)[:, None], 0), axis=0).astype(jnp.int32)
    found = table.reshape(size, coarse) == device
    sender = jnp.sum(jnp.where(found, jnp.arange(size)[:, None], 0), axis=0)
    ids = sender * coarse + order
    spot = jnp.sum((ids[None, :] < ids[:, None]).astype(jnp.int32), axis=1)
    at = spot[None, :] == order[:, None]
    last_a = jnp.sum(jnp.where(at, (sender % count_y)[None, :], 0), axis=1).astype(jnp.int32)
    last_b = jnp.sum(jnp.where(at, slot[None, :], 0), axis=1).astype(jnp.int32)

    def over_y(x):
        return lax.all_to_all(x, "gy", split_axis=0, concat_axis=0, tiled=True)

    def along_x(x):
        parts = [x[:depth]]
        for k in range(1, count_x):
            pairs = [(i, (i + k) % count_x) for i in range(count_x)]
            parts.append(lax.ppermute(x[k * depth : (k + 1) * depth], "gx", pairs))
        return jnp.concatenate(parts, axis=0)

    got_b = over_y(rows_b)
    got_a = along_x(rows_a)
    ring, one, two = by_ring(plan, place, outer, counts, ((got_a,), (), (got_b,)))
    fits = ring_fits(owner, one, two)
    end_a = over_y(move_rows(slot, mid_a_target, got_a, count_y))
    end_b = along_x(move_rows(mid_b_source, slot, got_b, coarse))

    def slow(*_):
        mine = table[index_x, index_y]
        slots = ((mine // count_y - index_x) % count_x) * depth + rank
        middle = jnp.concatenate([rows_a[slots], rows_b[mine % count_y]], axis=2)
        sides = outer.reshape(coarse, 2, B, B)
        return by_slots(jnp.concatenate([sides[:, :1], middle, sides[:, 1:]], axis=1), owner, device)

    return lax.cond(
        fits, lambda x, y, z: join_rows(last_a, last_b, place, x, y, z), slow, end_a, end_b, ring
    )


def by_slots(complete, owner, device):
    count_x, count_y = lax.axis_size("gx"), lax.axis_size("gy")
    index_x, index_y = device // count_y, device % count_y
    coarse = complete.shape[0]
    depth = coarse // count_x
    table = owner.reshape(count_x, count_y, coarse)
    order = jnp.arange(coarse)
    shift = table[0, 0] // count_y
    same = shift[None, :] == shift[:, None]
    rank = jnp.sum((same & (order[None, :] < order[:, None])).astype(jnp.int32), axis=1)
    mine = table[index_x, index_y]
    slot = (mine // count_y) * depth + rank
    hits = slot[None, :] == order[:, None]
    packed = complete[jnp.sum(jnp.where(hits, order[None, :], 0), axis=1)]
    moved = lax.all_to_all(packed, "gx", split_axis=0, concat_axis=0, tiled=True)
    from_x = (index_x - shift) % count_x
    column = table[:, index_y] % count_y
    target = jnp.sum(jnp.where(jnp.arange(count_x)[:, None] == from_x[None, :], column, 0), axis=0)
    hits = target[None, :] == jnp.arange(count_y)[:, None]
    packed = moved[jnp.sum(jnp.where(hits, (from_x * depth + rank)[None, :], 0), axis=1)]
    moved = lax.all_to_all(packed, "gy", split_axis=0, concat_axis=0, tiled=True)
    found = table.reshape(-1, coarse) == device
    sender = jnp.sum(jnp.where(found, jnp.arange(count_x * count_y)[:, None], 0), axis=0)
    ids = sender * coarse + order
    spot = jnp.sum((ids[None, :] < ids[:, None]).astype(jnp.int32), axis=1)
    hits = spot[None, :] == order[:, None]
    return moved[jnp.sum(jnp.where(hits, (sender % count_y)[None, :], 0), axis=1)]


def solution(mesh):
    in_specs = (
        P(("gx", "gy"), None, None, None),
        P(("gx", "gy"), None),
        P(("gx", "gy")),
        P(("gx", "gy"), None, None, None),
        P(),
        P(),
    )
    out_specs = P(("gx", "gy"), None, None, None)
    return jax.shard_map(shards, mesh=mesh, in_specs=in_specs, out_specs=out_specs, check_vma=False)
```

```python
import functools

import jax
import jax.numpy as jnp
from jax import lax
from jax.experimental import pallas as pl
from jax.experimental.pallas import tpu as pltpu
from jax.sharding import PartitionSpec as P

B = 128
KP = 2
LANES = 128
CWIN = 7
W = 6
BF = jnp.bfloat16
F32 = jnp.float32
SMEM = pltpu.SMEM
ANYWHERE = pl.BlockSpec(memory_space=pl.ANY)
VMEM = pltpu.VMEM


LEFT, OUT_LEFT, OUT_RIGHT, CODE, SLOT_A, SLOT_B, PLAN = 64, 128, 192, 256, 320, 352, 384
HALF = B // 2
MIDDLE = pl.ds(1, CWIN - 2)


def split(x):
    high = x.astype(BF)
    return high, (x - high.astype(F32)).astype(BF)


def left_operand(x):
    high, low = split(x)
    return jnp.concatenate([high, low, high], axis=1)


def right_operand(x):
    high, low = split(x)
    return jnp.concatenate([high, high, low], axis=0)


def matmul(left, right):
    return jnp.dot(left, right, preferred_element_type=F32)


def spread(total, flag, base, pair, slots):
    first, second = pair
    values = {
        base - 1: jnp.where(flag, first, 0.0),
        base: jnp.where(flag, second, first),
        base + 1: jnp.where(flag, 0.0, second),
    }
    for s, value in values.items():
        if s in slots:
            total[s] = value if total.get(s) is None else total[s] + value


def row_product(p_pair, tiles):
    turned = jnp.concatenate([p_pair[0].T, p_pair[1].T], axis=0)
    return matmul(left_operand(turned), right_operand(jnp.concatenate(tiles, axis=1)))


SLOTS = {0: (0, 1, 2, 3), 1: (1, 2, 3), 2: (1, 2, 3, 4)}


def row_copies(plan, c, row, out_a, out_b, out_outer, sems, back=False):
    pairs = (
        (row.at[MIDDLE, pl.ds(0, HALF)], out_a.at[plan[SLOT_A + c]]),
        (row.at[MIDDLE, pl.ds(HALF, HALF)], out_b.at[plan[SLOT_B + c]]),
        (row.at[0], out_outer.at[2 * c]),
        (row.at[CWIN - 1], out_outer.at[2 * c + 1]),
    )
    return [
        pltpu.make_async_copy(*((there, here) if back else (here, there)), sems.at[k])
        for k, (here, there) in enumerate(pairs)
    ]


def main_kernel(
    plan,
    a_ref, p_ref, before_ref, after_ref, behind_ref,
    out_a, out_b, out_outer,
    stage, carry, sems,
):
    step = pl.program_id(0)
    steps = pl.num_programs(0) - 1
    buf = lax.rem(step, 2)

    def copies(at, which, row):
        c = 2 * at - 1 + row
        return row_copies(plan, c, stage.at[which, row], out_a, out_b, out_outer, sems.at[which, row])

    def drain(at):
        which = lax.rem(at, 2)
        for row in range(2):
            @pl.when((2 * at - 1 + row >= 0) & (2 * at - 1 + row < 2 * steps))
            def _():
                for copy in copies(at, which, row):
                    copy.wait()

    @pl.when(step >= 2)
    def _():
        drain(step - 2)

    @pl.when(step == 0)
    def _():
        carry[...] = jnp.zeros_like(carry)

    stage[buf, 0] = carry[0]
    stage[buf, 1] = carry[1]

    @pl.when(step < steps)
    def _():
        carry[...] = jnp.zeros_like(carry)
        first = step * W
        flags = {q: plan[first + q + 4] > 0 for q in range(-1, W + 1)}

        def p_tile(q, m):
            if q < 0:
                return before_ref[0, m]
            if q >= W:
                return after_ref[0, m]
            return p_ref[q, m]

        lefts = {}
        for r in range(W):
            tiles = {
                0: jnp.where(plan[OUT_LEFT + first + r] > 0, a_ref[r, plan[LEFT + first + r]], 0.0),
                1: a_ref[r, 0],
                2: jnp.where(plan[OUT_RIGHT + first + r] > 0, a_ref[r, 3 - plan[LEFT + first + r]], 0.0),
            }
            for k in range(3):
                lefts[r, r + k - 1] = left_operand(tiles[k])
        total = {r: {} for r in range(W)}
        for q in range(-1, W + 1):
            rows = [r for r in (q - 1, q, q + 1) if 0 <= r < W]
            right = right_operand(jnp.concatenate([p_tile(q, 0), p_tile(q, 1)], axis=1))
            product = matmul(jnp.concatenate([lefts[r, q] for r in rows], axis=0), right)
            for n, r in enumerate(rows):
                pair = (product[n * B : (n + 1) * B, :B], product[n * B : (n + 1) * B, B:])
                spread(total[r], flags[q], q // 3 - r // 3 + 2, pair, SLOTS[r % 3])
        for r in range(W):
            slots = SLOTS[r % 3]
            product = row_product((p_ref[r, 0], p_ref[r, 1]), [total[r][s] for s in slots])
            g = r // 3
            for n, s in enumerate(slots):
                one = product[:B, n * B : (n + 1) * B]
                two = product[B:, n * B : (n + 1) * B]
                for delta, value in (
                    (-1, jnp.where(flags[r], one, 0.0)),
                    (0, jnp.where(flags[r], two, one)),
                    (1, jnp.where(flags[r], 0.0, two)),
                ):
                    place = g + delta + 1
                    if place < 2:
                        stage[buf, place, s + 1 - delta] += value
                    else:
                        carry[place - 2, s + 1 - delta] += value

    for row in range(2):
        @pl.when((2 * step - 1 + row >= 0) & (2 * step - 1 + row < 2 * steps))
        def _():
            for copy in copies(step, buf, row):
                copy.start()

    @pl.when(step == steps)
    def _():
        drain(step - 1)
        drain(step)


def main_product(plan, a_tiles, p_tiles, count_y, behind):
    rows = a_tiles.shape[0]
    steps = rows // W
    coarse = rows // 3
    last = steps - 1

    def spec(shape, index):
        return pl.BlockSpec(shape, index)

    return pl.pallas_call(
        main_kernel,
        grid_spec=pltpu.PrefetchScalarGridSpec(
            num_scalar_prefetch=1,
            grid=(steps + 1,),
            in_specs=[
                spec((W, 3, B, B), lambda s, *_: (jnp.minimum(s, last), 0, 0, 0)),
                spec((W, KP, B, B), lambda s, *_: (jnp.minimum(s, last), 0, 0, 0)),
                spec((1, KP, B, B), lambda s, *_: (jnp.maximum(jnp.minimum(s, last) * W - 1, 0), 0, 0, 0)),
                spec((1, KP, B, B), lambda s, *_: (jnp.minimum(s * W + W, rows - 1), 0, 0, 0)),
                ANYWHERE,
            ],
            out_specs=[ANYWHERE] * 3,
            scratch_shapes=[
                VMEM((2, 2, CWIN, B, B), F32),
                VMEM((2, CWIN, B, B), F32),
                pltpu.SemaphoreType.DMA((2, 2, 4)),
            ],
        ),
        out_shape=[
            jax.ShapeDtypeStruct((coarse, CWIN - 2, HALF, B), F32),
            jax.ShapeDtypeStruct((count_y, CWIN - 2, HALF, B), F32),
            jax.ShapeDtypeStruct((2 * coarse, B, B), F32),
        ],
        compiler_params=pltpu.CompilerParams(
            dimension_semantics=("arbitrary",), vmem_limit_bytes=56 << 20
        ),
        cost_estimate=pl.CostEstimate(
            flops=16_000_000_000, bytes_accessed=24_000_000, transcendentals=0
        ),
        name="triple_product",
    )(plan, a_tiles, p_tiles, p_tiles, p_tiles, behind)


def edge_kernel(
    plan,
    before, after, a_first, a_last, p_first, p_last, in_a, in_b, in_outer,
    out_a, out_b, out_outer,
    rows_ref, sems,
):
    coarse = out_a.shape[0]
    held = (0, 1, coarse - 2, coarse - 1)

    def copies(n, back):
        return row_copies(plan, held[n], rows_ref.at[n], out_a, out_b, out_outer, sems.at[n], back)

    for n in range(4):
        for copy in copies(n, True):
            copy.start()

    sums = []
    for side in range(2):
        halo = (before, after)[side]
        a_edge = (a_first, a_last)[side]
        own_p = (p_first, p_last)[side]
        own_flag = plan[(4, 3 * coarse + 3)[side]] > 0
        flags, tiles, p_at = {}, {}, {}
        for n in range(4):
            q = n - 1 if side == 0 else n
            flags[q] = plan[(0, 3 * coarse + 4)[side] + n] > 0
            p_at[q] = (halo[9 + 2 * n], halo[10 + 2 * n])
        near = 3 if side == 0 else -1
        flags[near] = own_flag
        p_at[near] = (own_p[0, 0], own_p[0, 1])
        total = {r: {} for r in range(3)}
        total[near] = {}
        for q in range(-1, 4):
            rows = [r for r in (q - 1, q, q + 1) if 0 <= r < 3]
            lefts = [left_operand(halo[3 * r + q - r + 1]) for r in rows]
            if q == (2 if side == 0 else 0):
                rows.append(near)
                lefts.append(left_operand(a_edge[0]))
            right = right_operand(jnp.concatenate(p_at[q], axis=1))
            product = matmul(jnp.concatenate(lefts, axis=0), right)
            for n, r in enumerate(rows):
                pair = (product[n * B : (n + 1) * B, :B], product[n * B : (n + 1) * B, B:])
                base = q // 3 - r // 3 + 2
                slots = SLOTS[r % 3] if r != near else (base - 1, base, base + 1)
                spread(total[r], flags[q], base, pair, slots)
        outer, inner = {}, {}

        def put(target, w, value):
            target[w] = value if w not in target else target[w] + value

        for r in range(3):
            slots = sorted(total[r])
            pick = 1 if side == 0 else 0
            turned = left_operand(p_at[r][pick].T)
            product = matmul(turned, right_operand(jnp.concatenate([total[r][s] for s in slots], axis=1)))
            for n, s in enumerate(slots):
                value = product[:, n * B : (n + 1) * B]
                if side == 0:
                    put(outer, s, jnp.where(flags[r], 0.0, value))
                else:
                    put(outer, s + 2, jnp.where(flags[r], value, 0.0))
        slots = sorted(total[near])
        product = row_product(p_at[near], [total[near][s] for s in slots])
        for n, s in enumerate(slots):
            one = product[:B, n * B : (n + 1) * B]
            two = product[B:, n * B : (n + 1) * B]
            put(outer, s + 1, jnp.where(own_flag, two, one))
            if side == 0:
                put(inner, s, jnp.where(own_flag, 0.0, two))
            else:
                put(inner, s + 2, jnp.where(own_flag, one, 0.0))
        sums.append((outer, inner))

    for n in range(4):
        for copy in copies(n, True):
            copy.wait()
    for n, target in ((0, sums[0][0]), (1, sums[0][1]), (2, sums[1][1]), (3, sums[1][0])):
        for w, value in target.items():
            rows_ref[n, w] += value
    for n in range(4):
        for copy in copies(n, False):
            copy.start()
    for n in range(4):
        for copy in copies(n, False):
            copy.wait()


def edge_product(plan, before, after, up, down, p_tiles, pieces):
    rows = p_tiles.shape[0]

    def whole(x):
        return pl.BlockSpec(x.shape, lambda *_: (0,) * x.ndim)

    return pl.pallas_call(
        edge_kernel,
        grid_spec=pltpu.PrefetchScalarGridSpec(
            num_scalar_prefetch=1,
            grid=(1,),
            in_specs=[whole(before), whole(after)]
            + [
                pl.BlockSpec((1, B, B), lambda *_: (0, 0, 0)),
                pl.BlockSpec((1, B, B), lambda *_: (8, 0, 0)),
                pl.BlockSpec((1, KP, B, B), lambda *_: (0, 0, 0, 0)),
                pl.BlockSpec((1, KP, B, B), lambda *_: (rows - 1, 0, 0, 0)),
            ]
            + [ANYWHERE] * 3,
            out_specs=[ANYWHERE] * 3,
            scratch_shapes=[VMEM((4, CWIN, B, B), F32), pltpu.SemaphoreType.DMA((4, 4))],
        ),
        out_shape=[jax.ShapeDtypeStruct(x.shape, F32) for x in pieces],
        input_output_aliases={7: 0, 8: 1, 9: 2},
        compiler_params=pltpu.CompilerParams(
            dimension_semantics=("arbitrary",), vmem_limit_bytes=32 << 20
        ),
        cost_estimate=pl.CostEstimate(flops=2_000_000_000, bytes_accessed=10_000_000, transcendentals=0),
        name="edge_rows",
    )(plan, before, after, down, up, p_tiles, p_tiles, *pieces)


def plan_kernel(place, cols, length, a_tiles, p_tiles, aggregate, owners, owners_all, plan, counts, up, down, near, mine_ref, spots, used, sem):
    fine = length.shape[0]
    coarse = fine // 3
    coarse_total = owners.shape[0] * LANES
    wide = aggregate.shape[0]
    fine_total = wide * LANES
    first = place[0] * fine
    line = jnp.where(first < 4, wide - 1, (first - 4) >> 7)
    begin = jnp.where(first < 4, LANES - 4, (first - 4) & (LANES - 1))
    lines = (line, jnp.where(line == wide - 1, 0, line + 1))
    index_loads = [
        pltpu.make_async_copy(aggregate.at[pl.ds(at, 1)], near.at[pl.ds(n, 1)], sem.at[n]) for n, at in enumerate(lines)
    ]
    row_before = (place[0] * coarse - 1) & (coarse_total - 1)
    line = row_before >> 7
    for n, at in enumerate((line, (line + 1) & (owners.shape[0] - 1))):
        index_loads.append(pltpu.make_async_copy(owners.at[pl.ds(at, 1)], mine_ref.at[pl.ds(n, 1)], sem.at[2 + n]))
    for load in index_loads:
        load.start()

    def entry(i):
        before = first + i - 1
        before = jnp.where(before < 0, fine_total - 1, before)
        left = jnp.where(cols[1, i] == before, 1, 2)
        return left, length[i] > left, length[i] > 3 - left

    sends = []
    for out, row, p_row in ((up, fine - 3, fine - 4), (down, 0, 0)):
        for r in range(3):
            left, on_left, on_right = entry(row + r)
            for k, slot, on in ((0, left, on_left), (2, 3 - left, on_right)):
                sends.append((a_tiles.at[row + r, slot], out.at[3 * r + k], on))
            sends.append((a_tiles.at[row + r, 0], out.at[3 * r + 1], None))
        for n in range(4):
            for m in range(KP):
                sends.append((p_tiles.at[p_row + n, m], out.at[9 + 2 * n + m], None))
    for k, (here, there, on) in enumerate(sends):
        if on is None:
            pltpu.make_async_copy(here, there, sem.at[4 + k]).start()
        else:

            @pl.when(on)
            def _():
                pltpu.make_async_copy(here, there, sem.at[4 + k]).start()

            @pl.when(jnp.logical_not(on))
            def _():
                there[...] = jnp.zeros(there.shape, F32)

    def flag(k, carry):
        row = first + k - 4
        row = jnp.where(row < 0, row + fine_total, jnp.where(row >= fine_total, row - fine_total, row))
        at = begin + k
        plan[k] = jnp.where(near[at >> 7, at & (LANES - 1)] != lax.div(row, 3), 1, 0)
        return carry

    for load in index_loads:
        load.wait()
    lax.fori_loop(0, fine + 8, flag, 0, unroll=8)

    def group(g, carry):
        for mod in range(3):
            i = 3 * g + mod
            left, on_left, on_right = entry(i)
            plan[LEFT + i] = left
            plan[OUT_LEFT + i] = jnp.where(on_left & (i > 0), 1, 0)
            plan[OUT_RIGHT + i] = jnp.where(on_right & (i < fine - 1), 1, 0)
            if mod == 0:
                plan[CODE + 2 * g] = jnp.where(on_left & (plan[i + 4] == 0) & (plan[i + 3] == 1), 1, 0)
            if mod == 2:
                plan[CODE + 2 * g + 1] = jnp.where(on_right & (plan[i + 4] == 1) & (plan[i + 5] == 0), 1, 0)
        return carry

    lax.fori_loop(0, coarse, group, 0, unroll=4)
    everyone = owners_all[...]
    ids = lax.broadcasted_iota(jnp.int32, everyone.shape, 0) * LANES + lax.broadcasted_iota(
        jnp.int32, everyone.shape, 1
    )

    def owner_of(k):
        at = (row_before & (LANES - 1)) + k
        return mine_ref[at >> 7, at & (LANES - 1)]

    def spot(k, carry):
        row = (row_before + k) & (coarse_total - 1)
        spots[k] = jnp.sum(jnp.where((everyone == owner_of(k)) & (ids < row), 1, 0))
        return carry

    lax.fori_loop(0, coarse + 2, spot, 0, unroll=6)
    for k in range(4):
        used[k] = 0
    cells = lax.broadcasted_iota(jnp.int32, counts.shape, 0) * LANES + lax.broadcasted_iota(
        jnp.int32, counts.shape, 1
    )

    def code(g, carry):
        for side, k in ((0, g + 2), (1, g)):
            on = plan[CODE + 2 * g + side]
            plan[CODE + 2 * g + side] = owner_of(k) * 1024 + spots[k] * 64 + side * (CWIN - 1) * 8 + on
            cell = side * coarse_total + ((row_before + k) & (coarse_total - 1))
            carry = jnp.where(cells == cell, on, carry)
        mine = owner_of(g + 1)
        shift = ((mine >> 5) - (place[0] >> 5)) & 3
        plan[SLOT_A + g] = shift * (coarse // 4) + used[shift]
        plan[SLOT_B + g] = mine & 31
        used[shift] = used[shift] + 1
        return carry

    ones = lax.fori_loop(0, coarse, code, jnp.zeros(counts.shape, jnp.int32), unroll=4)
    counts[...] = ones.astype(F32)
    for k, (here, there, on) in enumerate(sends):
        if on is None:
            pltpu.make_async_copy(here, there, sem.at[4 + k]).wait()
        else:

            @pl.when(on)
            def _():
                pltpu.make_async_copy(here, there, sem.at[4 + k]).wait()


def make_plan(place, a_cols, a_len, aggregate, owner, a_tiles, p_tiles):
    fine = a_len.shape[0]
    coarse = fine // 3
    owners = owner.reshape(-1, LANES)

    def whole(shape):
        return pl.BlockSpec(shape, lambda *_: (0,) * len(shape))

    halo = (9 + 4 * KP, B, B)
    return pl.pallas_call(
        plan_kernel,
        grid_spec=pltpu.PrefetchScalarGridSpec(
            num_scalar_prefetch=3,
            grid=(1,),
            in_specs=[ANYWHERE] * 4 + [whole(owners.shape)],
            out_specs=[
                pl.BlockSpec(memory_space=SMEM),
                whole((2 * coarse, LANES)),
                whole(halo),
                whole(halo),
            ],
            scratch_shapes=[
                SMEM((2, LANES), jnp.int32),
                SMEM((2, LANES), jnp.int32),
                SMEM((coarse + 2,), jnp.int32),
                SMEM((4,), jnp.int32),
                pltpu.SemaphoreType.DMA((4 + 2 * halo[0],)),
            ],
        ),
        out_shape=[
            jax.ShapeDtypeStruct((PLAN,), jnp.int32),
            jax.ShapeDtypeStruct((2 * coarse, LANES), F32),
            jax.ShapeDtypeStruct(halo, F32),
            jax.ShapeDtypeStruct(halo, F32),
        ],
        compiler_params=pltpu.CompilerParams(vmem_limit_bytes=60 << 20),
        cost_estimate=pl.CostEstimate(flops=0, bytes_accessed=5_000_000, transcendentals=0),
        name="plan",
    )(place, a_cols.T, a_len, a_tiles, p_tiles, aggregate.reshape(-1, LANES), owners, owners)


ORDER = "yzx"
SEND, STAY, SWAP = 8, 10, 11
SHIFT = {"x": 5, "z": 3, "y": 1}
COUNT = LANES - 1
TABLE = pl.ds(8, 32)


def corner_kernel(plan, a_tiles, p_tiles, left, right, out, a_buf, p_buf, result, sems, out_sem):
    fine, count = a_tiles.shape[0], out.shape[0]

    def loads(k):
        side = k & 1
        i = 3 * (k >> 1) + 2 * side
        j = i - 1 + 2 * side
        slot = jnp.where(side == 0, plan[LEFT + i], 3 - plan[LEFT + i])
        inside = (j >= 0) & (j < fine)
        near = jnp.where(inside, j, i)
        return side, inside, (
            pltpu.make_async_copy(a_tiles.at[i, slot], a_buf.at[k], sems.at[k, 0]),
            pltpu.make_async_copy(p_tiles.at[i, 1 - side], p_buf.at[k, 0], sems.at[k, 1]),
            pltpu.make_async_copy(p_tiles.at[near, side], p_buf.at[k, 1], sems.at[k, 2]),
        )

    def active(k):
        return (plan[CODE + k] & 7) > 0

    def back(k):
        return pltpu.make_async_copy(result.at[k], out.at[k], out_sem.at[k])

    def start(k, carry):
        @pl.when(active(k))
        def _():
            for copy in loads(k)[2]:
                copy.start()

        return carry

    def work(k, carry):
        @pl.when(active(k))
        def _():
            side, inside, copies = loads(k)
            for copy in copies:
                copy.wait()
            outside = jnp.where(side == 0, left[...], right[...])
            column = jnp.where(inside, p_buf[k, 1], outside)
            product = matmul(left_operand(a_buf[k]), right_operand(column))
            result[k] = matmul(left_operand(p_buf[k, 0].T), right_operand(product))
            back(k).start()

        return carry

    def finish(k, carry):
        @pl.when(active(k))
        def _():
            back(k).wait()

        return carry

    for step in (start, work, finish):
        lax.fori_loop(0, count, step, 0)


def corner_tiles(plan, a_tiles, p_tiles, left, right):
    count = 2 * (a_tiles.shape[0] // 3)
    tile = pl.BlockSpec((B, B), lambda *_: (0, 0))
    return pl.pallas_call(
        corner_kernel,
        grid_spec=pltpu.PrefetchScalarGridSpec(
            num_scalar_prefetch=1,
            grid=(1,),
            in_specs=[ANYWHERE, ANYWHERE, tile, tile],
            out_specs=ANYWHERE,
            scratch_shapes=[
                VMEM((count, B, B), F32),
                VMEM((count, 2, B, B), F32),
                VMEM((count, B, B), F32),
                pltpu.SemaphoreType.DMA((count, 3)),
                pltpu.SemaphoreType.DMA((count,)),
            ],
        ),
        out_shape=jax.ShapeDtypeStruct((count, B, B), F32),
        compiler_params=pltpu.CompilerParams(vmem_limit_bytes=60 << 20),
        cost_estimate=pl.CostEstimate(flops=100_000_000, bytes_accessed=4_000_000, transcendentals=0),
        name="corner_tiles",
    )(plan, a_tiles, p_tiles, left, right)


def fields(code):
    return code >> 10, (code >> 6) & 15, (code >> 3) & 7, code & 7


def read_headers(refs, heads, table_in, sem):
    copies = [pltpu.make_async_copy(x.at[0, pl.ds(0, 1)], heads.at[pl.ds(k, 1)], sem.at[k]) for k, x in enumerate(refs)]
    copies += [
        pltpu.make_async_copy(x.at[0, TABLE], table_in.at[k], sem.at[len(refs) + k]) for k, x in enumerate(refs)
    ]
    for copy in copies:
        copy.start()
    for copy in copies:
        copy.wait()
    table = table_in[0]
    for k in range(1, len(refs)):
        table = jnp.maximum(table, table_in[k])
    return table


def walk(refs, heads, body):
    for k, ref in enumerate(refs):

        def step(n, carry):
            body(heads[k, n].astype(jnp.int32), ref.at[1 + n])
            return carry

        lax.fori_loop(0, heads[k, COUNT].astype(jnp.int32), step, 0)


def sort_out(outs, sizes, feed, pick, buf, state, heads, table_out, copy_sem, out_sem):
    kinds = len(outs)
    bases = [sum(sizes[:k]) for k in range(kinds)]
    for k in range(kinds + 1):
        state[k] = 0

    def body(code, tile):
        where, wanted = pick(code)
        base, size = jnp.int32(bases[0]), jnp.int32(sizes[0])
        for k in range(1, kinds):
            base, size = jnp.where(where == k, bases[k], base), jnp.where(where == k, sizes[k], size)
        slot = state[where]

        @pl.when(wanted & (slot < size))
        def _():
            state[where] = slot + 1
            state[kinds] = state[kinds] + 1
            heads[where, slot] = code.astype(F32)
            pltpu.make_async_copy(tile, buf.at[base + slot], copy_sem.at[0]).start()

    feed(body)

    def wait(_, carry):
        pltpu.make_async_copy(buf.at[0], buf.at[0], copy_sem.at[0]).wait()
        return carry

    lax.fori_loop(0, state[kinds], wait, 0)
    always, maybe, n = [], [], 0
    for k, out in enumerate(outs):
        heads[k, COUNT] = state[k].astype(F32)
        always.append(pltpu.make_async_copy(heads.at[pl.ds(k, 1)], out.at[0, pl.ds(0, 1)], out_sem.at[n]))
        always.append(pltpu.make_async_copy(table_out, out.at[0, TABLE], out_sem.at[n + 1]))
        n += 2
        for slot in range(sizes[k]):
            copy = pltpu.make_async_copy(buf.at[bases[k] + slot], out.at[1 + slot], out_sem.at[n])
            maybe.append((state[k] > slot, copy))
            n += 1
    for copy in always:
        copy.start()
    for used, copy in maybe:
        pl.when(used)(copy.start)
    for used, copy in maybe:
        pl.when(used)(copy.wait)
    for copy in always:
        copy.wait()


SIZES = (STAY, SEND, SEND, SEND)


def sort_scratch(sizes):
    return [
        VMEM((sum(sizes), B, B), F32),
        SMEM((8,), jnp.int32),
        SMEM((4, LANES), F32),
        SMEM((4, LANES), F32),
        VMEM((4, 32, LANES), F32),
        VMEM((32, LANES), F32),
        pltpu.SemaphoreType.DMA((1,)),
        pltpu.SemaphoreType.DMA((8,)),
        pltpu.SemaphoreType.DMA((sum(sizes) + 2 * len(sizes),)),
    ]


def route_kernel(stage, behind, through, plan, place, *refs):
    refs = list(refs)
    came = [refs.pop(0) for _ in range(2 if stage == 0 else 4)]
    del refs[: behind + through]
    outs = [refs.pop(0) for _ in range(4)]
    del refs[:through]
    buf, state, heads_in, heads, table_in, table_out, copy_sem, head_sem, out_sem = refs
    if stage == 0:
        load = pltpu.make_async_copy(came[1], table_out, head_sem.at[0])
        load.start()
        load.wait()

        def feed(body):
            def step(k, carry):
                body(plan[CODE + k], came[0].at[k])
                return carry

            lax.fori_loop(0, came[0].shape[0], step, 0)
    else:
        table_out[...] = read_headers(came, heads_in, table_in, head_sem)

        def feed(body):
            walk(came, heads_in, body)

    shift = SHIFT[ORDER[stage]]
    mine = (place[0] >> shift) & 3
    odd = (place[0] & 1) == 1

    def pick(code):
        by = (code >> (10 + shift)) - mine
        return jnp.where(odd, -by, by) & 3, (code & 7) > 0

    sort_out(outs, SIZES, feed, pick, buf, state, heads, table_out, copy_sem, out_sem)


def route(stage, plan, place, came, behind=(), through=()):
    outs = [jax.ShapeDtypeStruct((size + 1, B, B), F32) for size in SIZES]
    first = 2 + len(came) + len(behind)
    result = pl.pallas_call(
        functools.partial(route_kernel, stage, len(behind), len(through)),
        grid_spec=pltpu.PrefetchScalarGridSpec(
            num_scalar_prefetch=2,
            grid=(1,),
            in_specs=[ANYWHERE] * (len(came) + len(behind) + len(through)),
            out_specs=[ANYWHERE] * (4 + len(through)),
            scratch_shapes=sort_scratch(SIZES),
        ),
        out_shape=outs + [jax.ShapeDtypeStruct(x.shape, x.dtype) for x in through],
        input_output_aliases={first + k: 4 + k for k in range(len(through))},
        compiler_params=pltpu.CompilerParams(vmem_limit_bytes=24 << 20),
        cost_estimate=pl.CostEstimate(flops=0, bytes_accessed=2_000_000, transcendentals=0),
        name="route",
    )(plan, place, *came, *behind, *through)
    return result[:4], result[4:]


def swap_kernel(place, *refs):
    came, out, scratch = refs[:4], refs[4], refs[5:]
    buf, state, heads_in, heads, table_in, table_out, copy_sem, head_sem, out_sem = scratch
    table_out[...] = read_headers(came, heads_in, table_in, head_sem)

    def pick(code):
        return jnp.int32(0), ((code >> 10) & 1) != (place[0] & 1)

    def feed(body):
        walk(came, heads_in, body)

    sort_out([out], (SWAP,), feed, pick, buf, state, heads, table_out, copy_sem, out_sem)


def swap_out(place, came):
    return pl.pallas_call(
        swap_kernel,
        grid_spec=pltpu.PrefetchScalarGridSpec(
            num_scalar_prefetch=1,
            grid=(1,),
            in_specs=[ANYWHERE] * 4,
            out_specs=ANYWHERE,
            scratch_shapes=sort_scratch((SWAP,)),
        ),
        out_shape=jax.ShapeDtypeStruct((SWAP + 1, B, B), F32),
        compiler_params=pltpu.CompilerParams(vmem_limit_bytes=24 << 20),
        cost_estimate=pl.CostEstimate(flops=0, bytes_accessed=2_000_000, transcendentals=0),
        name="swap_out",
    )(place, *came)


def relay(pairs, sems_in, sems_out):
    inward = [pltpu.make_async_copy(x, y, sems_in.at[k]) for k, (x, y, z) in enumerate(pairs)]
    outward = [pltpu.make_async_copy(y, z, sems_out.at[k]) for k, (x, y, z) in enumerate(pairs)]
    for copy in inward:
        copy.start()
    for come, go in zip(inward, outward):
        come.wait()
        go.start()
    for copy in outward:
        copy.wait()


def move_kernel(source_ref, target_ref, rows_in, rows_out, stage, sems_in, sems_out):
    relay(
        [(rows_in.at[source_ref[k]], stage.at[k], rows_out.at[target_ref[k]]) for k in range(stage.shape[0])],
        sems_in,
        sems_out,
    )


def move_rows(source, target, rows, places):
    count = source.shape[0]
    return pl.pallas_call(
        move_kernel,
        grid_spec=pltpu.PrefetchScalarGridSpec(
            num_scalar_prefetch=2,
            grid=(1,),
            in_specs=[ANYWHERE],
            out_specs=ANYWHERE,
            scratch_shapes=[
                VMEM((count,) + rows.shape[1:], F32),
                pltpu.SemaphoreType.DMA((count,)),
                pltpu.SemaphoreType.DMA((count,)),
            ],
        ),
        out_shape=jax.ShapeDtypeStruct((places,) + rows.shape[1:], F32),
        compiler_params=pltpu.CompilerParams(vmem_limit_bytes=56 << 20),
        cost_estimate=pl.CostEstimate(flops=0, bytes_accessed=8_000_000, transcendentals=0),
        name="move_rows",
    )(source, target, rows)


def join_kernel(source_a, source_b, place, rows_a, rows_b, *refs):
    got, refs = refs[:5], refs[5:]
    out, stage, copied, heads, table_in, copy_sem, head_sem, sems_in, sems_out = refs
    coarse = out.shape[0]
    inward, outward = [], []
    for k in range(coarse):
        for h, (rows, source) in enumerate(((rows_a, source_a), (rows_b, source_b))):
            inward.append(
                pltpu.make_async_copy(
                    rows.at[source[k]], stage.at[k, MIDDLE, pl.ds(h * HALF, HALF)], sems_in.at[2 * k + h]
                )
            )
        outward.append(pltpu.make_async_copy(stage.at[k], out.at[k], sems_out.at[k]))
    for copy in inward:
        copy.start()

    def clear(k, carry):
        stage[k, 0] = jnp.zeros((B, B), F32)
        stage[k, CWIN - 1] = jnp.zeros((B, B), F32)
        return carry

    lax.fori_loop(0, coarse, clear, 0)
    read_headers(got, heads, table_in, head_sem)
    core = place[0] & 1
    sem = copy_sem.at[0]
    copied[0] = 0

    def assign(code, tile):
        owner, row, column, _ = fields(code)

        @pl.when((owner & 1) == core)
        def _():
            pltpu.make_async_copy(tile, stage.at[row, column], sem).start()
            copied[0] = copied[0] + 1

    walk(got, heads, assign)

    def wait(_, carry):
        pltpu.make_async_copy(stage.at[0, 0], stage.at[0, 0], sem).wait()
        return carry

    lax.fori_loop(0, copied[0], wait, 0)
    for k in range(coarse):
        inward[2 * k].wait()
        inward[2 * k + 1].wait()
        outward[k].start()
    for copy in outward:
        copy.wait()


def join_rows(source_a, source_b, place, rows_a, rows_b, got):
    coarse = source_a.shape[0]
    return pl.pallas_call(
        join_kernel,
        grid_spec=pltpu.PrefetchScalarGridSpec(
            num_scalar_prefetch=3,
            grid=(1,),
            in_specs=[ANYWHERE] * (2 + len(got)),
            out_specs=ANYWHERE,
            scratch_shapes=[
                VMEM((coarse, CWIN, B, B), F32),
                SMEM((1,), jnp.int32),
                SMEM((len(got), LANES), F32),
                VMEM((len(got), 32, LANES), F32),
                pltpu.SemaphoreType.DMA((1,)),
                pltpu.SemaphoreType.DMA((2 * len(got),)),
                pltpu.SemaphoreType.DMA((2 * coarse,)),
                pltpu.SemaphoreType.DMA((coarse,)),
            ],
        ),
        out_shape=jax.ShapeDtypeStruct((coarse, CWIN, B, B), F32),
        compiler_params=pltpu.CompilerParams(vmem_limit_bytes=56 << 20),
        cost_estimate=pl.CostEstimate(flops=0, bytes_accessed=16_000_000, transcendentals=0),
        name="join_rows",
    )(source_a, source_b, place, rows_a, rows_b, *got)


def fits_kernel(owner_ref, one_ref, two_ref, out_ref):
    total = owner_ref.shape[1]
    devices, units = LANES, 2 * total
    owner = jnp.concatenate([owner_ref[...]] * 2, axis=1)
    table = jnp.maximum(one_ref[0, TABLE], two_ref[0, TABLE])
    tiles = jnp.concatenate([table[r : r + 1] for r in range(units // LANES)], axis=1)
    unit = lax.broadcasted_iota(jnp.int32, (1, units), 1)
    source = ((unit + jnp.where(unit < total, -1, 1)) & (total - 1)) // (total // devices)
    index = lax.broadcasted_iota(jnp.int32, (devices, units), 0)
    kinds = lax.broadcasted_iota(jnp.int32, (8, units), 0)

    def tally(holder, kind):
        left = jnp.where(holder == index, 1.0, 0.0).astype(BF)
        right = jnp.where(kinds == kind, tiles, 0.0).astype(BF)
        return lax.dot_general(left, right, (((1,), (1,)), ((), ())), preferred_element_type=F32)

    excess = jnp.full((devices, 1), -1.0, F32)
    holder = source
    for axis in ORDER:
        shift = SHIFT[axis]
        by = ((owner >> shift) - (holder >> shift)) & 3
        counts = tally(holder, by)
        for k, size in enumerate(SIZES):
            excess = jnp.maximum(excess, counts[:, k : k + 1] - float(size))
        holder = holder + ((((owner >> shift) & 3) - ((holder >> shift) & 3)) << shift)
    counts = tally(holder, (owner ^ holder) & 1)
    excess = jnp.maximum(excess, counts[:, 1:2] - float(SWAP))
    out_ref[...] = jnp.broadcast_to(jnp.max(excess, axis=0, keepdims=True), out_ref.shape)


def ring_fits(owner, one, two):
    turned = owner.reshape(1, -1)
    head = pl.BlockSpec((1,) + one.shape[1:], lambda *_: (0, 0, 0))
    return pl.pallas_call(
        fits_kernel,
        grid=(1,),
        in_specs=[pl.BlockSpec(turned.shape, lambda *_: (0, 0)), head, head],
        out_specs=pl.BlockSpec((8, LANES), lambda *_: (0, 0)),
        out_shape=jax.ShapeDtypeStruct((8, LANES), F32),
        compiler_params=pltpu.CompilerParams(vmem_limit_bytes=32 << 20),
        cost_estimate=pl.CostEstimate(flops=100_000_000, bytes_accessed=100_000, transcendentals=0),
        name="ring_fits",
    )(turned, one, two)[0, 0] <= 0.0


AXES = ("gx", "gy")


def neighbours(axis, way):
    shift, size = SHIFT[axis], lax.axis_size(AXES)
    pairs = []
    for i in range(size):
        by = way if i % 2 == 0 else -way
        pairs.append((i, (i & ~(3 << shift)) | ((((i >> shift) + by) & 3) << shift)))
    return pairs


def step(stage, sent):
    stay, one, across, two = sent
    shift, size = SHIFT[ORDER[stage]], lax.axis_size(AXES)
    far = [(i, i ^ (2 << shift)) for i in range(size)]
    return [
        stay,
        lax.ppermute(one, AXES, neighbours(ORDER[stage], 1)),
        lax.ppermute(across, AXES, far),
        lax.ppermute(two, AXES, neighbours(ORDER[stage], -1)),
    ]


def shards(a_tiles, a_cols, a_len, p_tiles, aggregate, owner):
    count_x, count_y = lax.axis_size("gx"), lax.axis_size("gy")
    index_x, index_y = lax.axis_index("gx"), lax.axis_index("gy")
    size = count_x * count_y
    device = index_x * count_y + index_y
    coarse = a_tiles.shape[0] // 3
    depth = coarse // count_x
    place = jnp.reshape(device, (1,)).astype(jnp.int32)
    above = [(i, (i + 1) % size) for i in range(size)]
    below = [(j, i) for i, j in above]
    left = lax.ppermute(p_tiles[-1, 0], AXES, above)
    right = lax.ppermute(p_tiles[0, 1], AXES, below)
    plan, counts, up, down = make_plan(place, a_cols, a_len, aggregate, owner, a_tiles, p_tiles)
    before = lax.ppermute(up, AXES, above)
    behind = lax.ppermute(down, AXES, below)
    corners = corner_tiles(plan, a_tiles, p_tiles, left, right)
    sent, _ = route(0, plan, place, [corners, counts])
    came = step(0, sent)
    pieces = main_product(plan, a_tiles, p_tiles, count_y, sent[0])
    rows_a, rows_b, outer = edge_product(plan, before, behind, up, down, p_tiles, pieces)
    sent, (rows_b,) = route(1, plan, place, came, through=(rows_b,))
    came = step(1, sent)

    table = owner.reshape(count_x, count_y, coarse)
    order = jnp.arange(coarse)
    shift = table[0, 0] // count_y
    same = shift[None, :] == shift[:, None]
    rank = jnp.sum((same & (order[None, :] < order[:, None])).astype(jnp.int32), axis=1)
    slot = (shift * depth + rank).astype(jnp.int32)
    from_x = (index_x - shift) % count_x
    column = table[:, index_y] % count_y
    mid_a_target = jnp.sum(
        jnp.where(jnp.arange(count_x)[:, None] == from_x[None, :], column, 0), axis=0
    ).astype(jnp.int32)
    hit = (table[index_x] % count_y) == index_y
    mid_b_source = jnp.sum(jnp.where(hit, jnp.arange(count_y)[:, None], 0), axis=0).astype(jnp.int32)
    found = table.reshape(size, coarse) == device
    sender = jnp.sum(jnp.where(found, jnp.arange(size)[:, None], 0), axis=0)
    ids = sender * coarse + order
    spot = jnp.sum((ids[None, :] < ids[:, None]).astype(jnp.int32), axis=1)
    at = spot[None, :] == order[:, None]
    last_a = jnp.sum(jnp.where(at, (sender % count_y)[None, :], 0), axis=1).astype(jnp.int32)
    last_b = jnp.sum(jnp.where(at, slot[None, :], 0), axis=1).astype(jnp.int32)

    def over_y(x):
        return lax.all_to_all(x, "gy", split_axis=0, concat_axis=0, tiled=True)

    def along_x(x):
        parts = [x[:depth]]
        for k in range(1, count_x):
            pairs = [(i, (i + k) % count_x) for i in range(count_x)]
            parts.append(lax.ppermute(x[k * depth : (k + 1) * depth], "gx", pairs))
        return jnp.concatenate(parts, axis=0)

    got_b = over_y(rows_b)
    got_a = along_x(rows_a)
    sent, _ = route(2, plan, place, came, behind=(got_a,))
    came = step(2, sent)
    one = swap_out(place, came)
    two = lax.ppermute(one, AXES, [(i, i ^ 1) for i in range(size)])
    fits = ring_fits(owner, one, two)
    ring = came + [two]
    end_a = over_y(move_rows(slot, mid_a_target, got_a, count_y))
    end_b = along_x(move_rows(mid_b_source, slot, got_b, coarse))

    def slow(*_):
        mine = table[index_x, index_y]
        slots = ((mine // count_y - index_x) % count_x) * depth + rank
        middle = jnp.concatenate([rows_a[slots], rows_b[mine % count_y]], axis=2)
        sides = outer.reshape(coarse, 2, B, B)
        return by_slots(jnp.concatenate([sides[:, :1], middle, sides[:, 1:]], axis=1), owner, device)

    return lax.cond(
        fits, lambda x, y, z: join_rows(last_a, last_b, place, x, y, z), slow, end_a, end_b, ring
    )


def by_slots(complete, owner, device):
    count_x, count_y = lax.axis_size("gx"), lax.axis_size("gy")
    index_x, index_y = device // count_y, device % count_y
    coarse = complete.shape[0]
    depth = coarse // count_x
    table = owner.reshape(count_x, count_y, coarse)
    order = jnp.arange(coarse)
    shift = table[0, 0] // count_y
    same = shift[None, :] == shift[:, None]
    rank = jnp.sum((same & (order[None, :] < order[:, None])).astype(jnp.int32), axis=1)
    mine = table[index_x, index_y]
    slot = (mine // count_y) * depth + rank
    hits = slot[None, :] == order[:, None]
    packed = complete[jnp.sum(jnp.where(hits, order[None, :], 0), axis=1)]
    moved = lax.all_to_all(packed, "gx", split_axis=0, concat_axis=0, tiled=True)
    from_x = (index_x - shift) % count_x
    column = table[:, index_y] % count_y
    target = jnp.sum(jnp.where(jnp.arange(count_x)[:, None] == from_x[None, :], column, 0), axis=0)
    hits = target[None, :] == jnp.arange(count_y)[:, None]
    packed = moved[jnp.sum(jnp.where(hits, (from_x * depth + rank)[None, :], 0), axis=1)]
    moved = lax.all_to_all(packed, "gy", split_axis=0, concat_axis=0, tiled=True)
    found = table.reshape(-1, coarse) == device
    sender = jnp.sum(jnp.where(found, jnp.arange(count_x * count_y)[:, None], 0), axis=0)
    ids = sender * coarse + order
    spot = jnp.sum((ids[None, :] < ids[:, None]).astype(jnp.int32), axis=1)
    hits = spot[None, :] == order[:, None]
    return moved[jnp.sum(jnp.where(hits, (sender % count_y)[None, :], 0), axis=1)]


def solution(mesh):
    in_specs = (
        P(("gx", "gy"), None, None, None),
        P(("gx", "gy"), None),
        P(("gx", "gy")),
        P(("gx", "gy"), None, None, None),
        P(),
        P(),
    )
    out_specs = P(("gx", "gy"), None, None, None)
    return jax.shard_map(shards, mesh=mesh, in_specs=in_specs, out_specs=out_specs, check_vma=False)
```

```python
import functools

import jax
import jax.numpy as jnp
from jax import lax
from jax.experimental import pallas as pl
from jax.experimental.pallas import tpu as pltpu
from jax.sharding import PartitionSpec as P

B = 128
KP = 2
LANES = 128
CWIN = 7
CB = 16
W = 6
BF = jnp.bfloat16
F32 = jnp.float32
SMEM = pltpu.SMEM
ANYWHERE = pl.BlockSpec(memory_space=pl.ANY)
VMEM = pltpu.VMEM


LEFT, OUT_LEFT, OUT_RIGHT, SLOTS_AT, PLAN = 64, 128, 192, (256, 272), 384
HALF = B // 2


def split(x):
    high = x.astype(BF)
    return high, (x - high.astype(F32)).astype(BF)


def left_operand(x):
    high, low = split(x)
    return jnp.concatenate([high, low, high], axis=1)


def right_operand(x):
    high, low = split(x)
    return jnp.concatenate([high, high, low], axis=0)


def matmul(left, right):
    return jnp.dot(left, right, preferred_element_type=F32)


def spread(total, flag, base, pair, slots):
    first, second = pair
    values = {
        base - 1: jnp.where(flag, first, 0.0),
        base: jnp.where(flag, second, first),
        base + 1: jnp.where(flag, 0.0, second),
    }
    for s, value in values.items():
        if s in slots:
            total[s] = value if total.get(s) is None else total[s] + value


def turn(p_tile, half):
    return p_tile.T[half * HALF : (half + 1) * HALF]


def row_product(p_pair, tiles, half):
    turned = jnp.concatenate([turn(p_pair[0], half), turn(p_pair[1], half)], axis=0)
    return matmul(left_operand(turned), right_operand(jnp.concatenate(tiles, axis=1)))


SLOTS = {0: (0, 1, 2, 3), 1: (1, 2, 3), 2: (1, 2, 3, 4)}


def main_kernel(
    half, plan,
    a_ref, p_ref, before_ref, after_ref, behind_ref,
    out,
    stage, carry, sems,
):
    step = pl.program_id(0)
    steps = pl.num_programs(0) - 1
    buf = lax.rem(step, 2)

    def copy_out(at, which, row):
        c = 2 * at - 1 + row
        return pltpu.make_async_copy(stage.at[which, row], out.at[plan[SLOTS_AT[half] + c]], sems.at[which, row])

    def drain(at):
        which = lax.rem(at, 2)
        for row in range(2):
            @pl.when((2 * at - 1 + row >= 0) & (2 * at - 1 + row < 2 * steps))
            def _():
                copy_out(at, which, row).wait()

    @pl.when(step >= 2)
    def _():
        drain(step - 2)

    @pl.when(step == 0)
    def _():
        carry[...] = jnp.zeros_like(carry)

    stage[buf, 0] = carry[0]
    stage[buf, 1] = carry[1]

    @pl.when(step < steps)
    def _():
        carry[...] = jnp.zeros_like(carry)
        first = step * W
        flags = {q: plan[first + q + 4] > 0 for q in range(-1, W + 1)}

        def p_tile(q, m):
            if q < 0:
                return before_ref[0, m]
            if q >= W:
                return after_ref[0, m]
            return p_ref[q, m]

        lefts = {}
        for r in range(W):
            tiles = {
                0: jnp.where(plan[OUT_LEFT + first + r] > 0, a_ref[r, plan[LEFT + first + r]], 0.0),
                1: a_ref[r, 0],
                2: jnp.where(plan[OUT_RIGHT + first + r] > 0, a_ref[r, 3 - plan[LEFT + first + r]], 0.0),
            }
            for k in range(3):
                lefts[r, r + k - 1] = left_operand(tiles[k])
        total = {r: {} for r in range(W)}
        for q in range(-1, W + 1):
            rows = [r for r in (q - 1, q, q + 1) if 0 <= r < W]
            right = right_operand(jnp.concatenate([p_tile(q, 0), p_tile(q, 1)], axis=1))
            product = matmul(jnp.concatenate([lefts[r, q] for r in rows], axis=0), right)
            for n, r in enumerate(rows):
                pair = (product[n * B : (n + 1) * B, :B], product[n * B : (n + 1) * B, B:])
                spread(total[r], flags[q], q // 3 - r // 3 + 2, pair, SLOTS[r % 3])
        for r in range(W):
            slots = SLOTS[r % 3]
            product = row_product((p_ref[r, 0], p_ref[r, 1]), [total[r][s] for s in slots], half)
            g = r // 3
            for n, s in enumerate(slots):
                one = product[:HALF, n * B : (n + 1) * B]
                two = product[HALF:, n * B : (n + 1) * B]
                for delta, value in (
                    (-1, jnp.where(flags[r], one, 0.0)),
                    (0, jnp.where(flags[r], two, one)),
                    (1, jnp.where(flags[r], 0.0, two)),
                ):
                    place = g + delta + 1
                    if place < 2:
                        stage[buf, place, s + 1 - delta] += value
                    else:
                        carry[place - 2, s + 1 - delta] += value

    for row in range(2):
        @pl.when((2 * step - 1 + row >= 0) & (2 * step - 1 + row < 2 * steps))
        def _():
            copy_out(step, buf, row).start()

    @pl.when(step == steps)
    def _():
        drain(step - 1)
        drain(step)


def main_product(half, plan, a_tiles, p_tiles, places, behind):
    rows = a_tiles.shape[0]
    steps = rows // W
    last = steps - 1

    def spec(shape, index):
        return pl.BlockSpec(shape, index)

    return pl.pallas_call(
        functools.partial(main_kernel, half),
        grid_spec=pltpu.PrefetchScalarGridSpec(
            num_scalar_prefetch=1,
            grid=(steps + 1,),
            in_specs=[
                spec((W, 3, B, B), lambda s, *_: (jnp.minimum(s, last), 0, 0, 0)),
                spec((W, KP, B, B), lambda s, *_: (jnp.minimum(s, last), 0, 0, 0)),
                spec((1, KP, B, B), lambda s, *_: (jnp.maximum(jnp.minimum(s, last) * W - 1, 0), 0, 0, 0)),
                spec((1, KP, B, B), lambda s, *_: (jnp.minimum(s * W + W, rows - 1), 0, 0, 0)),
                ANYWHERE,
            ],
            out_specs=ANYWHERE,
            scratch_shapes=[
                VMEM((2, 2, CWIN, HALF, B), F32),
                VMEM((2, CWIN, HALF, B), F32),
                pltpu.SemaphoreType.DMA((2, 2)),
            ],
        ),
        out_shape=jax.ShapeDtypeStruct((places, CWIN, HALF, B), F32),
        compiler_params=pltpu.CompilerParams(
            dimension_semantics=("arbitrary",), vmem_limit_bytes=56 << 20
        ),
        cost_estimate=pl.CostEstimate(
            flops=12_000_000_000, bytes_accessed=20_000_000, transcendentals=0
        ),
        name="triple_product",
    )(plan, a_tiles, p_tiles, p_tiles, p_tiles, behind)


def edge_kernel(
    half, plan,
    before, after, a_first, a_last, p_first, p_last, in_rows,
    out_rows,
    rows_ref, sems,
):
    coarse = CB
    held = (0, 1, coarse - 2, coarse - 1)

    def copy(n, back):
        there, here = out_rows.at[plan[SLOTS_AT[half] + held[n]]], rows_ref.at[n]
        if back:
            return pltpu.make_async_copy(there, here, sems.at[n])
        return pltpu.make_async_copy(here, there, sems.at[n])

    for n in range(4):
        copy(n, True).start()

    sums = []
    for side in range(2):
        halo = (before, after)[side]
        a_edge = (a_first, a_last)[side]
        own_p = (p_first, p_last)[side]
        own_flag = plan[(4, 3 * coarse + 3)[side]] > 0
        flags, tiles, p_at = {}, {}, {}
        for n in range(4):
            q = n - 1 if side == 0 else n
            flags[q] = plan[(0, 3 * coarse + 4)[side] + n] > 0
            p_at[q] = (halo[9 + 2 * n], halo[10 + 2 * n])
        near = 3 if side == 0 else -1
        flags[near] = own_flag
        p_at[near] = (own_p[0, 0], own_p[0, 1])
        total = {r: {} for r in range(3)}
        total[near] = {}
        for q in range(-1, 4):
            rows = [r for r in (q - 1, q, q + 1) if 0 <= r < 3]
            lefts = [left_operand(halo[3 * r + q - r + 1]) for r in rows]
            if q == (2 if side == 0 else 0):
                rows.append(near)
                lefts.append(left_operand(a_edge[0]))
            right = right_operand(jnp.concatenate(p_at[q], axis=1))
            product = matmul(jnp.concatenate(lefts, axis=0), right)
            for n, r in enumerate(rows):
                pair = (product[n * B : (n + 1) * B, :B], product[n * B : (n + 1) * B, B:])
                base = q // 3 - r // 3 + 2
                slots = SLOTS[r % 3] if r != near else (base - 1, base, base + 1)
                spread(total[r], flags[q], base, pair, slots)
        outer, inner = {}, {}

        def put(target, w, value):
            target[w] = value if w not in target else target[w] + value

        for r in range(3):
            slots = sorted(total[r])
            pick = 1 if side == 0 else 0
            turned = left_operand(turn(p_at[r][pick], half))
            product = matmul(turned, right_operand(jnp.concatenate([total[r][s] for s in slots], axis=1)))
            for n, s in enumerate(slots):
                value = product[:, n * B : (n + 1) * B]
                if side == 0:
                    put(outer, s, jnp.where(flags[r], 0.0, value))
                else:
                    put(outer, s + 2, jnp.where(flags[r], value, 0.0))
        slots = sorted(total[near])
        product = row_product(p_at[near], [total[near][s] for s in slots], half)
        for n, s in enumerate(slots):
            one = product[:HALF, n * B : (n + 1) * B]
            two = product[HALF:, n * B : (n + 1) * B]
            put(outer, s + 1, jnp.where(own_flag, two, one))
            if side == 0:
                put(inner, s, jnp.where(own_flag, 0.0, two))
            else:
                put(inner, s + 2, jnp.where(own_flag, one, 0.0))
        sums.append((outer, inner))

    for n in range(4):
        copy(n, True).wait()
    for n, target in ((0, sums[0][0]), (1, sums[0][1]), (2, sums[1][1]), (3, sums[1][0])):
        for w, value in target.items():
            rows_ref[n, w] += value
    for n in range(4):
        copy(n, False).start()
    for n in range(4):
        copy(n, False).wait()


def edge_product(half, plan, before, after, up, down, p_tiles, out_rows):
    rows = p_tiles.shape[0]

    def whole(x):
        return pl.BlockSpec(x.shape, lambda *_: (0,) * x.ndim)

    return pl.pallas_call(
        functools.partial(edge_kernel, half),
        grid_spec=pltpu.PrefetchScalarGridSpec(
            num_scalar_prefetch=1,
            grid=(1,),
            in_specs=[whole(before), whole(after)]
            + [
                pl.BlockSpec((1, B, B), lambda *_: (0, 0, 0)),
                pl.BlockSpec((1, B, B), lambda *_: (8, 0, 0)),
                pl.BlockSpec((1, KP, B, B), lambda *_: (0, 0, 0, 0)),
                pl.BlockSpec((1, KP, B, B), lambda *_: (rows - 1, 0, 0, 0)),
            ]
            + [ANYWHERE],
            out_specs=ANYWHERE,
            scratch_shapes=[VMEM((4, CWIN, HALF, B), F32), pltpu.SemaphoreType.DMA((4,))],
        ),
        out_shape=jax.ShapeDtypeStruct(out_rows.shape, F32),
        input_output_aliases={7: 0},
        compiler_params=pltpu.CompilerParams(
            dimension_semantics=("arbitrary",), vmem_limit_bytes=32 << 20
        ),
        cost_estimate=pl.CostEstimate(flops=2_000_000_000, bytes_accessed=10_000_000, transcendentals=0),
        name="edge_rows",
    )(plan, before, after, down, up, p_tiles, p_tiles, out_rows)


def plan_kernel(place, cols, length, a_tiles, p_tiles, aggregate, owners, plan, up, down, near, mine_ref, used, sem):
    fine = length.shape[0]
    coarse = fine // 3
    wide = aggregate.shape[0]
    fine_total = wide * LANES
    first = place[0] * fine
    line = jnp.where(first < 4, wide - 1, (first - 4) >> 7)
    begin = jnp.where(first < 4, LANES - 4, (first - 4) & (LANES - 1))
    lines = (line, jnp.where(line == wide - 1, 0, line + 1))
    index_loads = [
        pltpu.make_async_copy(aggregate.at[pl.ds(at, 1)], near.at[pl.ds(n, 1)], sem.at[n]) for n, at in enumerate(lines)
    ]
    own = place[0] * coarse
    index_loads.append(pltpu.make_async_copy(owners.at[pl.ds(own >> 7, 1)], mine_ref, sem.at[2]))
    for load in index_loads:
        load.start()

    def entry(i):
        before = first + i - 1
        before = jnp.where(before < 0, fine_total - 1, before)
        left = jnp.where(cols[1, i] == before, 1, 2)
        return left, length[i] > left, length[i] > 3 - left

    sends = []
    for out, row, p_row in ((up, fine - 3, fine - 4), (down, 0, 0)):
        for r in range(3):
            left, on_left, on_right = entry(row + r)
            for k, slot, on in ((0, left, on_left), (2, 3 - left, on_right)):
                sends.append((a_tiles.at[row + r, slot], out.at[3 * r + k], on))
            sends.append((a_tiles.at[row + r, 0], out.at[3 * r + 1], None))
        for n in range(4):
            for m in range(KP):
                sends.append((p_tiles.at[p_row + n, m], out.at[9 + 2 * n + m], None))
    for k, (here, there, on) in enumerate(sends):
        if on is None:
            pltpu.make_async_copy(here, there, sem.at[3 + k]).start()
        else:

            @pl.when(on)
            def _():
                pltpu.make_async_copy(here, there, sem.at[3 + k]).start()

            @pl.when(jnp.logical_not(on))
            def _():
                there[...] = jnp.zeros(there.shape, F32)

    def flag(k, carry):
        i = first + k - 4
        i = jnp.where(i < 0, i + fine_total, jnp.where(i >= fine_total, i - fine_total, i))
        at = begin + k
        plan[k] = jnp.where(near[at >> 7, at & (LANES - 1)] != lax.div(i, 3), 1, 0)
        return carry

    for load in index_loads:
        load.wait()
    lax.fori_loop(0, fine + 8, flag, 0, unroll=8)

    def group(g, carry):
        for mod in range(3):
            i = 3 * g + mod
            left, on_left, on_right = entry(i)
            plan[LEFT + i] = left
            plan[OUT_LEFT + i] = jnp.where(on_left & (i > 0), 1, 0)
            plan[OUT_RIGHT + i] = jnp.where(on_right & (i < fine - 1), 1, 0)
        return carry

    lax.fori_loop(0, coarse, group, 0, unroll=4)
    for k in range(4):
        used[k] = 0

    def slot(c, carry):
        mine = mine_ref[0, (own + c) & (LANES - 1)]
        shift = ((mine >> 5) - (place[0] >> 5)) & 3
        plan[SLOTS_AT[0] + c] = shift * (coarse // 4) + used[shift]
        plan[SLOTS_AT[1] + c] = mine & 31
        used[shift] = used[shift] + 1
        return carry

    lax.fori_loop(0, coarse, slot, 0)
    for k, (here, there, on) in enumerate(sends):
        if on is None:
            pltpu.make_async_copy(here, there, sem.at[3 + k]).wait()
        else:

            @pl.when(on)
            def _():
                pltpu.make_async_copy(here, there, sem.at[3 + k]).wait()


def make_plan(place, a_cols, a_len, aggregate, owner, a_tiles, p_tiles):
    fine = a_len.shape[0]
    owners = owner.reshape(-1, LANES)

    def whole(shape):
        return pl.BlockSpec(shape, lambda *_: (0,) * len(shape))

    halo = (9 + 4 * KP, B, B)
    return pl.pallas_call(
        plan_kernel,
        grid_spec=pltpu.PrefetchScalarGridSpec(
            num_scalar_prefetch=3,
            grid=(1,),
            in_specs=[ANYWHERE] * 4,
            out_specs=[
                pl.BlockSpec(memory_space=SMEM),
                whole(halo),
                whole(halo),
            ],
            scratch_shapes=[
                SMEM((2, LANES), jnp.int32),
                SMEM((1, LANES), jnp.int32),
                SMEM((4,), jnp.int32),
                pltpu.SemaphoreType.DMA((3 + 2 * halo[0],)),
            ],
        ),
        out_shape=[
            jax.ShapeDtypeStruct((PLAN,), jnp.int32),
            jax.ShapeDtypeStruct(halo, F32),
            jax.ShapeDtypeStruct(halo, F32),
        ],
        compiler_params=pltpu.CompilerParams(vmem_limit_bytes=60 << 20),
        cost_estimate=pl.CostEstimate(flops=0, bytes_accessed=5_000_000, transcendentals=0),
        name="plan",
    )(place, a_cols.T, a_len, a_tiles, p_tiles, aggregate.reshape(-1, LANES), owners)


def relay(pairs, sems_in, sems_out):
    inward = [pltpu.make_async_copy(x, y, sems_in.at[k]) for k, (x, y, z) in enumerate(pairs)]
    outward = [pltpu.make_async_copy(y, z, sems_out.at[k]) for k, (x, y, z) in enumerate(pairs)]
    for copy in inward:
        copy.start()
    for come, go in zip(inward, outward):
        come.wait()
        go.start()
    for copy in outward:
        copy.wait()


def move_kernel(source_ref, target_ref, rows_in, rows_out, stage, sems_in, sems_out):
    relay(
        [(rows_in.at[source_ref[k]], stage.at[k], rows_out.at[target_ref[k]]) for k in range(stage.shape[0])],
        sems_in,
        sems_out,
    )


def move_rows(source, target, rows, places):
    count = source.shape[0]
    return pl.pallas_call(
        move_kernel,
        grid_spec=pltpu.PrefetchScalarGridSpec(
            num_scalar_prefetch=2,
            grid=(1,),
            in_specs=[ANYWHERE],
            out_specs=ANYWHERE,
            scratch_shapes=[
                VMEM((count,) + rows.shape[1:], F32),
                pltpu.SemaphoreType.DMA((count,)),
                pltpu.SemaphoreType.DMA((count,)),
            ],
        ),
        out_shape=jax.ShapeDtypeStruct((places,) + rows.shape[1:], F32),
        compiler_params=pltpu.CompilerParams(vmem_limit_bytes=56 << 20),
        cost_estimate=pl.CostEstimate(flops=0, bytes_accessed=8_000_000, transcendentals=0),
        name="move_rows",
    )(source, target, rows)


def put_kernel(half, source, rows, *refs):
    out, stage, sems_in, sems_out = refs[-4:]
    part = pl.ds(half * HALF, HALF)
    relay(
        [(rows.at[source[k]], stage.at[k], out.at[k, :, part]) for k in range(stage.shape[0])], sems_in, sems_out
    )


def put_rows(half, source, rows, whole=None):
    count = source.shape[0]
    held = [] if whole is None else [whole]
    return pl.pallas_call(
        functools.partial(put_kernel, half),
        grid_spec=pltpu.PrefetchScalarGridSpec(
            num_scalar_prefetch=1,
            grid=(1,),
            in_specs=[ANYWHERE] * (1 + len(held)),
            out_specs=ANYWHERE,
            scratch_shapes=[
                VMEM((count,) + rows.shape[1:], F32),
                pltpu.SemaphoreType.DMA((count,)),
                pltpu.SemaphoreType.DMA((count,)),
            ],
        ),
        out_shape=jax.ShapeDtypeStruct((count, CWIN, B, B), F32),
        input_output_aliases={2: 0} if held else {},
        compiler_params=pltpu.CompilerParams(vmem_limit_bytes=60 << 20),
        cost_estimate=pl.CostEstimate(flops=0, bytes_accessed=8_000_000, transcendentals=0),
        name="put_rows",
    )(source, rows, *held)


AXES = ("gx", "gy")


def shards(a_tiles, a_cols, a_len, p_tiles, aggregate, owner):
    count_x, count_y = lax.axis_size("gx"), lax.axis_size("gy")
    index_x, index_y = lax.axis_index("gx"), lax.axis_index("gy")
    size = count_x * count_y
    device = index_x * count_y + index_y
    coarse = a_tiles.shape[0] // 3
    depth = coarse // count_x
    place = jnp.reshape(device, (1,)).astype(jnp.int32)
    plan, up, down = make_plan(place, a_cols, a_len, aggregate, owner, a_tiles, p_tiles)
    above = [(i, (i + 1) % size) for i in range(size)]
    below = [(j, i) for i, j in above]
    before = lax.ppermute(up, AXES, above)
    behind = lax.ppermute(down, AXES, below)

    def half_rows(half, places, after):
        rows = main_product(half, plan, a_tiles, p_tiles, places, after)
        return edge_product(half, plan, before, behind, up, down, p_tiles, rows)

    rows_b = half_rows(1, count_y, plan)
    rows_a = half_rows(0, coarse, rows_b)

    table = owner.reshape(count_x, count_y, coarse)
    order = jnp.arange(coarse)
    shift = table[0, 0] // count_y
    same = shift[None, :] == shift[:, None]
    rank = jnp.sum((same & (order[None, :] < order[:, None])).astype(jnp.int32), axis=1)
    slot = (shift * depth + rank).astype(jnp.int32)
    from_x = (index_x - shift) % count_x
    column = table[:, index_y] % count_y
    mid_a_target = jnp.sum(
        jnp.where(jnp.arange(count_x)[:, None] == from_x[None, :], column, 0), axis=0
    ).astype(jnp.int32)
    hit = (table[index_x] % count_y) == index_y
    mid_b_source = jnp.sum(jnp.where(hit, jnp.arange(count_y)[:, None], 0), axis=0).astype(jnp.int32)
    found = table.reshape(size, coarse) == device
    sender = jnp.sum(jnp.where(found, jnp.arange(size)[:, None], 0), axis=0)
    ids = sender * coarse + order
    spot = jnp.sum((ids[None, :] < ids[:, None]).astype(jnp.int32), axis=1)
    at = spot[None, :] == order[:, None]
    last_a = jnp.sum(jnp.where(at, (sender % count_y)[None, :], 0), axis=1).astype(jnp.int32)
    last_b = jnp.sum(jnp.where(at, slot[None, :], 0), axis=1).astype(jnp.int32)

    def over_y(x):
        return lax.all_to_all(x, "gy", split_axis=0, concat_axis=0, tiled=True)

    def along_x(x):
        parts = [x[:depth]]
        for k in range(1, count_x):
            pairs = [(i, (i + k) % count_x) for i in range(count_x)]
            parts.append(lax.ppermute(x[k * depth : (k + 1) * depth], "gx", pairs))
        return jnp.concatenate(parts, axis=0)

    got_b = over_y(rows_b)
    got_a = along_x(rows_a)
    end_a = over_y(move_rows(slot, mid_a_target, got_a, count_y))
    end_b = along_x(move_rows(mid_b_source, slot, got_b, coarse))
    return put_rows(0, last_a, end_a, put_rows(1, last_b, end_b))


def solution(mesh):
    in_specs = (
        P(("gx", "gy"), None, None, None),
        P(("gx", "gy"), None),
        P(("gx", "gy")),
        P(("gx", "gy"), None, None, None),
        P(),
        P(),
    )
    out_specs = P(("gx", "gy"), None, None, None)
    return jax.shard_map(shards, mesh=mesh, in_specs=in_specs, out_specs=out_specs, check_vma=False)
```

```python
import functools

import jax
import jax.numpy as jnp
from jax import lax
from jax.experimental import pallas as pl
from jax.experimental.pallas import tpu as pltpu
from jax.sharding import PartitionSpec as P

B = 128
KP = 2
LANES = 128
CWIN = 7
CB = 16
W = 12
G = W // 3
BF = jnp.bfloat16
F32 = jnp.float32
SMEM = pltpu.SMEM
ANYWHERE = pl.BlockSpec(memory_space=pl.ANY)
VMEM = pltpu.VMEM


LEFT, OUT_LEFT, OUT_RIGHT, SLOTS_AT, PLAN = 64, 128, 192, (256, 272), 384
HALF = B // 2


def split(x):
    high = x.astype(BF)
    return high, (x - high.astype(F32)).astype(BF)


def left_operand(x):
    high, low = split(x)
    return jnp.concatenate([high, low, high], axis=1)


def right_operand(x):
    high, low = split(x)
    return jnp.concatenate([high, high, low], axis=0)


def matmul(left, right):
    return jnp.dot(left, right, preferred_element_type=F32)


def spread(total, flag, base, pair, slots):
    first, second = pair
    values = {
        base - 1: jnp.where(flag, first, 0.0),
        base: jnp.where(flag, second, first),
        base + 1: jnp.where(flag, 0.0, second),
    }
    for s, value in values.items():
        if s in slots:
            total[s] = value if total.get(s) is None else total[s] + value


def turn(p_tile, half):
    return p_tile.T[half * HALF : (half + 1) * HALF]


def row_product(p_pair, tiles, half):
    turned = jnp.concatenate([turn(p_pair[0], half), turn(p_pair[1], half)], axis=0)
    return matmul(left_operand(turned), right_operand(jnp.concatenate(tiles, axis=1)))


SLOTS = {0: (0, 1, 2, 3), 1: (1, 2, 3), 2: (1, 2, 3, 4)}


def main_kernel(
    half, plan,
    a_ref, p_ref, before_ref, after_ref, behind_ref,
    out,
    stage, carry, sems,
):
    step = pl.program_id(0)
    steps = pl.num_programs(0) - 1
    buf = lax.rem(step, 2)

    def copy_out(at, which, row):
        c = G * at - 1 + row
        return pltpu.make_async_copy(stage.at[which, row], out.at[plan[SLOTS_AT[half] + c]], sems.at[which, row])

    def drain(at):
        which = lax.rem(at, 2)
        for row in range(G):
            @pl.when((G * at - 1 + row >= 0) & (G * at - 1 + row < G * steps))
            def _():
                copy_out(at, which, row).wait()

    @pl.when(step >= 2)
    def _():
        drain(step - 2)

    @pl.when(step == 0)
    def _():
        carry[...] = jnp.zeros_like(carry)

    stage[buf, 0] = carry[0]
    stage[buf, 1] = carry[1]
    for row in range(2, G):
        stage[buf, row] = jnp.zeros(carry.shape[1:], F32)

    @pl.when(step < steps)
    def _():
        carry[...] = jnp.zeros_like(carry)
        first = step * W
        flags = {q: plan[first + q + 4] > 0 for q in range(-1, W + 1)}

        def p_tile(q, m):
            if q < 0:
                return before_ref[0, m]
            if q >= W:
                return after_ref[0, m]
            return p_ref[q, m]

        def a_tile(r, q):
            if q == r:
                return a_ref[r, 0]
            at = first + r
            if q < r:
                return jnp.where(plan[OUT_LEFT + at] > 0, a_ref[r, plan[LEFT + at]], 0.0)
            return jnp.where(plan[OUT_RIGHT + at] > 0, a_ref[r, 3 - plan[LEFT + at]], 0.0)

        total = {r: {} for r in range(W)}
        for q in range(-1, W + 1):
            rows = [r for r in (q - 1, q, q + 1) if 0 <= r < W]
            right = right_operand(jnp.concatenate([p_tile(q, 0), p_tile(q, 1)], axis=1))
            product = matmul(jnp.concatenate([left_operand(a_tile(r, q)) for r in rows], axis=0), right)
            for n, r in enumerate(rows):
                pair = (product[n * B : (n + 1) * B, :B], product[n * B : (n + 1) * B, B:])
                spread(total[r], flags[q], q // 3 - r // 3 + 2, pair, SLOTS[r % 3])
            r = q - 1
            if r < 0:
                continue
            slots = SLOTS[r % 3]
            product = row_product((p_ref[r, 0], p_ref[r, 1]), [total[r][s] for s in slots], half)
            g = r // 3
            for n, s in enumerate(slots):
                one = product[:HALF, n * B : (n + 1) * B]
                two = product[HALF:, n * B : (n + 1) * B]
                for delta, value in (
                    (-1, jnp.where(flags[r], one, 0.0)),
                    (0, jnp.where(flags[r], two, one)),
                    (1, jnp.where(flags[r], 0.0, two)),
                ):
                    place = g + delta + 1
                    if place < G:
                        stage[buf, place, s + 1 - delta] += value
                    else:
                        carry[place - G, s + 1 - delta] += value

    for row in range(G):
        @pl.when((G * step - 1 + row >= 0) & (G * step - 1 + row < G * steps))
        def _():
            copy_out(step, buf, row).start()

    @pl.when(step == steps)
    def _():
        drain(step - 1)
        drain(step)


def main_product(half, plan, a_tiles, p_tiles, places, behind):
    rows = a_tiles.shape[0]
    steps = rows // W
    last = steps - 1

    def spec(shape, index):
        return pl.BlockSpec(shape, index)

    return pl.pallas_call(
        functools.partial(main_kernel, half),
        grid_spec=pltpu.PrefetchScalarGridSpec(
            num_scalar_prefetch=1,
            grid=(steps + 1,),
            in_specs=[
                spec((W, 3, B, B), lambda s, *_: (jnp.minimum(s, last), 0, 0, 0)),
                spec((W, KP, B, B), lambda s, *_: (jnp.minimum(s, last), 0, 0, 0)),
                spec((1, KP, B, B), lambda s, *_: (jnp.maximum(jnp.minimum(s, last) * W - 1, 0), 0, 0, 0)),
                spec((1, KP, B, B), lambda s, *_: (jnp.minimum(s * W + W, rows - 1), 0, 0, 0)),
                ANYWHERE,
            ],
            out_specs=ANYWHERE,
            scratch_shapes=[
                VMEM((2, G, CWIN, HALF, B), F32),
                VMEM((2, CWIN, HALF, B), F32),
                pltpu.SemaphoreType.DMA((2, G)),
            ],
        ),
        out_shape=jax.ShapeDtypeStruct((places, CWIN, HALF, B), F32),
        compiler_params=pltpu.CompilerParams(
            dimension_semantics=("arbitrary",), vmem_limit_bytes=56 << 20
        ),
        cost_estimate=pl.CostEstimate(
            flops=12_000_000_000, bytes_accessed=20_000_000, transcendentals=0
        ),
        name="triple_product",
    )(plan, a_tiles, p_tiles, p_tiles, p_tiles, behind)


def edge_kernel(
    half, plan,
    before, after, a_first, a_last, p_first, p_last, in_rows,
    out_rows,
    rows_ref, sems,
):
    coarse = CB
    held = (0, 1, coarse - 2, coarse - 1)

    def copy(n, back):
        there, here = out_rows.at[plan[SLOTS_AT[half] + held[n]]], rows_ref.at[n]
        if back:
            return pltpu.make_async_copy(there, here, sems.at[n])
        return pltpu.make_async_copy(here, there, sems.at[n])

    for n in range(4):
        copy(n, True).start()

    sums = []
    for side in range(2):
        halo = (before, after)[side]
        a_edge = (a_first, a_last)[side]
        own_p = (p_first, p_last)[side]
        own_flag = plan[(4, 3 * coarse + 3)[side]] > 0
        flags, tiles, p_at = {}, {}, {}
        for n in range(4):
            q = n - 1 if side == 0 else n
            flags[q] = plan[(0, 3 * coarse + 4)[side] + n] > 0
            p_at[q] = (halo[9 + 2 * n], halo[10 + 2 * n])
        near = 3 if side == 0 else -1
        flags[near] = own_flag
        p_at[near] = (own_p[0, 0], own_p[0, 1])
        total = {r: {} for r in range(3)}
        total[near] = {}
        for q in range(-1, 4):
            rows = [r for r in (q - 1, q, q + 1) if 0 <= r < 3]
            lefts = [left_operand(halo[3 * r + q - r + 1]) for r in rows]
            if q == (2 if side == 0 else 0):
                rows.append(near)
                lefts.append(left_operand(a_edge[0]))
            right = right_operand(jnp.concatenate(p_at[q], axis=1))
            product = matmul(jnp.concatenate(lefts, axis=0), right)
            for n, r in enumerate(rows):
                pair = (product[n * B : (n + 1) * B, :B], product[n * B : (n + 1) * B, B:])
                base = q // 3 - r // 3 + 2
                slots = SLOTS[r % 3] if r != near else (base - 1, base, base + 1)
                spread(total[r], flags[q], base, pair, slots)
        outer, inner = {}, {}

        def put(target, w, value):
            target[w] = value if w not in target else target[w] + value

        for r in range(3):
            slots = sorted(total[r])
            pick = 1 if side == 0 else 0
            turned = left_operand(turn(p_at[r][pick], half))
            product = matmul(turned, right_operand(jnp.concatenate([total[r][s] for s in slots], axis=1)))
            for n, s in enumerate(slots):
                value = product[:, n * B : (n + 1) * B]
                if side == 0:
                    put(outer, s, jnp.where(flags[r], 0.0, value))
                else:
                    put(outer, s + 2, jnp.where(flags[r], value, 0.0))
        slots = sorted(total[near])
        product = row_product(p_at[near], [total[near][s] for s in slots], half)
        for n, s in enumerate(slots):
            one = product[:HALF, n * B : (n + 1) * B]
            two = product[HALF:, n * B : (n + 1) * B]
            put(outer, s + 1, jnp.where(own_flag, two, one))
            if side == 0:
                put(inner, s, jnp.where(own_flag, 0.0, two))
            else:
                put(inner, s + 2, jnp.where(own_flag, one, 0.0))
        sums.append((outer, inner))

    for n in range(4):
        copy(n, True).wait()
    for n, target in ((0, sums[0][0]), (1, sums[0][1]), (2, sums[1][1]), (3, sums[1][0])):
        for w, value in target.items():
            rows_ref[n, w] += value
    for n in range(4):
        copy(n, False).start()
    for n in range(4):
        copy(n, False).wait()


def edge_product(half, plan, before, after, up, down, p_tiles, out_rows):
    rows = p_tiles.shape[0]

    def whole(x):
        return pl.BlockSpec(x.shape, lambda *_: (0,) * x.ndim)

    return pl.pallas_call(
        functools.partial(edge_kernel, half),
        grid_spec=pltpu.PrefetchScalarGridSpec(
            num_scalar_prefetch=1,
            grid=(1,),
            in_specs=[whole(before), whole(after)]
            + [
                pl.BlockSpec((1, B, B), lambda *_: (0, 0, 0)),
                pl.BlockSpec((1, B, B), lambda *_: (8, 0, 0)),
                pl.BlockSpec((1, KP, B, B), lambda *_: (0, 0, 0, 0)),
                pl.BlockSpec((1, KP, B, B), lambda *_: (rows - 1, 0, 0, 0)),
            ]
            + [ANYWHERE],
            out_specs=ANYWHERE,
            scratch_shapes=[VMEM((4, CWIN, HALF, B), F32), pltpu.SemaphoreType.DMA((4,))],
        ),
        out_shape=jax.ShapeDtypeStruct(out_rows.shape, F32),
        input_output_aliases={7: 0},
        compiler_params=pltpu.CompilerParams(
            dimension_semantics=("arbitrary",), vmem_limit_bytes=60 << 20
        ),
        cost_estimate=pl.CostEstimate(flops=2_000_000_000, bytes_accessed=10_000_000, transcendentals=0),
        name="edge_rows",
    )(plan, before, after, down, up, p_tiles, p_tiles, out_rows)


def plan_kernel(place, cols, length, a_tiles, p_tiles, aggregate, owners, plan, up, down, near, mine_ref, used, sem):
    fine = length.shape[0]
    coarse = fine // 3
    wide = aggregate.shape[0]
    fine_total = wide * LANES
    first = place[0] * fine
    line = jnp.where(first < 4, wide - 1, (first - 4) >> 7)
    begin = jnp.where(first < 4, LANES - 4, (first - 4) & (LANES - 1))
    lines = (line, jnp.where(line == wide - 1, 0, line + 1))
    index_loads = [
        pltpu.make_async_copy(aggregate.at[pl.ds(at, 1)], near.at[pl.ds(n, 1)], sem.at[n]) for n, at in enumerate(lines)
    ]
    own = place[0] * coarse
    index_loads.append(pltpu.make_async_copy(owners.at[pl.ds(own >> 7, 1)], mine_ref, sem.at[2]))
    for load in index_loads:
        load.start()

    def entry(i):
        before = first + i - 1
        before = jnp.where(before < 0, fine_total - 1, before)
        left = jnp.where(cols[1, i] == before, 1, 2)
        return left, length[i] > left, length[i] > 3 - left

    sends = []
    for out, row, p_row in ((up, fine - 3, fine - 4), (down, 0, 0)):
        for r in range(3):
            left, on_left, on_right = entry(row + r)
            for k, slot, on in ((0, left, on_left), (2, 3 - left, on_right)):
                sends.append((a_tiles.at[row + r, slot], out.at[3 * r + k], on))
            sends.append((a_tiles.at[row + r, 0], out.at[3 * r + 1], None))
        for n in range(4):
            for m in range(KP):
                sends.append((p_tiles.at[p_row + n, m], out.at[9 + 2 * n + m], None))
    for k, (here, there, on) in enumerate(sends):
        if on is None:
            pltpu.make_async_copy(here, there, sem.at[3 + k]).start()
        else:

            @pl.when(on)
            def _():
                pltpu.make_async_copy(here, there, sem.at[3 + k]).start()

            @pl.when(jnp.logical_not(on))
            def _():
                there[...] = jnp.zeros(there.shape, F32)

    def flag(k, carry):
        i = first + k - 4
        i = jnp.where(i < 0, i + fine_total, jnp.where(i >= fine_total, i - fine_total, i))
        at = begin + k
        plan[k] = jnp.where(near[at >> 7, at & (LANES - 1)] != lax.div(i, 3), 1, 0)
        return carry

    for load in index_loads:
        load.wait()
    lax.fori_loop(0, fine + 8, flag, 0, unroll=8)

    def group(g, carry):
        for mod in range(3):
            i = 3 * g + mod
            left, on_left, on_right = entry(i)
            plan[LEFT + i] = left
            plan[OUT_LEFT + i] = jnp.where(on_left & (i > 0), 1, 0)
            plan[OUT_RIGHT + i] = jnp.where(on_right & (i < fine - 1), 1, 0)
        return carry

    lax.fori_loop(0, coarse, group, 0, unroll=4)
    for k in range(4):
        used[k] = 0

    def slot(c, carry):
        mine = mine_ref[0, (own + c) & (LANES - 1)]
        shift = ((mine >> 5) - (place[0] >> 5)) & 3
        plan[SLOTS_AT[0] + c] = shift * (coarse // 4) + used[shift]
        plan[SLOTS_AT[1] + c] = mine & 31
        used[shift] = used[shift] + 1
        return carry

    lax.fori_loop(0, coarse, slot, 0)
    for k, (here, there, on) in enumerate(sends):
        if on is None:
            pltpu.make_async_copy(here, there, sem.at[3 + k]).wait()
        else:

            @pl.when(on)
            def _():
                pltpu.make_async_copy(here, there, sem.at[3 + k]).wait()


def make_plan(place, a_cols, a_len, aggregate, owner, a_tiles, p_tiles):
    fine = a_len.shape[0]
    owners = owner.reshape(-1, LANES)

    def whole(shape):
        return pl.BlockSpec(shape, lambda *_: (0,) * len(shape))

    halo = (9 + 4 * KP, B, B)
    return pl.pallas_call(
        plan_kernel,
        grid_spec=pltpu.PrefetchScalarGridSpec(
            num_scalar_prefetch=3,
            grid=(1,),
            in_specs=[ANYWHERE] * 4,
            out_specs=[
                pl.BlockSpec(memory_space=SMEM),
                whole(halo),
                whole(halo),
            ],
            scratch_shapes=[
                SMEM((2, LANES), jnp.int32),
                SMEM((1, LANES), jnp.int32),
                SMEM((4,), jnp.int32),
                pltpu.SemaphoreType.DMA((3 + 2 * halo[0],)),
            ],
        ),
        out_shape=[
            jax.ShapeDtypeStruct((PLAN,), jnp.int32),
            jax.ShapeDtypeStruct(halo, F32),
            jax.ShapeDtypeStruct(halo, F32),
        ],
        compiler_params=pltpu.CompilerParams(vmem_limit_bytes=60 << 20),
        cost_estimate=pl.CostEstimate(flops=0, bytes_accessed=5_000_000, transcendentals=0),
        name="plan",
    )(place, a_cols.T, a_len, a_tiles, p_tiles, aggregate.reshape(-1, LANES), owners)


def relay(pairs, sems_in, sems_out):
    inward = [pltpu.make_async_copy(x, y, sems_in.at[k]) for k, (x, y, z) in enumerate(pairs)]
    outward = [pltpu.make_async_copy(y, z, sems_out.at[k]) for k, (x, y, z) in enumerate(pairs)]
    for copy in inward:
        copy.start()
    for come, go in zip(inward, outward):
        come.wait()
        go.start()
    for copy in outward:
        copy.wait()


def move_kernel(source_ref, target_ref, rows_in, rows_out, stage, sems_in, sems_out):
    relay(
        [(rows_in.at[source_ref[k]], stage.at[k], rows_out.at[target_ref[k]]) for k in range(stage.shape[0])],
        sems_in,
        sems_out,
    )


def move_rows(source, target, rows, places):
    count = source.shape[0]
    return pl.pallas_call(
        move_kernel,
        grid_spec=pltpu.PrefetchScalarGridSpec(
            num_scalar_prefetch=2,
            grid=(1,),
            in_specs=[ANYWHERE],
            out_specs=ANYWHERE,
            scratch_shapes=[
                VMEM((count,) + rows.shape[1:], F32),
                pltpu.SemaphoreType.DMA((count,)),
                pltpu.SemaphoreType.DMA((count,)),
            ],
        ),
        out_shape=jax.ShapeDtypeStruct((places,) + rows.shape[1:], F32),
        compiler_params=pltpu.CompilerParams(vmem_limit_bytes=56 << 20),
        cost_estimate=pl.CostEstimate(flops=0, bytes_accessed=8_000_000, transcendentals=0),
        name="move_rows",
    )(source, target, rows)


def put_kernel(half, source, rows, *refs):
    out, stage, sems_in, sems_out = refs[-4:]
    part = pl.ds(half * HALF, HALF)
    relay(
        [(rows.at[source[k]], stage.at[k], out.at[k, :, part]) for k in range(stage.shape[0])], sems_in, sems_out
    )


def put_rows(half, source, rows, whole=None):
    count = source.shape[0]
    held = [] if whole is None else [whole]
    return pl.pallas_call(
        functools.partial(put_kernel, half),
        grid_spec=pltpu.PrefetchScalarGridSpec(
            num_scalar_prefetch=1,
            grid=(1,),
            in_specs=[ANYWHERE] * (1 + len(held)),
            out_specs=ANYWHERE,
            scratch_shapes=[
                VMEM((count,) + rows.shape[1:], F32),
                pltpu.SemaphoreType.DMA((count,)),
                pltpu.SemaphoreType.DMA((count,)),
            ],
        ),
        out_shape=jax.ShapeDtypeStruct((count, CWIN, B, B), F32),
        input_output_aliases={2: 0} if held else {},
        compiler_params=pltpu.CompilerParams(vmem_limit_bytes=60 << 20),
        cost_estimate=pl.CostEstimate(flops=0, bytes_accessed=8_000_000, transcendentals=0),
        name="put_rows",
    )(source, rows, *held)


AXES = ("gx", "gy")


def shards(a_tiles, a_cols, a_len, p_tiles, aggregate, owner):
    count_x, count_y = lax.axis_size("gx"), lax.axis_size("gy")
    index_x, index_y = lax.axis_index("gx"), lax.axis_index("gy")
    size = count_x * count_y
    device = index_x * count_y + index_y
    coarse = a_tiles.shape[0] // 3
    depth = coarse // count_x
    place = jnp.reshape(device, (1,)).astype(jnp.int32)
    plan, up, down = make_plan(place, a_cols, a_len, aggregate, owner, a_tiles, p_tiles)
    above = [(i, (i + 1) % size) for i in range(size)]
    below = [(j, i) for i, j in above]
    before = lax.ppermute(up, AXES, above)
    behind = lax.ppermute(down, AXES, below)

    def half_rows(half, places, after):
        rows = main_product(half, plan, a_tiles, p_tiles, places, after)
        return edge_product(half, plan, before, behind, up, down, p_tiles, rows)

    rows_b = half_rows(1, count_y, plan)
    rows_a = half_rows(0, coarse, rows_b)

    table = owner.reshape(count_x, count_y, coarse)
    order = jnp.arange(coarse)
    shift = table[0, 0] // count_y
    same = shift[None, :] == shift[:, None]
    rank = jnp.sum((same & (order[None, :] < order[:, None])).astype(jnp.int32), axis=1)
    slot = (shift * depth + rank).astype(jnp.int32)
    from_x = (index_x - shift) % count_x
    column = table[:, index_y] % count_y
    mid_a_target = jnp.sum(
        jnp.where(jnp.arange(count_x)[:, None] == from_x[None, :], column, 0), axis=0
    ).astype(jnp.int32)
    hit = (table[index_x] % count_y) == index_y
    mid_b_source = jnp.sum(jnp.where(hit, jnp.arange(count_y)[:, None], 0), axis=0).astype(jnp.int32)
    found = table.reshape(size, coarse) == device
    sender = jnp.sum(jnp.where(found, jnp.arange(size)[:, None], 0), axis=0)
    ids = sender * coarse + order
    spot = jnp.sum((ids[None, :] < ids[:, None]).astype(jnp.int32), axis=1)
    at = spot[None, :] == order[:, None]
    last_a = jnp.sum(jnp.where(at, (sender % count_y)[None, :], 0), axis=1).astype(jnp.int32)
    last_b = jnp.sum(jnp.where(at, slot[None, :], 0), axis=1).astype(jnp.int32)

    def over_y(x):
        return lax.all_to_all(x, "gy", split_axis=0, concat_axis=0, tiled=True)

    def along_x(x):
        parts = [x[:depth]]
        for k in range(1, count_x):
            pairs = [(i, (i + k) % count_x) for i in range(count_x)]
            parts.append(lax.ppermute(x[k * depth : (k + 1) * depth], "gx", pairs))
        return jnp.concatenate(parts, axis=0)

    got_b = over_y(rows_b)
    got_a = along_x(rows_a)
    end_a = over_y(move_rows(slot, mid_a_target, got_a, count_y))
    end_b = along_x(move_rows(mid_b_source, slot, got_b, coarse))
    return put_rows(0, last_a, end_a, put_rows(1, last_b, end_b))


def solution(mesh):
    in_specs = (
        P(("gx", "gy"), None, None, None),
        P(("gx", "gy"), None),
        P(("gx", "gy")),
        P(("gx", "gy"), None, None, None),
        P(),
        P(),
    )
    out_specs = P(("gx", "gy"), None, None, None)
    return jax.shard_map(shards, mesh=mesh, in_specs=in_specs, out_specs=out_specs, check_vma=False)
```

```python
import functools

import jax
import jax.numpy as jnp
from jax import lax
from jax.experimental import pallas as pl
from jax.experimental.pallas import tpu as pltpu
from jax.sharding import PartitionSpec as P

B = 128
KP = 2
LANES = 128
CWIN = 7
CB = 16
W = 6
BF = jnp.bfloat16
F32 = jnp.float32
SMEM = pltpu.SMEM
ANYWHERE = pl.BlockSpec(memory_space=pl.ANY)
VMEM = pltpu.VMEM


LEFT, OUT_LEFT, OUT_RIGHT, SLOTS_AT, PLAN = 64, 128, 192, (256, 272), 384
HALF = B // 2


def split(x):
    high = x.astype(BF)
    return high, (x - high.astype(F32)).astype(BF)


def left_operand(x):
    high, low = split(x)
    return jnp.concatenate([high, low, high], axis=1)


def right_operand(x):
    high, low = split(x)
    return jnp.concatenate([high, high, low], axis=0)


def matmul(left, right):
    return jnp.dot(left, right, preferred_element_type=F32)


def spread(total, flag, base, pair, slots):
    first, second = pair
    values = {
        base - 1: jnp.where(flag, first, 0.0),
        base: jnp.where(flag, second, first),
        base + 1: jnp.where(flag, 0.0, second),
    }
    for s, value in values.items():
        if s in slots:
            total[s] = value if total.get(s) is None else total[s] + value


def turn(p_tile, half):
    return p_tile.T[half * HALF : (half + 1) * HALF]


def row_product(p_pair, tiles, half):
    turned = jnp.concatenate([turn(p_pair[0], half), turn(p_pair[1], half)], axis=0)
    return matmul(left_operand(turned), right_operand(jnp.concatenate(tiles, axis=1)))


SLOTS = {0: (0, 1, 2, 3), 1: (1, 2, 3), 2: (1, 2, 3, 4)}


def main_kernel(
    half, plan,
    a_ref, p_ref, before_ref, after_ref, behind_ref,
    out,
    stage, carry, sems,
):
    step = pl.program_id(0)
    steps = pl.num_programs(0) - 1
    buf = lax.rem(step, 2)

    def copy_out(at, which, row):
        c = 2 * at - 1 + row
        return pltpu.make_async_copy(stage.at[which, row], out.at[plan[SLOTS_AT[half] + c]], sems.at[which, row])

    def drain(at):
        which = lax.rem(at, 2)
        for row in range(2):
            @pl.when((2 * at - 1 + row >= 0) & (2 * at - 1 + row < 2 * steps))
            def _():
                copy_out(at, which, row).wait()

    @pl.when(step >= 2)
    def _():
        drain(step - 2)

    @pl.when(step == 0)
    def _():
        carry[...] = jnp.zeros_like(carry)

    @pl.when(step == steps)
    def _():
        stage[buf, 0] = carry[0]

    @pl.when(step < steps)
    def _():
        sums = {(place, w): carry[place, w] for place in range(2) for w in range(CWIN)}
        first = step * W
        flags = {q: plan[first + q + 4] > 0 for q in range(-1, W + 1)}

        def p_tile(q, m):
            if q < 0:
                return before_ref[0, m]
            if q >= W:
                return after_ref[0, m]
            return p_ref[q, m]

        lefts = {}
        for r in range(W):
            tiles = {
                0: jnp.where(plan[OUT_LEFT + first + r] > 0, a_ref[r, plan[LEFT + first + r]], 0.0),
                1: a_ref[r, 0],
                2: jnp.where(plan[OUT_RIGHT + first + r] > 0, a_ref[r, 3 - plan[LEFT + first + r]], 0.0),
            }
            for k in range(3):
                lefts[r, r + k - 1] = left_operand(tiles[k])
        total = {r: {} for r in range(W)}
        for q in range(-1, W + 1):
            rows = [r for r in (q - 1, q, q + 1) if 0 <= r < W]
            right = right_operand(jnp.concatenate([p_tile(q, 0), p_tile(q, 1)], axis=1))
            product = matmul(jnp.concatenate([lefts[r, q] for r in rows], axis=0), right)
            for n, r in enumerate(rows):
                pair = (product[n * B : (n + 1) * B, :B], product[n * B : (n + 1) * B, B:])
                spread(total[r], flags[q], q // 3 - r // 3 + 2, pair, SLOTS[r % 3])
        for r in range(W):
            slots = SLOTS[r % 3]
            product = row_product((p_ref[r, 0], p_ref[r, 1]), [total[r][s] for s in slots], half)
            g = r // 3
            for n, s in enumerate(slots):
                one = product[:HALF, n * B : (n + 1) * B]
                two = product[HALF:, n * B : (n + 1) * B]
                for delta, value in (
                    (-1, jnp.where(flags[r], one, 0.0)),
                    (0, jnp.where(flags[r], two, one)),
                    (1, jnp.where(flags[r], 0.0, two)),
                ):
                    key = (g + delta + 1, s + 1 - delta)
                    sums[key] = value if key not in sums else sums[key] + value
        for place in range(4):
            for w in range(CWIN):
                value = sums.get((place, w))
                if value is None:
                    value = jnp.zeros((HALF, B), F32)
                if place < 2:
                    stage[buf, place, w] = value
                else:
                    carry[place - 2, w] = value

    for row in range(2):
        @pl.when((2 * step - 1 + row >= 0) & (2 * step - 1 + row < 2 * steps))
        def _():
            copy_out(step, buf, row).start()

    @pl.when(step == steps)
    def _():
        drain(step - 1)
        drain(step)


def main_product(half, plan, a_tiles, p_tiles, places, behind):
    rows = a_tiles.shape[0]
    steps = rows // W
    last = steps - 1

    def spec(shape, index):
        return pl.BlockSpec(shape, index)

    return pl.pallas_call(
        functools.partial(main_kernel, half),
        grid_spec=pltpu.PrefetchScalarGridSpec(
            num_scalar_prefetch=1,
            grid=(steps + 1,),
            in_specs=[
                spec((W, 3, B, B), lambda s, *_: (jnp.minimum(s, last), 0, 0, 0)),
                spec((W, KP, B, B), lambda s, *_: (jnp.minimum(s, last), 0, 0, 0)),
                spec((1, KP, B, B), lambda s, *_: (jnp.maximum(jnp.minimum(s, last) * W - 1, 0), 0, 0, 0)),
                spec((1, KP, B, B), lambda s, *_: (jnp.minimum(s * W + W, rows - 1), 0, 0, 0)),
                ANYWHERE,
            ],
            out_specs=ANYWHERE,
            scratch_shapes=[
                VMEM((2, 2, CWIN, HALF, B), F32),
                VMEM((2, CWIN, HALF, B), F32),
                pltpu.SemaphoreType.DMA((2, 2)),
            ],
        ),
        out_shape=jax.ShapeDtypeStruct((places, CWIN, HALF, B), F32),
        compiler_params=pltpu.CompilerParams(
            dimension_semantics=("arbitrary",), vmem_limit_bytes=56 << 20
        ),
        cost_estimate=pl.CostEstimate(
            flops=12_000_000_000, bytes_accessed=20_000_000, transcendentals=0
        ),
        name="triple_product",
    )(plan, a_tiles, p_tiles, p_tiles, p_tiles, behind)


def edge_kernel(
    half, plan,
    before, after, a_first, a_last, p_first, p_last, in_rows,
    out_rows,
    rows_ref, sems,
):
    coarse = CB
    held = (0, 1, coarse - 2, coarse - 1)

    def copy(n, back):
        there, here = out_rows.at[plan[SLOTS_AT[half] + held[n]]], rows_ref.at[n]
        if back:
            return pltpu.make_async_copy(there, here, sems.at[n])
        return pltpu.make_async_copy(here, there, sems.at[n])

    for n in range(4):
        copy(n, True).start()

    sums = []
    for side in range(2):
        halo = (before, after)[side]
        a_edge = (a_first, a_last)[side]
        own_p = (p_first, p_last)[side]
        own_flag = plan[(4, 3 * coarse + 3)[side]] > 0
        flags, tiles, p_at = {}, {}, {}
        for n in range(4):
            q = n - 1 if side == 0 else n
            flags[q] = plan[(0, 3 * coarse + 4)[side] + n] > 0
            p_at[q] = (halo[9 + 2 * n], halo[10 + 2 * n])
        near = 3 if side == 0 else -1
        flags[near] = own_flag
        p_at[near] = (own_p[0, 0], own_p[0, 1])
        total = {r: {} for r in range(3)}
        total[near] = {}
        for q in range(-1, 4):
            rows = [r for r in (q - 1, q, q + 1) if 0 <= r < 3]
            lefts = [left_operand(halo[3 * r + q - r + 1]) for r in rows]
            if q == (2 if side == 0 else 0):
                rows.append(near)
                lefts.append(left_operand(a_edge[0]))
            right = right_operand(jnp.concatenate(p_at[q], axis=1))
            product = matmul(jnp.concatenate(lefts, axis=0), right)
            for n, r in enumerate(rows):
                pair = (product[n * B : (n + 1) * B, :B], product[n * B : (n + 1) * B, B:])
                base = q // 3 - r // 3 + 2
                slots = SLOTS[r % 3] if r != near else (base - 1, base, base + 1)
                spread(total[r], flags[q], base, pair, slots)
        outer, inner = {}, {}

        def put(target, w, value):
            target[w] = value if w not in target else target[w] + value

        for r in range(3):
            slots = sorted(total[r])
            pick = 1 if side == 0 else 0
            turned = left_operand(turn(p_at[r][pick], half))
            product = matmul(turned, right_operand(jnp.concatenate([total[r][s] for s in slots], axis=1)))
            for n, s in enumerate(slots):
                value = product[:, n * B : (n + 1) * B]
                if side == 0:
                    put(outer, s, jnp.where(flags[r], 0.0, value))
                else:
                    put(outer, s + 2, jnp.where(flags[r], value, 0.0))
        slots = sorted(total[near])
        product = row_product(p_at[near], [total[near][s] for s in slots], half)
        for n, s in enumerate(slots):
            one = product[:HALF, n * B : (n + 1) * B]
            two = product[HALF:, n * B : (n + 1) * B]
            put(outer, s + 1, jnp.where(own_flag, two, one))
            if side == 0:
                put(inner, s, jnp.where(own_flag, 0.0, two))
            else:
                put(inner, s + 2, jnp.where(own_flag, one, 0.0))
        sums.append((outer, inner))

    for n in range(4):
        copy(n, True).wait()
    for n, target in ((0, sums[0][0]), (1, sums[0][1]), (2, sums[1][1]), (3, sums[1][0])):
        for w, value in target.items():
            rows_ref[n, w] += value
    for n in range(4):
        copy(n, False).start()
    for n in range(4):
        copy(n, False).wait()


def edge_product(half, plan, before, after, up, down, p_tiles, out_rows):
    rows = p_tiles.shape[0]

    def whole(x):
        return pl.BlockSpec(x.shape, lambda *_: (0,) * x.ndim)

    return pl.pallas_call(
        functools.partial(edge_kernel, half),
        grid_spec=pltpu.PrefetchScalarGridSpec(
            num_scalar_prefetch=1,
            grid=(1,),
            in_specs=[whole(before), whole(after)]
            + [
                pl.BlockSpec((1, B, B), lambda *_: (0, 0, 0)),
                pl.BlockSpec((1, B, B), lambda *_: (8, 0, 0)),
                pl.BlockSpec((1, KP, B, B), lambda *_: (0, 0, 0, 0)),
                pl.BlockSpec((1, KP, B, B), lambda *_: (rows - 1, 0, 0, 0)),
            ]
            + [ANYWHERE],
            out_specs=ANYWHERE,
            scratch_shapes=[VMEM((4, CWIN, HALF, B), F32), pltpu.SemaphoreType.DMA((4,))],
        ),
        out_shape=jax.ShapeDtypeStruct(out_rows.shape, F32),
        input_output_aliases={7: 0},
        compiler_params=pltpu.CompilerParams(
            dimension_semantics=("arbitrary",), vmem_limit_bytes=60 << 20
        ),
        cost_estimate=pl.CostEstimate(flops=2_000_000_000, bytes_accessed=10_000_000, transcendentals=0),
        name="edge_rows",
    )(plan, before, after, down, up, p_tiles, p_tiles, out_rows)


def plan_kernel(place, cols, length, a_tiles, p_tiles, aggregate, owners, plan, up, down, near, mine_ref, used, sem):
    fine = length.shape[0]
    coarse = fine // 3
    wide = aggregate.shape[0]
    fine_total = wide * LANES
    first = place[0] * fine
    line = jnp.where(first < 4, wide - 1, (first - 4) >> 7)
    begin = jnp.where(first < 4, LANES - 4, (first - 4) & (LANES - 1))
    lines = (line, jnp.where(line == wide - 1, 0, line + 1))
    index_loads = [
        pltpu.make_async_copy(aggregate.at[pl.ds(at, 1)], near.at[pl.ds(n, 1)], sem.at[n]) for n, at in enumerate(lines)
    ]
    own = place[0] * coarse
    index_loads.append(pltpu.make_async_copy(owners.at[pl.ds(own >> 7, 1)], mine_ref, sem.at[2]))
    for load in index_loads:
        load.start()

    def entry(i):
        before = first + i - 1
        before = jnp.where(before < 0, fine_total - 1, before)
        left = jnp.where(cols[1, i] == before, 1, 2)
        return left, length[i] > left, length[i] > 3 - left

    sends = []
    for out, row, p_row in ((up, fine - 3, fine - 4), (down, 0, 0)):
        for r in range(3):
            left, on_left, on_right = entry(row + r)
            for k, slot, on in ((0, left, on_left), (2, 3 - left, on_right)):
                sends.append((a_tiles.at[row + r, slot], out.at[3 * r + k], on))
            sends.append((a_tiles.at[row + r, 0], out.at[3 * r + 1], None))
        for n in range(4):
            for m in range(KP):
                sends.append((p_tiles.at[p_row + n, m], out.at[9 + 2 * n + m], None))
    for k, (here, there, on) in enumerate(sends):
        if on is None:
            pltpu.make_async_copy(here, there, sem.at[3 + k]).start()
        else:

            @pl.when(on)
            def _():
                pltpu.make_async_copy(here, there, sem.at[3 + k]).start()

            @pl.when(jnp.logical_not(on))
            def _():
                there[...] = jnp.zeros(there.shape, F32)

    def flag(k, carry):
        i = first + k - 4
        i = jnp.where(i < 0, i + fine_total, jnp.where(i >= fine_total, i - fine_total, i))
        at = begin + k
        plan[k] = jnp.where(near[at >> 7, at & (LANES - 1)] != lax.div(i, 3), 1, 0)
        return carry

    for load in index_loads:
        load.wait()
    lax.fori_loop(0, fine + 8, flag, 0, unroll=8)

    def group(g, carry):
        for mod in range(3):
            i = 3 * g + mod
            left, on_left, on_right = entry(i)
            plan[LEFT + i] = left
            plan[OUT_LEFT + i] = jnp.where(on_left & (i > 0), 1, 0)
            plan[OUT_RIGHT + i] = jnp.where(on_right & (i < fine - 1), 1, 0)
        return carry

    lax.fori_loop(0, coarse, group, 0, unroll=4)
    for k in range(4):
        used[k] = 0

    def slot(c, carry):
        mine = mine_ref[0, (own + c) & (LANES - 1)]
        shift = ((mine >> 5) - (place[0] >> 5)) & 3
        plan[SLOTS_AT[0] + c] = shift * (coarse // 4) + used[shift]
        plan[SLOTS_AT[1] + c] = mine & 31
        used[shift] = used[shift] + 1
        return carry

    lax.fori_loop(0, coarse, slot, 0)
    for k, (here, there, on) in enumerate(sends):
        if on is None:
            pltpu.make_async_copy(here, there, sem.at[3 + k]).wait()
        else:

            @pl.when(on)
            def _():
                pltpu.make_async_copy(here, there, sem.at[3 + k]).wait()


def make_plan(place, a_cols, a_len, aggregate, owner, a_tiles, p_tiles):
    fine = a_len.shape[0]
    owners = owner.reshape(-1, LANES)

    def whole(shape):
        return pl.BlockSpec(shape, lambda *_: (0,) * len(shape))

    halo = (9 + 4 * KP, B, B)
    return pl.pallas_call(
        plan_kernel,
        grid_spec=pltpu.PrefetchScalarGridSpec(
            num_scalar_prefetch=3,
            grid=(1,),
            in_specs=[ANYWHERE] * 4,
            out_specs=[
                pl.BlockSpec(memory_space=SMEM),
                whole(halo),
                whole(halo),
            ],
            scratch_shapes=[
                SMEM((2, LANES), jnp.int32),
                SMEM((1, LANES), jnp.int32),
                SMEM((4,), jnp.int32),
                pltpu.SemaphoreType.DMA((3 + 2 * halo[0],)),
            ],
        ),
        out_shape=[
            jax.ShapeDtypeStruct((PLAN,), jnp.int32),
            jax.ShapeDtypeStruct(halo, F32),
            jax.ShapeDtypeStruct(halo, F32),
        ],
        compiler_params=pltpu.CompilerParams(vmem_limit_bytes=60 << 20),
        cost_estimate=pl.CostEstimate(flops=0, bytes_accessed=5_000_000, transcendentals=0),
        name="plan",
    )(place, a_cols.T, a_len, a_tiles, p_tiles, aggregate.reshape(-1, LANES), owners)


def relay(pairs, sems_in, sems_out):
    inward = [pltpu.make_async_copy(x, y, sems_in.at[k]) for k, (x, y, z) in enumerate(pairs)]
    outward = [pltpu.make_async_copy(y, z, sems_out.at[k]) for k, (x, y, z) in enumerate(pairs)]
    for copy in inward:
        copy.start()
    for come, go in zip(inward, outward):
        come.wait()
        go.start()
    for copy in outward:
        copy.wait()


def move_kernel(source_ref, target_ref, rows_in, rows_out, stage, sems_in, sems_out):
    relay(
        [(rows_in.at[source_ref[k]], stage.at[k], rows_out.at[target_ref[k]]) for k in range(stage.shape[0])],
        sems_in,
        sems_out,
    )


def move_rows(source, target, rows, places):
    count = source.shape[0]
    return pl.pallas_call(
        move_kernel,
        grid_spec=pltpu.PrefetchScalarGridSpec(
            num_scalar_prefetch=2,
            grid=(1,),
            in_specs=[ANYWHERE],
            out_specs=ANYWHERE,
            scratch_shapes=[
                VMEM((count,) + rows.shape[1:], F32),
                pltpu.SemaphoreType.DMA((count,)),
                pltpu.SemaphoreType.DMA((count,)),
            ],
        ),
        out_shape=jax.ShapeDtypeStruct((places,) + rows.shape[1:], F32),
        compiler_params=pltpu.CompilerParams(vmem_limit_bytes=56 << 20),
        cost_estimate=pl.CostEstimate(flops=0, bytes_accessed=8_000_000, transcendentals=0),
        name="move_rows",
    )(source, target, rows)


def put_kernel(half, source, rows, *refs):
    out, stage, sems_in, sems_out = refs[-4:]
    part = pl.ds(half * HALF, HALF)
    relay(
        [(rows.at[source[k]], stage.at[k], out.at[k, :, part]) for k in range(stage.shape[0])], sems_in, sems_out
    )


def put_rows(half, source, rows, whole=None):
    count = source.shape[0]
    held = [] if whole is None else [whole]
    return pl.pallas_call(
        functools.partial(put_kernel, half),
        grid_spec=pltpu.PrefetchScalarGridSpec(
            num_scalar_prefetch=1,
            grid=(1,),
            in_specs=[ANYWHERE] * (1 + len(held)),
            out_specs=ANYWHERE,
            scratch_shapes=[
                VMEM((count,) + rows.shape[1:], F32),
                pltpu.SemaphoreType.DMA((count,)),
                pltpu.SemaphoreType.DMA((count,)),
            ],
        ),
        out_shape=jax.ShapeDtypeStruct((count, CWIN, B, B), F32),
        input_output_aliases={2: 0} if held else {},
        compiler_params=pltpu.CompilerParams(vmem_limit_bytes=60 << 20),
        cost_estimate=pl.CostEstimate(flops=0, bytes_accessed=8_000_000, transcendentals=0),
        name="put_rows",
    )(source, rows, *held)


AXES = ("gx", "gy")


def shards(a_tiles, a_cols, a_len, p_tiles, aggregate, owner):
    count_x, count_y = lax.axis_size("gx"), lax.axis_size("gy")
    index_x, index_y = lax.axis_index("gx"), lax.axis_index("gy")
    size = count_x * count_y
    device = index_x * count_y + index_y
    coarse = a_tiles.shape[0] // 3
    depth = coarse // count_x
    place = jnp.reshape(device, (1,)).astype(jnp.int32)
    plan, up, down = make_plan(place, a_cols, a_len, aggregate, owner, a_tiles, p_tiles)
    above = [(i, (i + 1) % size) for i in range(size)]
    below = [(j, i) for i, j in above]
    before = lax.ppermute(up, AXES, above)
    behind = lax.ppermute(down, AXES, below)

    def half_rows(half, places, after):
        rows = main_product(half, plan, a_tiles, p_tiles, places, after)
        return edge_product(half, plan, before, behind, up, down, p_tiles, rows)

    rows_b = half_rows(1, count_y, plan)
    rows_a = half_rows(0, coarse, rows_b)

    table = owner.reshape(count_x, count_y, coarse)
    order = jnp.arange(coarse)
    shift = table[0, 0] // count_y
    same = shift[None, :] == shift[:, None]
    rank = jnp.sum((same & (order[None, :] < order[:, None])).astype(jnp.int32), axis=1)
    slot = (shift * depth + rank).astype(jnp.int32)
    from_x = (index_x - shift) % count_x
    column = table[:, index_y] % count_y
    mid_a_target = jnp.sum(
        jnp.where(jnp.arange(count_x)[:, None] == from_x[None, :], column, 0), axis=0
    ).astype(jnp.int32)
    hit = (table[index_x] % count_y) == index_y
    mid_b_source = jnp.sum(jnp.where(hit, jnp.arange(count_y)[:, None], 0), axis=0).astype(jnp.int32)
    found = table.reshape(size, coarse) == device
    sender = jnp.sum(jnp.where(found, jnp.arange(size)[:, None], 0), axis=0)
    ids = sender * coarse + order
    spot = jnp.sum((ids[None, :] < ids[:, None]).astype(jnp.int32), axis=1)
    at = spot[None, :] == order[:, None]
    last_a = jnp.sum(jnp.where(at, (sender % count_y)[None, :], 0), axis=1).astype(jnp.int32)
    last_b = jnp.sum(jnp.where(at, slot[None, :], 0), axis=1).astype(jnp.int32)

    def over_y(x):
        return lax.all_to_all(x, "gy", split_axis=0, concat_axis=0, tiled=True)

    def along_x(x):
        parts = [x[:depth]]
        for k in range(1, count_x):
            pairs = [(i, (i + k) % count_x) for i in range(count_x)]
            parts.append(lax.ppermute(x[k * depth : (k + 1) * depth], "gx", pairs))
        return jnp.concatenate(parts, axis=0)

    got_b = over_y(rows_b)
    got_a = along_x(rows_a)
    end_a = over_y(move_rows(slot, mid_a_target, got_a, count_y))
    end_b = along_x(move_rows(mid_b_source, slot, got_b, coarse))
    return put_rows(0, last_a, end_a, put_rows(1, last_b, end_b))


def solution(mesh):
    in_specs = (
        P(("gx", "gy"), None, None, None),
        P(("gx", "gy"), None),
        P(("gx", "gy")),
        P(("gx", "gy"), None, None, None),
        P(),
        P(),
    )
    out_specs = P(("gx", "gy"), None, None, None)
    return jax.shard_map(shards, mesh=mesh, in_specs=in_specs, out_specs=out_specs, check_vma=False)
```

```python
import functools

import jax
import jax.numpy as jnp
from jax import lax
from jax.experimental import pallas as pl
from jax.experimental.pallas import tpu as pltpu
from jax.sharding import PartitionSpec as P

B = 128
KP = 2
LANES = 128
CWIN = 7
CB = 16
W = 12
G = W // 3
BF = jnp.bfloat16
F32 = jnp.float32
SMEM = pltpu.SMEM
ANYWHERE = pl.BlockSpec(memory_space=pl.ANY)
VMEM = pltpu.VMEM


LEFT, OUT_LEFT, OUT_RIGHT, SLOTS_AT, PLAN = 64, 128, 192, (256, 272), 384
HALF = B // 2


def split(x):
    high = x.astype(BF)
    return high, (x - high.astype(F32)).astype(BF)


def left_operand(x):
    high, low = split(x)
    return jnp.concatenate([high, low, high], axis=1)


def right_operand(x):
    high, low = split(x)
    return jnp.concatenate([high, high, low], axis=0)


def matmul(left, right):
    return jnp.dot(left, right, preferred_element_type=F32)


def spread(total, flag, base, pair, slots):
    first, second = pair
    values = {
        base - 1: jnp.where(flag, first, 0.0),
        base: jnp.where(flag, second, first),
        base + 1: jnp.where(flag, 0.0, second),
    }
    for s, value in values.items():
        if s in slots:
            total[s] = value if total.get(s) is None else total[s] + value


def turn(p_tile, half):
    return p_tile.T[half * HALF : (half + 1) * HALF]


def row_product(p_pair, tiles, half):
    turned = jnp.concatenate([turn(p_pair[0], half), turn(p_pair[1], half)], axis=0)
    return matmul(left_operand(turned), right_operand(jnp.concatenate(tiles, axis=1)))


SLOTS = {0: (0, 1, 2, 3), 1: (1, 2, 3), 2: (1, 2, 3, 4)}


def main_kernel(
    half, plan,
    a_ref, p_ref, before_ref, after_ref, behind_ref,
    out,
    stage, carry, sems,
):
    step = pl.program_id(0)
    steps = pl.num_programs(0) - 1
    buf = lax.rem(step, 2)

    def copy_out(at, which, row):
        c = G * at - 1 + row
        return pltpu.make_async_copy(stage.at[which, row], out.at[plan[SLOTS_AT[half] + c]], sems.at[which, row])

    def drain(at):
        which = lax.rem(at, 2)
        for row in range(G):
            @pl.when((G * at - 1 + row >= 0) & (G * at - 1 + row < G * steps))
            def _():
                copy_out(at, which, row).wait()

    @pl.when(step >= 2)
    def _():
        drain(step - 2)

    @pl.when(step == 0)
    def _():
        carry[...] = jnp.zeros_like(carry)

    @pl.when(step == steps)
    def _():
        stage[buf, 0] = carry[0]

    @pl.when(step < steps)
    def _():
        sums = {(place, w): carry[place, w] for place in range(2) for w in range(CWIN)}
        first = step * W
        flags = {q: plan[first + q + 4] > 0 for q in range(-1, W + 1)}

        def p_tile(q, m):
            if q < 0:
                return before_ref[0, m]
            if q >= W:
                return after_ref[0, m]
            return p_ref[q, m]

        lefts = {}
        for r in range(W):
            tiles = {
                0: jnp.where(plan[OUT_LEFT + first + r] > 0, a_ref[r, plan[LEFT + first + r]], 0.0),
                1: a_ref[r, 0],
                2: jnp.where(plan[OUT_RIGHT + first + r] > 0, a_ref[r, 3 - plan[LEFT + first + r]], 0.0),
            }
            for k in range(3):
                lefts[r, r + k - 1] = left_operand(tiles[k])
        total = {r: {} for r in range(W)}
        for q in range(-1, W + 1):
            rows = [r for r in (q - 1, q, q + 1) if 0 <= r < W]
            right = right_operand(jnp.concatenate([p_tile(q, 0), p_tile(q, 1)], axis=1))
            product = matmul(jnp.concatenate([lefts[r, q] for r in rows], axis=0), right)
            for n, r in enumerate(rows):
                pair = (product[n * B : (n + 1) * B, :B], product[n * B : (n + 1) * B, B:])
                spread(total[r], flags[q], q // 3 - r // 3 + 2, pair, SLOTS[r % 3])
        for r in range(W):
            slots = SLOTS[r % 3]
            product = row_product((p_ref[r, 0], p_ref[r, 1]), [total[r][s] for s in slots], half)
            g = r // 3
            for n, s in enumerate(slots):
                one = product[:HALF, n * B : (n + 1) * B]
                two = product[HALF:, n * B : (n + 1) * B]
                for delta, value in (
                    (-1, jnp.where(flags[r], one, 0.0)),
                    (0, jnp.where(flags[r], two, one)),
                    (1, jnp.where(flags[r], 0.0, two)),
                ):
                    key = (g + delta + 1, s + 1 - delta)
                    sums[key] = value if key not in sums else sums[key] + value
        for place in range(G + 2):
            for w in range(CWIN):
                value = sums.get((place, w))
                if value is None:
                    value = jnp.zeros((HALF, B), F32)
                if place < G:
                    stage[buf, place, w] = value
                else:
                    carry[place - G, w] = value

    for row in range(G):
        @pl.when((G * step - 1 + row >= 0) & (G * step - 1 + row < G * steps))
        def _():
            copy_out(step, buf, row).start()

    @pl.when(step == steps)
    def _():
        drain(step - 1)
        drain(step)


def main_product(half, plan, a_tiles, p_tiles, places, behind):
    rows = a_tiles.shape[0]
    steps = rows // W
    last = steps - 1

    def spec(shape, index):
        return pl.BlockSpec(shape, index)

    return pl.pallas_call(
        functools.partial(main_kernel, half),
        grid_spec=pltpu.PrefetchScalarGridSpec(
            num_scalar_prefetch=1,
            grid=(steps + 1,),
            in_specs=[
                spec((W, 3, B, B), lambda s, *_: (jnp.minimum(s, last), 0, 0, 0)),
                spec((W, KP, B, B), lambda s, *_: (jnp.minimum(s, last), 0, 0, 0)),
                spec((1, KP, B, B), lambda s, *_: (jnp.maximum(jnp.minimum(s, last) * W - 1, 0), 0, 0, 0)),
                spec((1, KP, B, B), lambda s, *_: (jnp.minimum(s * W + W, rows - 1), 0, 0, 0)),
                ANYWHERE,
            ],
            out_specs=ANYWHERE,
            scratch_shapes=[
                VMEM((2, G, CWIN, HALF, B), F32),
                VMEM((2, CWIN, HALF, B), F32),
                pltpu.SemaphoreType.DMA((2, G)),
            ],
        ),
        out_shape=jax.ShapeDtypeStruct((places, CWIN, HALF, B), F32),
        compiler_params=pltpu.CompilerParams(
            dimension_semantics=("arbitrary",), vmem_limit_bytes=56 << 20
        ),
        cost_estimate=pl.CostEstimate(
            flops=12_000_000_000, bytes_accessed=20_000_000, transcendentals=0
        ),
        name="triple_product",
    )(plan, a_tiles, p_tiles, p_tiles, p_tiles, behind)


def edge_kernel(
    half, plan,
    before, after, a_first, a_last, p_first, p_last, in_rows,
    out_rows,
    rows_ref, sems,
):
    coarse = CB
    held = (0, 1, coarse - 2, coarse - 1)

    def copy(n, back):
        there, here = out_rows.at[plan[SLOTS_AT[half] + held[n]]], rows_ref.at[n]
        if back:
            return pltpu.make_async_copy(there, here, sems.at[n])
        return pltpu.make_async_copy(here, there, sems.at[n])

    for n in range(4):
        copy(n, True).start()

    sums = []
    for side in range(2):
        halo = (before, after)[side]
        a_edge = (a_first, a_last)[side]
        own_p = (p_first, p_last)[side]
        own_flag = plan[(4, 3 * coarse + 3)[side]] > 0
        flags, tiles, p_at = {}, {}, {}
        for n in range(4):
            q = n - 1 if side == 0 else n
            flags[q] = plan[(0, 3 * coarse + 4)[side] + n] > 0
            p_at[q] = (halo[9 + 2 * n], halo[10 + 2 * n])
        near = 3 if side == 0 else -1
        flags[near] = own_flag
        p_at[near] = (own_p[0, 0], own_p[0, 1])
        total = {r: {} for r in range(3)}
        total[near] = {}
        for q in range(-1, 4):
            rows = [r for r in (q - 1, q, q + 1) if 0 <= r < 3]
            lefts = [left_operand(halo[3 * r + q - r + 1]) for r in rows]
            if q == (2 if side == 0 else 0):
                rows.append(near)
                lefts.append(left_operand(a_edge[0]))
            right = right_operand(jnp.concatenate(p_at[q], axis=1))
            product = matmul(jnp.concatenate(lefts, axis=0), right)
            for n, r in enumerate(rows):
                pair = (product[n * B : (n + 1) * B, :B], product[n * B : (n + 1) * B, B:])
                base = q // 3 - r // 3 + 2
                slots = SLOTS[r % 3] if r != near else (base - 1, base, base + 1)
                spread(total[r], flags[q], base, pair, slots)
        outer, inner = {}, {}

        def put(target, w, value):
            target[w] = value if w not in target else target[w] + value

        for r in range(3):
            slots = sorted(total[r])
            pick = 1 if side == 0 else 0
            turned = left_operand(turn(p_at[r][pick], half))
            product = matmul(turned, right_operand(jnp.concatenate([total[r][s] for s in slots], axis=1)))
            for n, s in enumerate(slots):
                value = product[:, n * B : (n + 1) * B]
                if side == 0:
                    put(outer, s, jnp.where(flags[r], 0.0, value))
                else:
                    put(outer, s + 2, jnp.where(flags[r], value, 0.0))
        slots = sorted(total[near])
        product = row_product(p_at[near], [total[near][s] for s in slots], half)
        for n, s in enumerate(slots):
            one = product[:HALF, n * B : (n + 1) * B]
            two = product[HALF:, n * B : (n + 1) * B]
            put(outer, s + 1, jnp.where(own_flag, two, one))
            if side == 0:
                put(inner, s, jnp.where(own_flag, 0.0, two))
            else:
                put(inner, s + 2, jnp.where(own_flag, one, 0.0))
        sums.append((outer, inner))

    for n in range(4):
        copy(n, True).wait()
    for n, target in ((0, sums[0][0]), (1, sums[0][1]), (2, sums[1][1]), (3, sums[1][0])):
        for w, value in target.items():
            rows_ref[n, w] += value
    for n in range(4):
        copy(n, False).start()
    for n in range(4):
        copy(n, False).wait()


def edge_product(half, plan, before, after, up, down, p_tiles, out_rows):
    rows = p_tiles.shape[0]

    def whole(x):
        return pl.BlockSpec(x.shape, lambda *_: (0,) * x.ndim)

    return pl.pallas_call(
        functools.partial(edge_kernel, half),
        grid_spec=pltpu.PrefetchScalarGridSpec(
            num_scalar_prefetch=1,
            grid=(1,),
            in_specs=[whole(before), whole(after)]
            + [
                pl.BlockSpec((1, B, B), lambda *_: (0, 0, 0)),
                pl.BlockSpec((1, B, B), lambda *_: (8, 0, 0)),
                pl.BlockSpec((1, KP, B, B), lambda *_: (0, 0, 0, 0)),
                pl.BlockSpec((1, KP, B, B), lambda *_: (rows - 1, 0, 0, 0)),
            ]
            + [ANYWHERE],
            out_specs=ANYWHERE,
            scratch_shapes=[VMEM((4, CWIN, HALF, B), F32), pltpu.SemaphoreType.DMA((4,))],
        ),
        out_shape=jax.ShapeDtypeStruct(out_rows.shape, F32),
        input_output_aliases={7: 0},
        compiler_params=pltpu.CompilerParams(
            dimension_semantics=("arbitrary",), vmem_limit_bytes=60 << 20
        ),
        cost_estimate=pl.CostEstimate(flops=2_000_000_000, bytes_accessed=10_000_000, transcendentals=0),
        name="edge_rows",
    )(plan, before, after, down, up, p_tiles, p_tiles, out_rows)


def plan_kernel(place, cols, length, a_tiles, p_tiles, aggregate, owners, plan, up, down, near, mine_ref, used, sem):
    fine = length.shape[0]
    coarse = fine // 3
    wide = aggregate.shape[0]
    fine_total = wide * LANES
    first = place[0] * fine
    line = jnp.where(first < 4, wide - 1, (first - 4) >> 7)
    begin = jnp.where(first < 4, LANES - 4, (first - 4) & (LANES - 1))
    lines = (line, jnp.where(line == wide - 1, 0, line + 1))
    index_loads = [
        pltpu.make_async_copy(aggregate.at[pl.ds(at, 1)], near.at[pl.ds(n, 1)], sem.at[n]) for n, at in enumerate(lines)
    ]
    own = place[0] * coarse
    index_loads.append(pltpu.make_async_copy(owners.at[pl.ds(own >> 7, 1)], mine_ref, sem.at[2]))
    for load in index_loads:
        load.start()

    def entry(i):
        before = first + i - 1
        before = jnp.where(before < 0, fine_total - 1, before)
        left = jnp.where(cols[1, i] == before, 1, 2)
        return left, length[i] > left, length[i] > 3 - left

    sends = []
    for out, row, p_row in ((up, fine - 3, fine - 4), (down, 0, 0)):
        for r in range(3):
            left, on_left, on_right = entry(row + r)
            for k, slot, on in ((0, left, on_left), (2, 3 - left, on_right)):
                sends.append((a_tiles.at[row + r, slot], out.at[3 * r + k], on))
            sends.append((a_tiles.at[row + r, 0], out.at[3 * r + 1], None))
        for n in range(4):
            for m in range(KP):
                sends.append((p_tiles.at[p_row + n, m], out.at[9 + 2 * n + m], None))
    for k, (here, there, on) in enumerate(sends):
        if on is None:
            pltpu.make_async_copy(here, there, sem.at[3 + k]).start()
        else:

            @pl.when(on)
            def _():
                pltpu.make_async_copy(here, there, sem.at[3 + k]).start()

            @pl.when(jnp.logical_not(on))
            def _():
                there[...] = jnp.zeros(there.shape, F32)

    def flag(k, carry):
        i = first + k - 4
        i = jnp.where(i < 0, i + fine_total, jnp.where(i >= fine_total, i - fine_total, i))
        at = begin + k
        plan[k] = jnp.where(near[at >> 7, at & (LANES - 1)] != lax.div(i, 3), 1, 0)
        return carry

    for load in index_loads:
        load.wait()
    lax.fori_loop(0, fine + 8, flag, 0, unroll=8)

    def group(g, carry):
        for mod in range(3):
            i = 3 * g + mod
            left, on_left, on_right = entry(i)
            plan[LEFT + i] = left
            plan[OUT_LEFT + i] = jnp.where(on_left & (i > 0), 1, 0)
            plan[OUT_RIGHT + i] = jnp.where(on_right & (i < fine - 1), 1, 0)
        return carry

    lax.fori_loop(0, coarse, group, 0, unroll=4)
    for k in range(4):
        used[k] = 0

    def slot(c, carry):
        mine = mine_ref[0, (own + c) & (LANES - 1)]
        shift = ((mine >> 5) - (place[0] >> 5)) & 3
        plan[SLOTS_AT[0] + c] = shift * (coarse // 4) + used[shift]
        plan[SLOTS_AT[1] + c] = mine & 31
        used[shift] = used[shift] + 1
        return carry

    lax.fori_loop(0, coarse, slot, 0, unroll=4)
    for k, (here, there, on) in enumerate(sends):
        if on is None:
            pltpu.make_async_copy(here, there, sem.at[3 + k]).wait()
        else:

            @pl.when(on)
            def _():
                pltpu.make_async_copy(here, there, sem.at[3 + k]).wait()


def make_plan(place, a_cols, a_len, aggregate, owner, a_tiles, p_tiles):
    fine = a_len.shape[0]
    owners = owner.reshape(-1, LANES)

    def whole(shape):
        return pl.BlockSpec(shape, lambda *_: (0,) * len(shape))

    halo = (9 + 4 * KP, B, B)
    return pl.pallas_call(
        plan_kernel,
        grid_spec=pltpu.PrefetchScalarGridSpec(
            num_scalar_prefetch=3,
            grid=(1,),
            in_specs=[ANYWHERE] * 4,
            out_specs=[
                pl.BlockSpec(memory_space=SMEM),
                whole(halo),
                whole(halo),
            ],
            scratch_shapes=[
                SMEM((2, LANES), jnp.int32),
                SMEM((1, LANES), jnp.int32),
                SMEM((4,), jnp.int32),
                pltpu.SemaphoreType.DMA((3 + 2 * halo[0],)),
            ],
        ),
        out_shape=[
            jax.ShapeDtypeStruct((PLAN,), jnp.int32),
            jax.ShapeDtypeStruct(halo, F32),
            jax.ShapeDtypeStruct(halo, F32),
        ],
        compiler_params=pltpu.CompilerParams(vmem_limit_bytes=60 << 20),
        cost_estimate=pl.CostEstimate(flops=0, bytes_accessed=5_000_000, transcendentals=0),
        name="plan",
    )(place, a_cols.T, a_len, a_tiles, p_tiles, aggregate.reshape(-1, LANES), owners)


def relay(pairs, sems_in, sems_out):
    inward = [pltpu.make_async_copy(x, y, sems_in.at[k]) for k, (x, y, z) in enumerate(pairs)]
    outward = [pltpu.make_async_copy(y, z, sems_out.at[k]) for k, (x, y, z) in enumerate(pairs)]
    for copy in inward:
        copy.start()
    for come, go in zip(inward, outward):
        come.wait()
        go.start()
    for copy in outward:
        copy.wait()


def move_kernel(source_ref, target_ref, rows_in, rows_out, stage, sems_in, sems_out):
    relay(
        [(rows_in.at[source_ref[k]], stage.at[k], rows_out.at[target_ref[k]]) for k in range(stage.shape[0])],
        sems_in,
        sems_out,
    )


def move_rows(source, target, rows, places):
    count = source.shape[0]
    return pl.pallas_call(
        move_kernel,
        grid_spec=pltpu.PrefetchScalarGridSpec(
            num_scalar_prefetch=2,
            grid=(1,),
            in_specs=[ANYWHERE],
            out_specs=ANYWHERE,
            scratch_shapes=[
                VMEM((count,) + rows.shape[1:], F32),
                pltpu.SemaphoreType.DMA((count,)),
                pltpu.SemaphoreType.DMA((count,)),
            ],
        ),
        out_shape=jax.ShapeDtypeStruct((places,) + rows.shape[1:], F32),
        compiler_params=pltpu.CompilerParams(vmem_limit_bytes=56 << 20),
        cost_estimate=pl.CostEstimate(flops=0, bytes_accessed=8_000_000, transcendentals=0),
        name="move_rows",
    )(source, target, rows)


def put_kernel(half, source, rows, *refs):
    out, stage, sems_in, sems_out = refs[-4:]
    part = pl.ds(half * HALF, HALF)
    relay(
        [(rows.at[source[k]], stage.at[k], out.at[k, :, part]) for k in range(stage.shape[0])], sems_in, sems_out
    )


def put_rows(half, source, rows, whole=None):
    count = source.shape[0]
    held = [] if whole is None else [whole]
    return pl.pallas_call(
        functools.partial(put_kernel, half),
        grid_spec=pltpu.PrefetchScalarGridSpec(
            num_scalar_prefetch=1,
            grid=(1,),
            in_specs=[ANYWHERE] * (1 + len(held)),
            out_specs=ANYWHERE,
            scratch_shapes=[
                VMEM((count,) + rows.shape[1:], F32),
                pltpu.SemaphoreType.DMA((count,)),
                pltpu.SemaphoreType.DMA((count,)),
            ],
        ),
        out_shape=jax.ShapeDtypeStruct((count, CWIN, B, B), F32),
        input_output_aliases={2: 0} if held else {},
        compiler_params=pltpu.CompilerParams(vmem_limit_bytes=60 << 20),
        cost_estimate=pl.CostEstimate(flops=0, bytes_accessed=8_000_000, transcendentals=0),
        name="put_rows",
    )(source, rows, *held)


AXES = ("gx", "gy")


def shards(a_tiles, a_cols, a_len, p_tiles, aggregate, owner):
    count_x, count_y = lax.axis_size("gx"), lax.axis_size("gy")
    index_x, index_y = lax.axis_index("gx"), lax.axis_index("gy")
    size = count_x * count_y
    device = index_x * count_y + index_y
    coarse = a_tiles.shape[0] // 3
    depth = coarse // count_x
    place = jnp.reshape(device, (1,)).astype(jnp.int32)
    plan, up, down = make_plan(place, a_cols, a_len, aggregate, owner, a_tiles, p_tiles)
    above = [(i, (i + 1) % size) for i in range(size)]
    below = [(j, i) for i, j in above]
    before = lax.ppermute(up, AXES, above)
    behind = lax.ppermute(down, AXES, below)

    def half_rows(half, places, after):
        rows = main_product(half, plan, a_tiles, p_tiles, places, after)
        return edge_product(half, plan, before, behind, up, down, p_tiles, rows)

    rows_b = half_rows(1, count_y, plan)
    rows_a = half_rows(0, coarse, rows_b)

    table = owner.reshape(count_x, count_y, coarse)
    order = jnp.arange(coarse)
    shift = table[0, 0] // count_y
    same = shift[None, :] == shift[:, None]
    rank = jnp.sum((same & (order[None, :] < order[:, None])).astype(jnp.int32), axis=1)
    slot = (shift * depth + rank).astype(jnp.int32)
    from_x = (index_x - shift) % count_x
    column = table[:, index_y] % count_y
    mid_a_target = jnp.sum(
        jnp.where(jnp.arange(count_x)[:, None] == from_x[None, :], column, 0), axis=0
    ).astype(jnp.int32)
    hit = (table[index_x] % count_y) == index_y
    mid_b_source = jnp.sum(jnp.where(hit, jnp.arange(count_y)[:, None], 0), axis=0).astype(jnp.int32)
    found = table.reshape(size, coarse) == device
    sender = jnp.sum(jnp.where(found, jnp.arange(size)[:, None], 0), axis=0)
    ids = sender * coarse + order
    spot = jnp.sum((ids[None, :] < ids[:, None]).astype(jnp.int32), axis=1)
    at = spot[None, :] == order[:, None]
    last_a = jnp.sum(jnp.where(at, (sender % count_y)[None, :], 0), axis=1).astype(jnp.int32)
    last_b = jnp.sum(jnp.where(at, slot[None, :], 0), axis=1).astype(jnp.int32)

    def over_y(x):
        return lax.all_to_all(x, "gy", split_axis=0, concat_axis=0, tiled=True)

    def along_x(x):
        parts = [x[:depth]]
        for k in range(1, count_x):
            pairs = [(i, (i + k) % count_x) for i in range(count_x)]
            parts.append(lax.ppermute(x[k * depth : (k + 1) * depth], "gx", pairs))
        return jnp.concatenate(parts, axis=0)

    got_b = over_y(rows_b)
    got_a = along_x(rows_a)
    end_a = over_y(move_rows(slot, mid_a_target, got_a, count_y))
    end_b = along_x(move_rows(mid_b_source, slot, got_b, coarse))
    return put_rows(0, last_a, end_a, put_rows(1, last_b, end_b))


def solution(mesh):
    in_specs = (
        P(("gx", "gy"), None, None, None),
        P(("gx", "gy"), None),
        P(("gx", "gy")),
        P(("gx", "gy"), None, None, None),
        P(),
        P(),
    )
    out_specs = P(("gx", "gy"), None, None, None)
    return jax.shard_map(shards, mesh=mesh, in_specs=in_specs, out_specs=out_specs, check_vma=False)
```

```python
import functools

import jax
import jax.numpy as jnp
from jax import lax
from jax.experimental import pallas as pl
from jax.experimental.pallas import tpu as pltpu
from jax.sharding import PartitionSpec as P

B = 128
KP = 2
LANES = 128
CWIN = 7
CB = 16
W = 12
G = W // 3
BF = jnp.bfloat16
F32 = jnp.float32
SMEM = pltpu.SMEM
ANYWHERE = pl.BlockSpec(memory_space=pl.ANY)
VMEM = pltpu.VMEM


LEFT, OUT_LEFT, OUT_RIGHT, SLOTS_AT, PLAN = 64, 128, 192, (256, 272), 384
HALF = B // 2


def split(x):
    high = x.astype(BF)
    return high, (x - high.astype(F32)).astype(BF)


def left_operand(x):
    high, low = split(x)
    return jnp.concatenate([high, low, high], axis=1)


def right_operand(x):
    high, low = split(x)
    return jnp.concatenate([high, high, low], axis=0)


def matmul(left, right):
    return jnp.dot(left, right, preferred_element_type=F32)


def spread(total, flag, base, pair, slots):
    first, second = pair
    values = {
        base - 1: jnp.where(flag, first, 0.0),
        base: jnp.where(flag, second, first),
        base + 1: jnp.where(flag, 0.0, second),
    }
    for s, value in values.items():
        if s in slots:
            total[s] = value if total.get(s) is None else total[s] + value


def turn(p_tile, half):
    return p_tile.T[half * HALF : (half + 1) * HALF]


def row_product(p_pair, tiles, half):
    turned = jnp.concatenate([turn(p_pair[0], half), turn(p_pair[1], half)], axis=0)
    return matmul(left_operand(turned), right_operand(jnp.concatenate(tiles, axis=1)))


SLOTS = {0: (0, 1, 2, 3), 1: (1, 2, 3), 2: (1, 2, 3, 4)}


def staggered(items, produce, consume):
    held = None
    for item in items:
        made = produce(item)
        if held is not None:
            consume(*held)
        held = item, made
    consume(*held)


def main_kernel(
    half, plan,
    a_ref, p_ref, before_ref, after_ref, behind_ref,
    out,
    stage, carry, sems,
):
    step = pl.program_id(0)
    steps = pl.num_programs(0) - 1
    buf = lax.rem(step, 2)

    def copy_out(at, which, row):
        c = G * at - 1 + row
        return pltpu.make_async_copy(stage.at[which, row], out.at[plan[SLOTS_AT[half] + c]], sems.at[which, row])

    def drain(at):
        which = lax.rem(at, 2)
        for row in range(G):
            @pl.when((G * at - 1 + row >= 0) & (G * at - 1 + row < G * steps))
            def _():
                copy_out(at, which, row).wait()

    @pl.when(step >= 2)
    def _():
        drain(step - 2)

    @pl.when(step == 0)
    def _():
        carry[...] = jnp.zeros_like(carry)

    @pl.when(step == steps)
    def _():
        stage[buf, 0] = carry[0]

    @pl.when(step < steps)
    def _():
        sums = {(place, w): carry[place, w] for place in range(2) for w in range(CWIN)}
        first = step * W
        flags = {q: plan[first + q + 4] > 0 for q in range(-1, W + 1)}

        def p_tile(q, m):
            if q < 0:
                return before_ref[0, m]
            if q >= W:
                return after_ref[0, m]
            return p_ref[q, m]

        lefts = {}
        for r in range(W):
            tiles = {
                0: jnp.where(plan[OUT_LEFT + first + r] > 0, a_ref[r, plan[LEFT + first + r]], 0.0),
                1: a_ref[r, 0],
                2: jnp.where(plan[OUT_RIGHT + first + r] > 0, a_ref[r, 3 - plan[LEFT + first + r]], 0.0),
            }
            for k in range(3):
                lefts[r, r + k - 1] = left_operand(tiles[k])
        total = {r: {} for r in range(W)}

        def rows_of(q):
            return [r for r in (q - 1, q, q + 1) if 0 <= r < W]

        def column(q):
            right = right_operand(jnp.concatenate([p_tile(q, 0), p_tile(q, 1)], axis=1))
            return matmul(jnp.concatenate([lefts[r, q] for r in rows_of(q)], axis=0), right)

        def add_column(q, product):
            for n, r in enumerate(rows_of(q)):
                pair = (product[n * B : (n + 1) * B, :B], product[n * B : (n + 1) * B, B:])
                spread(total[r], flags[q], q // 3 - r // 3 + 2, pair, SLOTS[r % 3])

        staggered(range(-1, W + 1), column, add_column)

        def row(r):
            return row_product((p_ref[r, 0], p_ref[r, 1]), [total[r][s] for s in SLOTS[r % 3]], half)

        def add_row(r, product):
            for n, s in enumerate(SLOTS[r % 3]):
                one = product[:HALF, n * B : (n + 1) * B]
                two = product[HALF:, n * B : (n + 1) * B]
                for delta, value in (
                    (-1, jnp.where(flags[r], one, 0.0)),
                    (0, jnp.where(flags[r], two, one)),
                    (1, jnp.where(flags[r], 0.0, two)),
                ):
                    key = (r // 3 + delta + 1, s + 1 - delta)
                    sums[key] = value if key not in sums else sums[key] + value

        staggered(range(W), row, add_row)
        for place in range(G + 2):
            for w in range(CWIN):
                value = sums.get((place, w))
                if value is None:
                    value = jnp.zeros((HALF, B), F32)
                if place < G:
                    stage[buf, place, w] = value
                else:
                    carry[place - G, w] = value

    for row in range(G):
        @pl.when((G * step - 1 + row >= 0) & (G * step - 1 + row < G * steps))
        def _():
            copy_out(step, buf, row).start()

    @pl.when(step == steps)
    def _():
        drain(step - 1)
        drain(step)


def main_product(half, plan, a_tiles, p_tiles, places, behind):
    rows = a_tiles.shape[0]
    steps = rows // W
    last = steps - 1

    def spec(shape, index):
        return pl.BlockSpec(shape, index)

    return pl.pallas_call(
        functools.partial(main_kernel, half),
        grid_spec=pltpu.PrefetchScalarGridSpec(
            num_scalar_prefetch=1,
            grid=(steps + 1,),
            in_specs=[
                spec((W, 3, B, B), lambda s, *_: (jnp.minimum(s, last), 0, 0, 0)),
                spec((W, KP, B, B), lambda s, *_: (jnp.minimum(s, last), 0, 0, 0)),
                spec((1, KP, B, B), lambda s, *_: (jnp.maximum(jnp.minimum(s, last) * W - 1, 0), 0, 0, 0)),
                spec((1, KP, B, B), lambda s, *_: (jnp.minimum(s * W + W, rows - 1), 0, 0, 0)),
                ANYWHERE,
            ],
            out_specs=ANYWHERE,
            scratch_shapes=[
                VMEM((2, G, CWIN, HALF, B), F32),
                VMEM((2, CWIN, HALF, B), F32),
                pltpu.SemaphoreType.DMA((2, G)),
            ],
        ),
        out_shape=jax.ShapeDtypeStruct((places, CWIN, HALF, B), F32),
        compiler_params=pltpu.CompilerParams(
            dimension_semantics=("arbitrary",), vmem_limit_bytes=56 << 20
        ),
        cost_estimate=pl.CostEstimate(
            flops=12_000_000_000, bytes_accessed=20_000_000, transcendentals=0
        ),
        name="triple_product",
    )(plan, a_tiles, p_tiles, p_tiles, p_tiles, behind)


def edge_kernel(
    half, plan,
    before, after, a_first, a_last, p_first, p_last, in_rows,
    out_rows,
    rows_ref, sems,
):
    coarse = CB
    held = (0, 1, coarse - 2, coarse - 1)

    def copy(n, back):
        there, here = out_rows.at[plan[SLOTS_AT[half] + held[n]]], rows_ref.at[n]
        if back:
            return pltpu.make_async_copy(there, here, sems.at[n])
        return pltpu.make_async_copy(here, there, sems.at[n])

    for n in range(4):
        copy(n, True).start()

    sums, sides = [], []
    for side in range(2):
        halo = (before, after)[side]
        a_edge = (a_first, a_last)[side]
        own_p = (p_first, p_last)[side]
        own_flag = plan[(4, 3 * coarse + 3)[side]] > 0
        flags, tiles, p_at = {}, {}, {}
        for n in range(4):
            q = n - 1 if side == 0 else n
            flags[q] = plan[(0, 3 * coarse + 4)[side] + n] > 0
            p_at[q] = (halo[9 + 2 * n], halo[10 + 2 * n])
        near = 3 if side == 0 else -1
        flags[near] = own_flag
        p_at[near] = (own_p[0, 0], own_p[0, 1])
        total = {r: {} for r in range(3)}
        total[near] = {}
        for q in range(-1, 4):
            rows = [r for r in (q - 1, q, q + 1) if 0 <= r < 3]
            lefts = [left_operand(halo[3 * r + q - r + 1]) for r in rows]
            if q == (2 if side == 0 else 0):
                rows.append(near)
                lefts.append(left_operand(a_edge[0]))
            right = right_operand(jnp.concatenate(p_at[q], axis=1))
            product = matmul(jnp.concatenate(lefts, axis=0), right)
            for n, r in enumerate(rows):
                pair = (product[n * B : (n + 1) * B, :B], product[n * B : (n + 1) * B, B:])
                base = q // 3 - r // 3 + 2
                slots = SLOTS[r % 3] if r != near else (base - 1, base, base + 1)
                spread(total[r], flags[q], base, pair, slots)
        sides.append((total, flags, p_at, near, own_flag))
    for side, (total, flags, p_at, near, own_flag) in enumerate(sides):
        outer, inner = {}, {}

        def put(target, w, value):
            target[w] = value if w not in target else target[w] + value

        for r in range(3):
            slots = sorted(total[r])
            pick = 1 if side == 0 else 0
            turned = left_operand(turn(p_at[r][pick], half))
            product = matmul(turned, right_operand(jnp.concatenate([total[r][s] for s in slots], axis=1)))
            for n, s in enumerate(slots):
                value = product[:, n * B : (n + 1) * B]
                if side == 0:
                    put(outer, s, jnp.where(flags[r], 0.0, value))
                else:
                    put(outer, s + 2, jnp.where(flags[r], value, 0.0))
        slots = sorted(total[near])
        product = row_product(p_at[near], [total[near][s] for s in slots], half)
        for n, s in enumerate(slots):
            one = product[:HALF, n * B : (n + 1) * B]
            two = product[HALF:, n * B : (n + 1) * B]
            put(outer, s + 1, jnp.where(own_flag, two, one))
            if side == 0:
                put(inner, s, jnp.where(own_flag, 0.0, two))
            else:
                put(inner, s + 2, jnp.where(own_flag, one, 0.0))
        sums.append((outer, inner))

    for n in range(4):
        copy(n, True).wait()
    for n, target in ((0, sums[0][0]), (1, sums[0][1]), (2, sums[1][1]), (3, sums[1][0])):
        for w, value in target.items():
            rows_ref[n, w] += value
    for n in range(4):
        copy(n, False).start()
    for n in range(4):
        copy(n, False).wait()


def edge_product(half, plan, before, after, up, down, p_tiles, out_rows):
    rows = p_tiles.shape[0]

    def whole(x):
        return pl.BlockSpec(x.shape, lambda *_: (0,) * x.ndim)

    return pl.pallas_call(
        functools.partial(edge_kernel, half),
        grid_spec=pltpu.PrefetchScalarGridSpec(
            num_scalar_prefetch=1,
            grid=(1,),
            in_specs=[whole(before), whole(after)]
            + [
                pl.BlockSpec((1, B, B), lambda *_: (0, 0, 0)),
                pl.BlockSpec((1, B, B), lambda *_: (8, 0, 0)),
                pl.BlockSpec((1, KP, B, B), lambda *_: (0, 0, 0, 0)),
                pl.BlockSpec((1, KP, B, B), lambda *_: (rows - 1, 0, 0, 0)),
            ]
            + [ANYWHERE],
            out_specs=ANYWHERE,
            scratch_shapes=[VMEM((4, CWIN, HALF, B), F32), pltpu.SemaphoreType.DMA((4,))],
        ),
        out_shape=jax.ShapeDtypeStruct(out_rows.shape, F32),
        input_output_aliases={7: 0},
        compiler_params=pltpu.CompilerParams(
            dimension_semantics=("arbitrary",), vmem_limit_bytes=60 << 20
        ),
        cost_estimate=pl.CostEstimate(flops=2_000_000_000, bytes_accessed=10_000_000, transcendentals=0),
        name="edge_rows",
    )(plan, before, after, down, up, p_tiles, p_tiles, out_rows)


def plan_kernel(place, cols, length, a_tiles, p_tiles, aggregate, owners, plan, up, down, near, mine_ref, used, sem):
    fine = length.shape[0]
    coarse = fine // 3
    wide = aggregate.shape[0]
    fine_total = wide * LANES
    first = place[0] * fine
    line = jnp.where(first < 4, wide - 1, (first - 4) >> 7)
    begin = jnp.where(first < 4, LANES - 4, (first - 4) & (LANES - 1))
    lines = (line, jnp.where(line == wide - 1, 0, line + 1))
    index_loads = [
        pltpu.make_async_copy(aggregate.at[pl.ds(at, 1)], near.at[pl.ds(n, 1)], sem.at[n]) for n, at in enumerate(lines)
    ]
    own = place[0] * coarse
    index_loads.append(pltpu.make_async_copy(owners.at[pl.ds(own >> 7, 1)], mine_ref, sem.at[2]))
    for load in index_loads:
        load.start()

    def entry(i):
        before = first + i - 1
        before = jnp.where(before < 0, fine_total - 1, before)
        left = jnp.where(cols[1, i] == before, 1, 2)
        return left, length[i] > left, length[i] > 3 - left

    sends = []
    for out, row, p_row in ((up, fine - 3, fine - 4), (down, 0, 0)):
        for r in range(3):
            left, on_left, on_right = entry(row + r)
            for k, slot, on in ((0, left, on_left), (2, 3 - left, on_right)):
                sends.append((a_tiles.at[row + r, slot], out.at[3 * r + k], on))
            sends.append((a_tiles.at[row + r, 0], out.at[3 * r + 1], None))
        for n in range(4):
            for m in range(KP):
                sends.append((p_tiles.at[p_row + n, m], out.at[9 + 2 * n + m], None))
    for k, (here, there, on) in enumerate(sends):
        if on is None:
            pltpu.make_async_copy(here, there, sem.at[3 + k]).start()
        else:

            @pl.when(on)
            def _():
                pltpu.make_async_copy(here, there, sem.at[3 + k]).start()

            @pl.when(jnp.logical_not(on))
            def _():
                there[...] = jnp.zeros(there.shape, F32)

    def flag(k, carry):
        i = first + k - 4
        i = jnp.where(i < 0, i + fine_total, jnp.where(i >= fine_total, i - fine_total, i))
        at = begin + k
        plan[k] = jnp.where(near[at >> 7, at & (LANES - 1)] != lax.div(i, 3), 1, 0)
        return carry

    for load in index_loads:
        load.wait()
    lax.fori_loop(0, fine + 8, flag, 0, unroll=8)

    def group(g, carry):
        for mod in range(3):
            i = 3 * g + mod
            left, on_left, on_right = entry(i)
            plan[LEFT + i] = left
            plan[OUT_LEFT + i] = jnp.where(on_left & (i > 0), 1, 0)
            plan[OUT_RIGHT + i] = jnp.where(on_right & (i < fine - 1), 1, 0)
        return carry

    lax.fori_loop(0, coarse, group, 0, unroll=4)
    for k in range(4):
        used[k] = 0

    def slot(c, carry):
        mine = mine_ref[0, (own + c) & (LANES - 1)]
        shift = ((mine >> 5) - (place[0] >> 5)) & 3
        plan[SLOTS_AT[0] + c] = shift * (coarse // 4) + used[shift]
        plan[SLOTS_AT[1] + c] = mine & 31
        used[shift] = used[shift] + 1
        return carry

    lax.fori_loop(0, coarse, slot, 0, unroll=4)
    for k, (here, there, on) in enumerate(sends):
        if on is None:
            pltpu.make_async_copy(here, there, sem.at[3 + k]).wait()
        else:

            @pl.when(on)
            def _():
                pltpu.make_async_copy(here, there, sem.at[3 + k]).wait()


def make_plan(place, a_cols, a_len, aggregate, owner, a_tiles, p_tiles):
    fine = a_len.shape[0]
    owners = owner.reshape(-1, LANES)

    def whole(shape):
        return pl.BlockSpec(shape, lambda *_: (0,) * len(shape))

    halo = (9 + 4 * KP, B, B)
    return pl.pallas_call(
        plan_kernel,
        grid_spec=pltpu.PrefetchScalarGridSpec(
            num_scalar_prefetch=3,
            grid=(1,),
            in_specs=[ANYWHERE] * 4,
            out_specs=[
                pl.BlockSpec(memory_space=SMEM),
                whole(halo),
                whole(halo),
            ],
            scratch_shapes=[
                SMEM((2, LANES), jnp.int32),
                SMEM((1, LANES), jnp.int32),
                SMEM((4,), jnp.int32),
                pltpu.SemaphoreType.DMA((3 + 2 * halo[0],)),
            ],
        ),
        out_shape=[
            jax.ShapeDtypeStruct((PLAN,), jnp.int32),
            jax.ShapeDtypeStruct(halo, F32),
            jax.ShapeDtypeStruct(halo, F32),
        ],
        compiler_params=pltpu.CompilerParams(vmem_limit_bytes=60 << 20),
        cost_estimate=pl.CostEstimate(flops=0, bytes_accessed=5_000_000, transcendentals=0),
        name="plan",
    )(place, a_cols.T, a_len, a_tiles, p_tiles, aggregate.reshape(-1, LANES), owners)


def relay(pairs, sems_in, sems_out):
    inward = [pltpu.make_async_copy(x, y, sems_in.at[k]) for k, (x, y, z) in enumerate(pairs)]
    outward = [pltpu.make_async_copy(y, z, sems_out.at[k]) for k, (x, y, z) in enumerate(pairs)]
    for copy in inward:
        copy.start()
    for come, go in zip(inward, outward):
        come.wait()
        go.start()
    for copy in outward:
        copy.wait()


def move_kernel(source_ref, target_ref, rows_in, rows_out, stage, sems_in, sems_out):
    relay(
        [(rows_in.at[source_ref[k]], stage.at[k], rows_out.at[target_ref[k]]) for k in range(stage.shape[0])],
        sems_in,
        sems_out,
    )


def move_rows(source, target, rows, places):
    count = source.shape[0]
    return pl.pallas_call(
        move_kernel,
        grid_spec=pltpu.PrefetchScalarGridSpec(
            num_scalar_prefetch=2,
            grid=(1,),
            in_specs=[ANYWHERE],
            out_specs=ANYWHERE,
            scratch_shapes=[
                VMEM((count,) + rows.shape[1:], F32),
                pltpu.SemaphoreType.DMA((count,)),
                pltpu.SemaphoreType.DMA((count,)),
            ],
        ),
        out_shape=jax.ShapeDtypeStruct((places,) + rows.shape[1:], F32),
        compiler_params=pltpu.CompilerParams(vmem_limit_bytes=56 << 20),
        cost_estimate=pl.CostEstimate(flops=0, bytes_accessed=8_000_000, transcendentals=0),
        name="move_rows",
    )(source, target, rows)


def put_kernel(half, source, rows, *refs):
    out, stage, sems_in, sems_out = refs[-4:]
    part = pl.ds(half * HALF, HALF)
    relay(
        [(rows.at[source[k]], stage.at[k], out.at[k, :, part]) for k in range(stage.shape[0])], sems_in, sems_out
    )


def put_rows(half, source, rows, whole=None):
    count = source.shape[0]
    held = [] if whole is None else [whole]
    return pl.pallas_call(
        functools.partial(put_kernel, half),
        grid_spec=pltpu.PrefetchScalarGridSpec(
            num_scalar_prefetch=1,
            grid=(1,),
            in_specs=[ANYWHERE] * (1 + len(held)),
            out_specs=ANYWHERE,
            scratch_shapes=[
                VMEM((count,) + rows.shape[1:], F32),
                pltpu.SemaphoreType.DMA((count,)),
                pltpu.SemaphoreType.DMA((count,)),
            ],
        ),
        out_shape=jax.ShapeDtypeStruct((count, CWIN, B, B), F32),
        input_output_aliases={2: 0} if held else {},
        compiler_params=pltpu.CompilerParams(vmem_limit_bytes=60 << 20),
        cost_estimate=pl.CostEstimate(flops=0, bytes_accessed=8_000_000, transcendentals=0),
        name="put_rows",
    )(source, rows, *held)


AXES = ("gx", "gy")


def shards(a_tiles, a_cols, a_len, p_tiles, aggregate, owner):
    count_x, count_y = lax.axis_size("gx"), lax.axis_size("gy")
    index_x, index_y = lax.axis_index("gx"), lax.axis_index("gy")
    size = count_x * count_y
    device = index_x * count_y + index_y
    coarse = a_tiles.shape[0] // 3
    depth = coarse // count_x
    place = jnp.reshape(device, (1,)).astype(jnp.int32)
    plan, up, down = make_plan(place, a_cols, a_len, aggregate, owner, a_tiles, p_tiles)
    above = [(i, (i + 1) % size) for i in range(size)]
    below = [(j, i) for i, j in above]
    before = lax.ppermute(up, AXES, above)
    behind = lax.ppermute(down, AXES, below)

    def half_rows(half, places, after):
        rows = main_product(half, plan, a_tiles, p_tiles, places, after)
        return edge_product(half, plan, before, behind, up, down, p_tiles, rows)

    rows_b = half_rows(1, count_y, plan)
    rows_a = half_rows(0, coarse, rows_b)

    table = owner.reshape(count_x, count_y, coarse)
    order = jnp.arange(coarse)
    shift = table[0, 0] // count_y
    same = shift[None, :] == shift[:, None]
    rank = jnp.sum((same & (order[None, :] < order[:, None])).astype(jnp.int32), axis=1)
    slot = (shift * depth + rank).astype(jnp.int32)
    from_x = (index_x - shift) % count_x
    column = table[:, index_y] % count_y
    mid_a_target = jnp.sum(
        jnp.where(jnp.arange(count_x)[:, None] == from_x[None, :], column, 0), axis=0
    ).astype(jnp.int32)
    hit = (table[index_x] % count_y) == index_y
    mid_b_source = jnp.sum(jnp.where(hit, jnp.arange(count_y)[:, None], 0), axis=0).astype(jnp.int32)
    found = table.reshape(size, coarse) == device
    sender = jnp.sum(jnp.where(found, jnp.arange(size)[:, None], 0), axis=0)
    ids = sender * coarse + order
    spot = jnp.sum((ids[None, :] < ids[:, None]).astype(jnp.int32), axis=1)
    at = spot[None, :] == order[:, None]
    last_a = jnp.sum(jnp.where(at, (sender % count_y)[None, :], 0), axis=1).astype(jnp.int32)
    last_b = jnp.sum(jnp.where(at, slot[None, :], 0), axis=1).astype(jnp.int32)

    def over_y(x):
        return lax.all_to_all(x, "gy", split_axis=0, concat_axis=0, tiled=True)

    def along_x(x):
        parts = [x[:depth]]
        for k in range(1, count_x):
            pairs = [(i, (i + k) % count_x) for i in range(count_x)]
            parts.append(lax.ppermute(x[k * depth : (k + 1) * depth], "gx", pairs))
        return jnp.concatenate(parts, axis=0)

    got_b = over_y(rows_b)
    got_a = along_x(rows_a)
    end_a = over_y(move_rows(slot, mid_a_target, got_a, count_y))
    end_b = along_x(move_rows(mid_b_source, slot, got_b, coarse))
    return put_rows(0, last_a, end_a, put_rows(1, last_b, end_b))


def solution(mesh):
    in_specs = (
        P(("gx", "gy"), None, None, None),
        P(("gx", "gy"), None),
        P(("gx", "gy")),
        P(("gx", "gy"), None, None, None),
        P(),
        P(),
    )
    out_specs = P(("gx", "gy"), None, None, None)
    return jax.shard_map(shards, mesh=mesh, in_specs=in_specs, out_specs=out_specs, check_vma=False)
```

```python
import functools

import jax
import jax.numpy as jnp
from jax import lax
from jax.experimental import pallas as pl
from jax.experimental.pallas import tpu as pltpu
from jax.sharding import PartitionSpec as P

B = 128
KP = 2
LANES = 128
CWIN = 7
CB = 16
W = 12
G = W // 3
BF = jnp.bfloat16
F32 = jnp.float32
SMEM = pltpu.SMEM
ANYWHERE = pl.BlockSpec(memory_space=pl.ANY)
VMEM = pltpu.VMEM


LEFT, OUT_LEFT, OUT_RIGHT, SLOTS_AT, PLAN = 64, 128, 192, (256, 272), 384
HALF = B // 2


def split(x):
    high = x.astype(BF)
    return high, (x - high.astype(F32)).astype(BF)


def left_operand(x):
    high, low = split(x)
    return jnp.concatenate([high, low, high], axis=1)


def right_operand(x):
    high, low = split(x)
    return jnp.concatenate([high, high, low], axis=0)


def matmul(left, right):
    return jnp.dot(left, right, preferred_element_type=F32)


def spread(total, flag, base, pair, slots):
    first, second = pair
    values = {
        base - 1: jnp.where(flag, first, 0.0),
        base: jnp.where(flag, second, first),
        base + 1: jnp.where(flag, 0.0, second),
    }
    for s, value in values.items():
        if s in slots:
            total[s] = value if total.get(s) is None else total[s] + value


def turn(p_tile, half):
    return p_tile.T[half * HALF : (half + 1) * HALF]


def row_product(p_pair, tiles, half):
    turned = jnp.concatenate([turn(p_pair[0], half), turn(p_pair[1], half)], axis=0)
    return matmul(left_operand(turned), right_operand(jnp.concatenate(tiles, axis=1)))


SLOTS = {0: (0, 1, 2, 3), 1: (1, 2, 3), 2: (1, 2, 3, 4)}


def main_kernel(
    half, plan,
    a_ref, p_ref, before_ref, after_ref, behind_ref,
    out,
    stage, carry, sems,
):
    step = pl.program_id(0)
    steps = pl.num_programs(0) - 1
    buf = lax.rem(step, 2)

    def copy_out(at, which, row):
        c = G * at - 1 + row
        return pltpu.make_async_copy(stage.at[which, row], out.at[plan[SLOTS_AT[half] + c]], sems.at[which, row])

    def drain(at):
        which = lax.rem(at, 2)
        for row in range(G):
            @pl.when((G * at - 1 + row >= 0) & (G * at - 1 + row < G * steps))
            def _():
                copy_out(at, which, row).wait()

    @pl.when(step >= 2)
    def _():
        drain(step - 2)

    @pl.when(step == 0)
    def _():
        carry[...] = jnp.zeros_like(carry)

    @pl.when(step == steps)
    def _():
        stage[buf, 0] = carry[0]

    @pl.when(step < steps)
    def _():
        sums = {(place, w): carry[place, w] for place in range(2) for w in range(CWIN)}
        first = step * W
        flags = {q: plan[first + q + 4] > 0 for q in range(-1, W + 1)}

        def p_tile(q, m):
            if q < 0:
                return before_ref[0, m]
            if q >= W:
                return after_ref[0, m]
            return p_ref[q, m]

        lefts = {}
        for r in range(W):
            tiles = {
                0: jnp.where(plan[OUT_LEFT + first + r] > 0, a_ref[r, plan[LEFT + first + r]], 0.0),
                1: a_ref[r, 0],
                2: jnp.where(plan[OUT_RIGHT + first + r] > 0, a_ref[r, 3 - plan[LEFT + first + r]], 0.0),
            }
            for k in range(3):
                lefts[r, r + k - 1] = left_operand(tiles[k])
        total = {r: {} for r in range(W)}
        for q in range(-1, W + 1):
            rows = [r for r in (q - 1, q, q + 1) if 0 <= r < W]
            right = right_operand(jnp.concatenate([p_tile(q, 0), p_tile(q, 1)], axis=1))
            product = matmul(jnp.concatenate([lefts[r, q] for r in rows], axis=0), right)
            for n, r in enumerate(rows):
                pair = (product[n * B : (n + 1) * B, :B], product[n * B : (n + 1) * B, B:])
                spread(total[r], flags[q], q // 3 - r // 3 + 2, pair, SLOTS[r % 3])
        for r in range(W):
            slots = SLOTS[r % 3]
            product = row_product((p_ref[r, 0], p_ref[r, 1]), [total[r][s] for s in slots], half)
            g = r // 3
            for n, s in enumerate(slots):
                one = product[:HALF, n * B : (n + 1) * B]
                two = product[HALF:, n * B : (n + 1) * B]
                for delta, value in (
                    (-1, jnp.where(flags[r], one, 0.0)),
                    (0, jnp.where(flags[r], two, one)),
                    (1, jnp.where(flags[r], 0.0, two)),
                ):
                    key = (g + delta + 1, s + 1 - delta)
                    sums[key] = value if key not in sums else sums[key] + value
        for place in range(G + 2):
            for w in range(CWIN):
                value = sums.get((place, w))
                if value is None:
                    value = jnp.zeros((HALF, B), F32)
                if place < G:
                    stage[buf, place, w] = value
                else:
                    carry[place - G, w] = value

    for row in range(G):
        @pl.when((G * step - 1 + row >= 0) & (G * step - 1 + row < G * steps))
        def _():
            copy_out(step, buf, row).start()

    @pl.when(step == steps)
    def _():
        drain(step - 1)
        drain(step)


def main_product(half, plan, a_tiles, p_tiles, places, behind):
    rows = a_tiles.shape[0]
    steps = rows // W
    last = steps - 1

    def spec(shape, index):
        return pl.BlockSpec(shape, index)

    return pl.pallas_call(
        functools.partial(main_kernel, half),
        grid_spec=pltpu.PrefetchScalarGridSpec(
            num_scalar_prefetch=1,
            grid=(steps + 1,),
            in_specs=[
                spec((W, 3, B, B), lambda s, *_: (jnp.minimum(s, last), 0, 0, 0)),
                spec((W, KP, B, B), lambda s, *_: (jnp.minimum(s, last), 0, 0, 0)),
                spec((1, KP, B, B), lambda s, *_: (jnp.maximum(jnp.minimum(s, last) * W - 1, 0), 0, 0, 0)),
                spec((1, KP, B, B), lambda s, *_: (jnp.minimum(s * W + W, rows - 1), 0, 0, 0)),
                ANYWHERE,
            ],
            out_specs=ANYWHERE,
            scratch_shapes=[
                VMEM((2, G, CWIN, HALF, B), F32),
                VMEM((2, CWIN, HALF, B), F32),
                pltpu.SemaphoreType.DMA((2, G)),
            ],
        ),
        out_shape=jax.ShapeDtypeStruct((places, CWIN, HALF, B), F32),
        compiler_params=pltpu.CompilerParams(
            dimension_semantics=("arbitrary",), vmem_limit_bytes=56 << 20
        ),
        cost_estimate=pl.CostEstimate(
            flops=12_000_000_000, bytes_accessed=20_000_000, transcendentals=0
        ),
        name="triple_product",
    )(plan, a_tiles, p_tiles, p_tiles, p_tiles, behind)


def edge_kernel(
    half, plan,
    before, after, a_first, a_last, p_first, p_last, in_rows,
    out_rows,
    rows_ref, sems,
):
    coarse = CB
    held = (0, 1, coarse - 2, coarse - 1)

    def copy(n, back):
        there, here = out_rows.at[plan[SLOTS_AT[half] + held[n]]], rows_ref.at[n]
        if back:
            return pltpu.make_async_copy(there, here, sems.at[n])
        return pltpu.make_async_copy(here, there, sems.at[n])

    for n in range(4):
        copy(n, True).start()

    sums = []
    for side in range(2):
        halo = (before, after)[side]
        a_edge = (a_first, a_last)[side]
        own_p = (p_first, p_last)[side]
        own_flag = plan[(4, 3 * coarse + 3)[side]] > 0
        flags, tiles, p_at = {}, {}, {}
        for n in range(4):
            q = n - 1 if side == 0 else n
            flags[q] = plan[(0, 3 * coarse + 4)[side] + n] > 0
            p_at[q] = (halo[9 + 2 * n], halo[10 + 2 * n])
        near = 3 if side == 0 else -1
        flags[near] = own_flag
        p_at[near] = (own_p[0, 0], own_p[0, 1])
        total = {r: {} for r in range(3)}
        total[near] = {}
        for q in range(-1, 4):
            rows = [r for r in (q - 1, q, q + 1) if 0 <= r < 3]
            lefts = [left_operand(halo[3 * r + q - r + 1]) for r in rows]
            if q == (2 if side == 0 else 0):
                rows.append(near)
                lefts.append(left_operand(a_edge[0]))
            right = right_operand(jnp.concatenate(p_at[q], axis=1))
            product = matmul(jnp.concatenate(lefts, axis=0), right)
            for n, r in enumerate(rows):
                pair = (product[n * B : (n + 1) * B, :B], product[n * B : (n + 1) * B, B:])
                base = q // 3 - r // 3 + 2
                slots = SLOTS[r % 3] if r != near else (base - 1, base, base + 1)
                spread(total[r], flags[q], base, pair, slots)
        outer, inner = {}, {}

        def put(target, w, value):
            target[w] = value if w not in target else target[w] + value

        for r in range(3):
            slots = sorted(total[r])
            pick = 1 if side == 0 else 0
            turned = left_operand(turn(p_at[r][pick], half))
            product = matmul(turned, right_operand(jnp.concatenate([total[r][s] for s in slots], axis=1)))
            for n, s in enumerate(slots):
                value = product[:, n * B : (n + 1) * B]
                if side == 0:
                    put(outer, s, jnp.where(flags[r], 0.0, value))
                else:
                    put(outer, s + 2, jnp.where(flags[r], value, 0.0))
        slots = sorted(total[near])
        product = row_product(p_at[near], [total[near][s] for s in slots], half)
        for n, s in enumerate(slots):
            one = product[:HALF, n * B : (n + 1) * B]
            two = product[HALF:, n * B : (n + 1) * B]
            put(outer, s + 1, jnp.where(own_flag, two, one))
            if side == 0:
                put(inner, s, jnp.where(own_flag, 0.0, two))
            else:
                put(inner, s + 2, jnp.where(own_flag, one, 0.0))
        sums.append((outer, inner))

    for n in range(4):
        copy(n, True).wait()
    for n, target in ((0, sums[0][0]), (1, sums[0][1]), (2, sums[1][1]), (3, sums[1][0])):
        for w, value in target.items():
            rows_ref[n, w] += value
    for n in range(4):
        copy(n, False).start()
    for n in range(4):
        copy(n, False).wait()


def edge_product(half, plan, before, after, up, down, p_tiles, out_rows):
    rows = p_tiles.shape[0]

    def whole(x):
        return pl.BlockSpec(x.shape, lambda *_: (0,) * x.ndim)

    return pl.pallas_call(
        functools.partial(edge_kernel, half),
        grid_spec=pltpu.PrefetchScalarGridSpec(
            num_scalar_prefetch=1,
            grid=(1,),
            in_specs=[whole(before), whole(after)]
            + [
                pl.BlockSpec((1, B, B), lambda *_: (0, 0, 0)),
                pl.BlockSpec((1, B, B), lambda *_: (8, 0, 0)),
                pl.BlockSpec((1, KP, B, B), lambda *_: (0, 0, 0, 0)),
                pl.BlockSpec((1, KP, B, B), lambda *_: (rows - 1, 0, 0, 0)),
            ]
            + [ANYWHERE],
            out_specs=ANYWHERE,
            scratch_shapes=[VMEM((4, CWIN, HALF, B), F32), pltpu.SemaphoreType.DMA((4,))],
        ),
        out_shape=jax.ShapeDtypeStruct(out_rows.shape, F32),
        input_output_aliases={7: 0},
        compiler_params=pltpu.CompilerParams(
            dimension_semantics=("arbitrary",), vmem_limit_bytes=50 << 20
        ),
        cost_estimate=pl.CostEstimate(flops=2_000_000_000, bytes_accessed=10_000_000, transcendentals=0),
        name="edge_rows",
    )(plan, before, after, down, up, p_tiles, p_tiles, out_rows)


def plan_kernel(place, cols, length, a_tiles, p_tiles, aggregate, owners, plan, up, down, near, mine_ref, used, sem):
    fine = length.shape[0]
    coarse = fine // 3
    wide = aggregate.shape[0]
    fine_total = wide * LANES
    first = place[0] * fine
    line = jnp.where(first < 4, wide - 1, (first - 4) >> 7)
    begin = jnp.where(first < 4, LANES - 4, (first - 4) & (LANES - 1))
    lines = (line, jnp.where(line == wide - 1, 0, line + 1))
    index_loads = [
        pltpu.make_async_copy(aggregate.at[pl.ds(at, 1)], near.at[pl.ds(n, 1)], sem.at[n]) for n, at in enumerate(lines)
    ]
    own = place[0] * coarse
    index_loads.append(pltpu.make_async_copy(owners.at[pl.ds(own >> 7, 1)], mine_ref, sem.at[2]))
    for load in index_loads:
        load.start()

    def entry(i):
        before = first + i - 1
        before = jnp.where(before < 0, fine_total - 1, before)
        left = jnp.where(cols[1, i] == before, 1, 2)
        return left, length[i] > left, length[i] > 3 - left

    sends = []
    for out, row, p_row in ((up, fine - 3, fine - 4), (down, 0, 0)):
        for r in range(3):
            left, on_left, on_right = entry(row + r)
            for k, slot, on in ((0, left, on_left), (2, 3 - left, on_right)):
                sends.append((a_tiles.at[row + r, slot], out.at[3 * r + k], on))
            sends.append((a_tiles.at[row + r, 0], out.at[3 * r + 1], None))
        for n in range(4):
            for m in range(KP):
                sends.append((p_tiles.at[p_row + n, m], out.at[9 + 2 * n + m], None))
    for k, (here, there, on) in enumerate(sends):
        if on is None:
            pltpu.make_async_copy(here, there, sem.at[3 + k]).start()
        else:

            @pl.when(on)
            def _():
                pltpu.make_async_copy(here, there, sem.at[3 + k]).start()

            @pl.when(jnp.logical_not(on))
            def _():
                there[...] = jnp.zeros(there.shape, F32)

    def flag(k, carry):
        i = first + k - 4
        i = jnp.where(i < 0, i + fine_total, jnp.where(i >= fine_total, i - fine_total, i))
        at = begin + k
        plan[k] = jnp.where(near[at >> 7, at & (LANES - 1)] != lax.div(i, 3), 1, 0)
        return carry

    for load in index_loads:
        load.wait()
    lax.fori_loop(0, fine + 8, flag, 0, unroll=8)

    def group(g, carry):
        for mod in range(3):
            i = 3 * g + mod
            left, on_left, on_right = entry(i)
            plan[LEFT + i] = left
            plan[OUT_LEFT + i] = jnp.where(on_left & (i > 0), 1, 0)
            plan[OUT_RIGHT + i] = jnp.where(on_right & (i < fine - 1), 1, 0)
        return carry

    lax.fori_loop(0, coarse, group, 0, unroll=4)
    for k in range(4):
        used[k] = 0

    def slot(c, carry):
        mine = mine_ref[0, (own + c) & (LANES - 1)]
        shift = ((mine >> 5) - (place[0] >> 5)) & 3
        plan[SLOTS_AT[0] + c] = shift * (coarse // 4) + used[shift]
        plan[SLOTS_AT[1] + c] = mine & 31
        used[shift] = used[shift] + 1
        return carry

    lax.fori_loop(0, coarse, slot, 0, unroll=4)
    for k, (here, there, on) in enumerate(sends):
        if on is None:
            pltpu.make_async_copy(here, there, sem.at[3 + k]).wait()
        else:

            @pl.when(on)
            def _():
                pltpu.make_async_copy(here, there, sem.at[3 + k]).wait()


def make_plan(place, a_cols, a_len, aggregate, owner, a_tiles, p_tiles):
    fine = a_len.shape[0]
    owners = owner.reshape(-1, LANES)

    def whole(shape):
        return pl.BlockSpec(shape, lambda *_: (0,) * len(shape))

    halo = (9 + 4 * KP, B, B)
    return pl.pallas_call(
        plan_kernel,
        grid_spec=pltpu.PrefetchScalarGridSpec(
            num_scalar_prefetch=3,
            grid=(1,),
            in_specs=[ANYWHERE] * 4,
            out_specs=[
                pl.BlockSpec(memory_space=SMEM),
                whole(halo),
                whole(halo),
            ],
            scratch_shapes=[
                SMEM((2, LANES), jnp.int32),
                SMEM((1, LANES), jnp.int32),
                SMEM((4,), jnp.int32),
                pltpu.SemaphoreType.DMA((3 + 2 * halo[0],)),
            ],
        ),
        out_shape=[
            jax.ShapeDtypeStruct((PLAN,), jnp.int32),
            jax.ShapeDtypeStruct(halo, F32),
            jax.ShapeDtypeStruct(halo, F32),
        ],
        compiler_params=pltpu.CompilerParams(vmem_limit_bytes=60 << 20),
        cost_estimate=pl.CostEstimate(flops=0, bytes_accessed=5_000_000, transcendentals=0),
        name="plan",
    )(place, a_cols.T, a_len, a_tiles, p_tiles, aggregate.reshape(-1, LANES), owners)


def relay(pairs, sems_in, sems_out):
    inward = [pltpu.make_async_copy(x, y, sems_in.at[k]) for k, (x, y, z) in enumerate(pairs)]
    outward = [pltpu.make_async_copy(y, z, sems_out.at[k]) for k, (x, y, z) in enumerate(pairs)]
    for copy in inward:
        copy.start()
    for come, go in zip(inward, outward):
        come.wait()
        go.start()
    for copy in outward:
        copy.wait()


def move_kernel(source_ref, target_ref, rows_in, rows_out, stage, sems_in, sems_out):
    relay(
        [(rows_in.at[source_ref[k]], stage.at[k], rows_out.at[target_ref[k]]) for k in range(stage.shape[0])],
        sems_in,
        sems_out,
    )


def move_rows(source, target, rows, places):
    count = source.shape[0]
    return pl.pallas_call(
        move_kernel,
        grid_spec=pltpu.PrefetchScalarGridSpec(
            num_scalar_prefetch=2,
            grid=(1,),
            in_specs=[ANYWHERE],
            out_specs=ANYWHERE,
            scratch_shapes=[
                VMEM((count,) + rows.shape[1:], F32),
                pltpu.SemaphoreType.DMA((count,)),
                pltpu.SemaphoreType.DMA((count,)),
            ],
        ),
        out_shape=jax.ShapeDtypeStruct((places,) + rows.shape[1:], F32),
        compiler_params=pltpu.CompilerParams(vmem_limit_bytes=56 << 20),
        cost_estimate=pl.CostEstimate(flops=0, bytes_accessed=8_000_000, transcendentals=0),
        name="move_rows",
    )(source, target, rows)


def put_kernel(half, source, rows, *refs):
    out, stage, sems_in, sems_out = refs[-4:]
    part = pl.ds(half * HALF, HALF)
    relay(
        [(rows.at[source[k]], stage.at[k], out.at[k, :, part]) for k in range(stage.shape[0])], sems_in, sems_out
    )


def put_rows(half, source, rows, whole=None):
    count = source.shape[0]
    held = [] if whole is None else [whole]
    return pl.pallas_call(
        functools.partial(put_kernel, half),
        grid_spec=pltpu.PrefetchScalarGridSpec(
            num_scalar_prefetch=1,
            grid=(1,),
            in_specs=[ANYWHERE] * (1 + len(held)),
            out_specs=ANYWHERE,
            scratch_shapes=[
                VMEM((count,) + rows.shape[1:], F32),
                pltpu.SemaphoreType.DMA((count,)),
                pltpu.SemaphoreType.DMA((count,)),
            ],
        ),
        out_shape=jax.ShapeDtypeStruct((count, CWIN, B, B), F32),
        input_output_aliases={2: 0} if held else {},
        compiler_params=pltpu.CompilerParams(vmem_limit_bytes=60 << 20),
        cost_estimate=pl.CostEstimate(flops=0, bytes_accessed=8_000_000, transcendentals=0),
        name="put_rows",
    )(source, rows, *held)


AXES = ("gx", "gy")


def shards(a_tiles, a_cols, a_len, p_tiles, aggregate, owner):
    count_x, count_y = lax.axis_size("gx"), lax.axis_size("gy")
    index_x, index_y = lax.axis_index("gx"), lax.axis_index("gy")
    size = count_x * count_y
    device = index_x * count_y + index_y
    coarse = a_tiles.shape[0] // 3
    depth = coarse // count_x
    place = jnp.reshape(device, (1,)).astype(jnp.int32)
    plan, up, down = make_plan(place, a_cols, a_len, aggregate, owner, a_tiles, p_tiles)
    above = [(i, (i + 1) % size) for i in range(size)]
    below = [(j, i) for i, j in above]
    before = lax.ppermute(up, AXES, above)
    behind = lax.ppermute(down, AXES, below)

    def half_rows(half, places, after):
        rows = main_product(half, plan, a_tiles, p_tiles, places, after)
        return edge_product(half, plan, before, behind, up, down, p_tiles, rows)

    rows_b = half_rows(1, count_y, plan)
    rows_a = half_rows(0, coarse, rows_b)

    table = owner.reshape(count_x, count_y, coarse)
    order = jnp.arange(coarse)
    shift = table[0, 0] // count_y
    same = shift[None, :] == shift[:, None]
    rank = jnp.sum((same & (order[None, :] < order[:, None])).astype(jnp.int32), axis=1)
    slot = (shift * depth + rank).astype(jnp.int32)
    from_x = (index_x - shift) % count_x
    column = table[:, index_y] % count_y
    mid_a_target = jnp.sum(
        jnp.where(jnp.arange(count_x)[:, None] == from_x[None, :], column, 0), axis=0
    ).astype(jnp.int32)
    hit = (table[index_x] % count_y) == index_y
    mid_b_source = jnp.sum(jnp.where(hit, jnp.arange(count_y)[:, None], 0), axis=0).astype(jnp.int32)
    found = table.reshape(size, coarse) == device
    sender = jnp.sum(jnp.where(found, jnp.arange(size)[:, None], 0), axis=0)
    ids = sender * coarse + order
    spot = jnp.sum((ids[None, :] < ids[:, None]).astype(jnp.int32), axis=1)
    at = spot[None, :] == order[:, None]
    last_a = jnp.sum(jnp.where(at, (sender % count_y)[None, :], 0), axis=1).astype(jnp.int32)
    last_b = jnp.sum(jnp.where(at, slot[None, :], 0), axis=1).astype(jnp.int32)

    def over_y(x):
        return lax.all_to_all(x, "gy", split_axis=0, concat_axis=0, tiled=True)

    def along_x(x):
        parts = [x[:depth]]
        for k in range(1, count_x):
            pairs = [(i, (i + k) % count_x) for i in range(count_x)]
            parts.append(lax.ppermute(x[k * depth : (k + 1) * depth], "gx", pairs))
        return jnp.concatenate(parts, axis=0)

    got_b = over_y(rows_b)
    got_a = along_x(rows_a)
    end_a = over_y(move_rows(slot, mid_a_target, got_a, count_y))
    end_b = along_x(move_rows(mid_b_source, slot, got_b, coarse))
    return put_rows(0, last_a, end_a, put_rows(1, last_b, end_b))


def solution(mesh):
    in_specs = (
        P(("gx", "gy"), None, None, None),
        P(("gx", "gy"), None),
        P(("gx", "gy")),
        P(("gx", "gy"), None, None, None),
        P(),
        P(),
    )
    out_specs = P(("gx", "gy"), None, None, None)
    return jax.shard_map(shards, mesh=mesh, in_specs=in_specs, out_specs=out_specs, check_vma=False)
```

```python
import functools

import jax
import jax.numpy as jnp
from jax import lax
from jax.experimental import pallas as pl
from jax.experimental.pallas import tpu as pltpu
from jax.sharding import PartitionSpec as P

B = 128
KP = 2
LANES = 128
CWIN = 7
CB = 16
W = 12
G = W // 3
BF = jnp.bfloat16
F32 = jnp.float32
SMEM = pltpu.SMEM
ANYWHERE = pl.BlockSpec(memory_space=pl.ANY)
VMEM = pltpu.VMEM


LEFT, OUT_LEFT, OUT_RIGHT, SLOTS_AT, PLAN = 64, 128, 192, (256, 272), 384
HALF = B // 2


def split(x):
    high = x.astype(BF)
    return high, (x - high.astype(F32)).astype(BF)


def left_operand(x):
    high, low = split(x)
    return jnp.concatenate([high, low, high], axis=1)


def right_operand(x):
    high, low = split(x)
    return jnp.concatenate([high, high, low], axis=0)


def matmul(left, right):
    return jnp.dot(left, right, preferred_element_type=F32)


def spread(total, flag, base, pair, slots):
    first, second = pair
    values = {
        base - 1: jnp.where(flag, first, 0.0),
        base: jnp.where(flag, second, first),
        base + 1: jnp.where(flag, 0.0, second),
    }
    for s, value in values.items():
        if s in slots:
            total[s] = value if total.get(s) is None else total[s] + value


def turn(p_tile, half):
    return p_tile.T[half * HALF : (half + 1) * HALF]


def row_product(p_pair, tiles, half):
    part = slice(half * HALF, (half + 1) * HALF)
    turned = jnp.concatenate([p_pair[0][:, part], p_pair[1][:, part]], axis=1).T
    return matmul(left_operand(turned), right_operand(jnp.concatenate(tiles, axis=1)))


SLOTS = {0: (0, 1, 2, 3), 1: (1, 2, 3), 2: (1, 2, 3, 4)}


def main_kernel(
    half, plan,
    a_ref, p_ref, before_ref, after_ref, behind_ref,
    out,
    stage, carry, sems,
):
    step = pl.program_id(0)
    steps = pl.num_programs(0) - 1
    buf = lax.rem(step, 2)

    def copy_out(at, which, row):
        c = G * at - 1 + row
        return pltpu.make_async_copy(stage.at[which, row], out.at[plan[SLOTS_AT[half] + c]], sems.at[which, row])

    def drain(at):
        which = lax.rem(at, 2)
        for row in range(G):
            @pl.when((G * at - 1 + row >= 0) & (G * at - 1 + row < G * steps))
            def _():
                copy_out(at, which, row).wait()

    @pl.when(step >= 2)
    def _():
        drain(step - 2)

    @pl.when(step == 0)
    def _():
        carry[...] = jnp.zeros_like(carry)

    @pl.when(step == steps)
    def _():
        stage[buf, 0] = carry[0]

    @pl.when(step < steps)
    def _():
        sums = {(place, w): carry[place, w] for place in range(2) for w in range(CWIN)}
        first = step * W
        flags = {q: plan[first + q + 4] > 0 for q in range(-1, W + 1)}

        def p_tile(q, m):
            if q < 0:
                return before_ref[0, m]
            if q >= W:
                return after_ref[0, m]
            return p_ref[q, m]

        lefts = {}
        for r in range(W):
            tiles = {
                0: jnp.where(plan[OUT_LEFT + first + r] > 0, a_ref[r, plan[LEFT + first + r]], 0.0),
                1: a_ref[r, 0],
                2: jnp.where(plan[OUT_RIGHT + first + r] > 0, a_ref[r, 3 - plan[LEFT + first + r]], 0.0),
            }
            for k in range(3):
                lefts[r, r + k - 1] = left_operand(tiles[k])
        total = {r: {} for r in range(W)}
        for q in range(-1, W + 1):
            rows = [r for r in (q - 1, q, q + 1) if 0 <= r < W]
            right = right_operand(jnp.concatenate([p_tile(q, 0), p_tile(q, 1)], axis=1))
            product = matmul(jnp.concatenate([lefts[r, q] for r in rows], axis=0), right)
            for n, r in enumerate(rows):
                pair = (product[n * B : (n + 1) * B, :B], product[n * B : (n + 1) * B, B:])
                spread(total[r], flags[q], q // 3 - r // 3 + 2, pair, SLOTS[r % 3])
        for r in range(W):
            slots = SLOTS[r % 3]
            product = row_product((p_ref[r, 0], p_ref[r, 1]), [total[r][s] for s in slots], half)
            g = r // 3
            for n, s in enumerate(slots):
                one = product[:HALF, n * B : (n + 1) * B]
                two = product[HALF:, n * B : (n + 1) * B]
                for delta, value in (
                    (-1, jnp.where(flags[r], one, 0.0)),
                    (0, jnp.where(flags[r], two, one)),
                    (1, jnp.where(flags[r], 0.0, two)),
                ):
                    key = (g + delta + 1, s + 1 - delta)
                    sums[key] = value if key not in sums else sums[key] + value
        for place in range(G + 2):
            for w in range(CWIN):
                value = sums.get((place, w))
                if value is None:
                    value = jnp.zeros((HALF, B), F32)
                if place < G:
                    stage[buf, place, w] = value
                else:
                    carry[place - G, w] = value

    for row in range(G):
        @pl.when((G * step - 1 + row >= 0) & (G * step - 1 + row < G * steps))
        def _():
            copy_out(step, buf, row).start()

    @pl.when(step == steps)
    def _():
        drain(step - 1)
        drain(step)


def main_product(half, plan, a_tiles, p_tiles, places, behind):
    rows = a_tiles.shape[0]
    steps = rows // W
    last = steps - 1

    def spec(shape, index):
        return pl.BlockSpec(shape, index)

    return pl.pallas_call(
        functools.partial(main_kernel, half),
        grid_spec=pltpu.PrefetchScalarGridSpec(
            num_scalar_prefetch=1,
            grid=(steps + 1,),
            in_specs=[
                spec((W, 3, B, B), lambda s, *_: (jnp.minimum(s, last), 0, 0, 0)),
                spec((W, KP, B, B), lambda s, *_: (jnp.minimum(s, last), 0, 0, 0)),
                spec((1, KP, B, B), lambda s, *_: (jnp.maximum(jnp.minimum(s, last) * W - 1, 0), 0, 0, 0)),
                spec((1, KP, B, B), lambda s, *_: (jnp.minimum(s * W + W, rows - 1), 0, 0, 0)),
                ANYWHERE,
            ],
            out_specs=ANYWHERE,
            scratch_shapes=[
                VMEM((2, G, CWIN, HALF, B), F32),
                VMEM((2, CWIN, HALF, B), F32),
                pltpu.SemaphoreType.DMA((2, G)),
            ],
        ),
        out_shape=jax.ShapeDtypeStruct((places, CWIN, HALF, B), F32),
        compiler_params=pltpu.CompilerParams(
            dimension_semantics=("arbitrary",), vmem_limit_bytes=56 << 20
        ),
        cost_estimate=pl.CostEstimate(
            flops=12_000_000_000, bytes_accessed=20_000_000, transcendentals=0
        ),
        name="triple_product",
    )(plan, a_tiles, p_tiles, p_tiles, p_tiles, behind)


def edge_kernel(
    half, plan,
    before, after, a_first, a_last, p_first, p_last, in_rows,
    out_rows,
    rows_ref, sems,
):
    coarse = CB
    held = (0, 1, coarse - 2, coarse - 1)

    def copy(n, back):
        there, here = out_rows.at[plan[SLOTS_AT[half] + held[n]]], rows_ref.at[n]
        if back:
            return pltpu.make_async_copy(there, here, sems.at[n])
        return pltpu.make_async_copy(here, there, sems.at[n])

    for n in range(4):
        copy(n, True).start()

    sums = []
    for side in range(2):
        halo = (before, after)[side]
        a_edge = (a_first, a_last)[side]
        own_p = (p_first, p_last)[side]
        own_flag = plan[(4, 3 * coarse + 3)[side]] > 0
        flags, tiles, p_at = {}, {}, {}
        for n in range(4):
            q = n - 1 if side == 0 else n
            flags[q] = plan[(0, 3 * coarse + 4)[side] + n] > 0
            p_at[q] = (halo[9 + 2 * n], halo[10 + 2 * n])
        near = 3 if side == 0 else -1
        flags[near] = own_flag
        p_at[near] = (own_p[0, 0], own_p[0, 1])
        total = {r: {} for r in range(3)}
        total[near] = {}
        for q in range(-1, 4):
            rows = [r for r in (q - 1, q, q + 1) if 0 <= r < 3]
            lefts = [left_operand(halo[3 * r + q - r + 1]) for r in rows]
            if q == (2 if side == 0 else 0):
                rows.append(near)
                lefts.append(left_operand(a_edge[0]))
            right = right_operand(jnp.concatenate(p_at[q], axis=1))
            product = matmul(jnp.concatenate(lefts, axis=0), right)
            for n, r in enumerate(rows):
                pair = (product[n * B : (n + 1) * B, :B], product[n * B : (n + 1) * B, B:])
                base = q // 3 - r // 3 + 2
                slots = SLOTS[r % 3] if r != near else (base - 1, base, base + 1)
                spread(total[r], flags[q], base, pair, slots)
        outer, inner = {}, {}

        def put(target, w, value):
            target[w] = value if w not in target else target[w] + value

        for r in range(3):
            slots = sorted(total[r])
            pick = 1 if side == 0 else 0
            turned = left_operand(turn(p_at[r][pick], half))
            product = matmul(turned, right_operand(jnp.concatenate([total[r][s] for s in slots], axis=1)))
            for n, s in enumerate(slots):
                value = product[:, n * B : (n + 1) * B]
                if side == 0:
                    put(outer, s, jnp.where(flags[r], 0.0, value))
                else:
                    put(outer, s + 2, jnp.where(flags[r], value, 0.0))
        slots = sorted(total[near])
        product = row_product(p_at[near], [total[near][s] for s in slots], half)
        for n, s in enumerate(slots):
            one = product[:HALF, n * B : (n + 1) * B]
            two = product[HALF:, n * B : (n + 1) * B]
            put(outer, s + 1, jnp.where(own_flag, two, one))
            if side == 0:
                put(inner, s, jnp.where(own_flag, 0.0, two))
            else:
                put(inner, s + 2, jnp.where(own_flag, one, 0.0))
        sums.append((outer, inner))

    for n in range(4):
        copy(n, True).wait()
    for n, target in ((0, sums[0][0]), (1, sums[0][1]), (2, sums[1][1]), (3, sums[1][0])):
        for w, value in target.items():
            rows_ref[n, w] += value
    for n in range(4):
        copy(n, False).start()
    for n in range(4):
        copy(n, False).wait()


def edge_product(half, plan, before, after, up, down, p_tiles, out_rows):
    rows = p_tiles.shape[0]

    def whole(x):
        return pl.BlockSpec(x.shape, lambda *_: (0,) * x.ndim)

    return pl.pallas_call(
        functools.partial(edge_kernel, half),
        grid_spec=pltpu.PrefetchScalarGridSpec(
            num_scalar_prefetch=1,
            grid=(1,),
            in_specs=[whole(before), whole(after)]
            + [
                pl.BlockSpec((1, B, B), lambda *_: (0, 0, 0)),
                pl.BlockSpec((1, B, B), lambda *_: (8, 0, 0)),
                pl.BlockSpec((1, KP, B, B), lambda *_: (0, 0, 0, 0)),
                pl.BlockSpec((1, KP, B, B), lambda *_: (rows - 1, 0, 0, 0)),
            ]
            + [ANYWHERE],
            out_specs=ANYWHERE,
            scratch_shapes=[VMEM((4, CWIN, HALF, B), F32), pltpu.SemaphoreType.DMA((4,))],
        ),
        out_shape=jax.ShapeDtypeStruct(out_rows.shape, F32),
        input_output_aliases={7: 0},
        compiler_params=pltpu.CompilerParams(
            dimension_semantics=("arbitrary",), vmem_limit_bytes=50 << 20
        ),
        cost_estimate=pl.CostEstimate(flops=2_000_000_000, bytes_accessed=10_000_000, transcendentals=0),
        name="edge_rows",
    )(plan, before, after, down, up, p_tiles, p_tiles, out_rows)


def plan_kernel(place, cols, length, a_tiles, p_tiles, aggregate, owners, plan, up, down, near, mine_ref, used, sem):
    fine = length.shape[0]
    coarse = fine // 3
    wide = aggregate.shape[0]
    fine_total = wide * LANES
    first = place[0] * fine
    line = jnp.where(first < 4, wide - 1, (first - 4) >> 7)
    begin = jnp.where(first < 4, LANES - 4, (first - 4) & (LANES - 1))
    lines = (line, jnp.where(line == wide - 1, 0, line + 1))
    index_loads = [
        pltpu.make_async_copy(aggregate.at[pl.ds(at, 1)], near.at[pl.ds(n, 1)], sem.at[n]) for n, at in enumerate(lines)
    ]
    own = place[0] * coarse
    index_loads.append(pltpu.make_async_copy(owners.at[pl.ds(own >> 7, 1)], mine_ref, sem.at[2]))
    for load in index_loads:
        load.start()

    def entry(i):
        before = first + i - 1
        before = jnp.where(before < 0, fine_total - 1, before)
        left = jnp.where(cols[1, i] == before, 1, 2)
        return left, length[i] > left, length[i] > 3 - left

    sends = []
    for out, row, p_row in ((up, fine - 3, fine - 4), (down, 0, 0)):
        for r in range(3):
            left, on_left, on_right = entry(row + r)
            for k, slot, on in ((0, left, on_left), (2, 3 - left, on_right)):
                sends.append((a_tiles.at[row + r, slot], out.at[3 * r + k], on))
            sends.append((a_tiles.at[row + r, 0], out.at[3 * r + 1], None))
        for n in range(4):
            for m in range(KP):
                sends.append((p_tiles.at[p_row + n, m], out.at[9 + 2 * n + m], None))
    for k, (here, there, on) in enumerate(sends):
        if on is None:
            pltpu.make_async_copy(here, there, sem.at[3 + k]).start()
        else:

            @pl.when(on)
            def _():
                pltpu.make_async_copy(here, there, sem.at[3 + k]).start()

            @pl.when(jnp.logical_not(on))
            def _():
                there[...] = jnp.zeros(there.shape, F32)

    def flag(k, carry):
        i = first + k - 4
        i = jnp.where(i < 0, i + fine_total, jnp.where(i >= fine_total, i - fine_total, i))
        at = begin + k
        plan[k] = jnp.where(near[at >> 7, at & (LANES - 1)] != lax.div(i, 3), 1, 0)
        return carry

    for load in index_loads:
        load.wait()
    lax.fori_loop(0, fine + 8, flag, 0, unroll=8)

    def group(g, carry):
        for mod in range(3):
            i = 3 * g + mod
            left, on_left, on_right = entry(i)
            plan[LEFT + i] = left
            plan[OUT_LEFT + i] = jnp.where(on_left & (i > 0), 1, 0)
            plan[OUT_RIGHT + i] = jnp.where(on_right & (i < fine - 1), 1, 0)
        return carry

    lax.fori_loop(0, coarse, group, 0, unroll=4)
    for k in range(4):
        used[k] = 0

    def slot(c, carry):
        mine = mine_ref[0, (own + c) & (LANES - 1)]
        shift = ((mine >> 5) - (place[0] >> 5)) & 3
        plan[SLOTS_AT[0] + c] = shift * (coarse // 4) + used[shift]
        plan[SLOTS_AT[1] + c] = mine & 31
        used[shift] = used[shift] + 1
        return carry

    lax.fori_loop(0, coarse, slot, 0, unroll=4)
    for k, (here, there, on) in enumerate(sends):
        if on is None:
            pltpu.make_async_copy(here, there, sem.at[3 + k]).wait()
        else:

            @pl.when(on)
            def _():
                pltpu.make_async_copy(here, there, sem.at[3 + k]).wait()


def make_plan(place, a_cols, a_len, aggregate, owner, a_tiles, p_tiles):
    fine = a_len.shape[0]
    owners = owner.reshape(-1, LANES)

    def whole(shape):
        return pl.BlockSpec(shape, lambda *_: (0,) * len(shape))

    halo = (9 + 4 * KP, B, B)
    return pl.pallas_call(
        plan_kernel,
        grid_spec=pltpu.PrefetchScalarGridSpec(
            num_scalar_prefetch=3,
            grid=(1,),
            in_specs=[ANYWHERE] * 4,
            out_specs=[
                pl.BlockSpec(memory_space=SMEM),
                whole(halo),
                whole(halo),
            ],
            scratch_shapes=[
                SMEM((2, LANES), jnp.int32),
                SMEM((1, LANES), jnp.int32),
                SMEM((4,), jnp.int32),
                pltpu.SemaphoreType.DMA((3 + 2 * halo[0],)),
            ],
        ),
        out_shape=[
            jax.ShapeDtypeStruct((PLAN,), jnp.int32),
            jax.ShapeDtypeStruct(halo, F32),
            jax.ShapeDtypeStruct(halo, F32),
        ],
        compiler_params=pltpu.CompilerParams(vmem_limit_bytes=60 << 20),
        cost_estimate=pl.CostEstimate(flops=0, bytes_accessed=5_000_000, transcendentals=0),
        name="plan",
    )(place, a_cols.T, a_len, a_tiles, p_tiles, aggregate.reshape(-1, LANES), owners)


def relay(pairs, sems_in, sems_out):
    inward = [pltpu.make_async_copy(x, y, sems_in.at[k]) for k, (x, y, z) in enumerate(pairs)]
    outward = [pltpu.make_async_copy(y, z, sems_out.at[k]) for k, (x, y, z) in enumerate(pairs)]
    for copy in inward:
        copy.start()
    for come, go in zip(inward, outward):
        come.wait()
        go.start()
    for copy in outward:
        copy.wait()


def move_kernel(source_ref, target_ref, rows_in, rows_out, stage, sems_in, sems_out):
    relay(
        [(rows_in.at[source_ref[k]], stage.at[k], rows_out.at[target_ref[k]]) for k in range(stage.shape[0])],
        sems_in,
        sems_out,
    )


def move_rows(source, target, rows, places):
    count = source.shape[0]
    return pl.pallas_call(
        move_kernel,
        grid_spec=pltpu.PrefetchScalarGridSpec(
            num_scalar_prefetch=2,
            grid=(1,),
            in_specs=[ANYWHERE],
            out_specs=ANYWHERE,
            scratch_shapes=[
                VMEM((count,) + rows.shape[1:], F32),
                pltpu.SemaphoreType.DMA((count,)),
                pltpu.SemaphoreType.DMA((count,)),
            ],
        ),
        out_shape=jax.ShapeDtypeStruct((places,) + rows.shape[1:], F32),
        compiler_params=pltpu.CompilerParams(vmem_limit_bytes=56 << 20),
        cost_estimate=pl.CostEstimate(flops=0, bytes_accessed=8_000_000, transcendentals=0),
        name="move_rows",
    )(source, target, rows)


def put_kernel(half, source, rows, *refs):
    out, stage, sems_in, sems_out = refs[-4:]
    part = pl.ds(half * HALF, HALF)
    relay(
        [(rows.at[source[k]], stage.at[k], out.at[k, :, part]) for k in range(stage.shape[0])], sems_in, sems_out
    )


def put_rows(half, source, rows, whole=None):
    count = source.shape[0]
    held = [] if whole is None else [whole]
    return pl.pallas_call(
        functools.partial(put_kernel, half),
        grid_spec=pltpu.PrefetchScalarGridSpec(
            num_scalar_prefetch=1,
            grid=(1,),
            in_specs=[ANYWHERE] * (1 + len(held)),
            out_specs=ANYWHERE,
            scratch_shapes=[
                VMEM((count,) + rows.shape[1:], F32),
                pltpu.SemaphoreType.DMA((count,)),
                pltpu.SemaphoreType.DMA((count,)),
            ],
        ),
        out_shape=jax.ShapeDtypeStruct((count, CWIN, B, B), F32),
        input_output_aliases={2: 0} if held else {},
        compiler_params=pltpu.CompilerParams(vmem_limit_bytes=60 << 20),
        cost_estimate=pl.CostEstimate(flops=0, bytes_accessed=8_000_000, transcendentals=0),
        name="put_rows",
    )(source, rows, *held)


AXES = ("gx", "gy")


def shards(a_tiles, a_cols, a_len, p_tiles, aggregate, owner):
    count_x, count_y = lax.axis_size("gx"), lax.axis_size("gy")
    index_x, index_y = lax.axis_index("gx"), lax.axis_index("gy")
    size = count_x * count_y
    device = index_x * count_y + index_y
    coarse = a_tiles.shape[0] // 3
    depth = coarse // count_x
    place = jnp.reshape(device, (1,)).astype(jnp.int32)
    plan, up, down = make_plan(place, a_cols, a_len, aggregate, owner, a_tiles, p_tiles)
    above = [(i, (i + 1) % size) for i in range(size)]
    below = [(j, i) for i, j in above]
    before = lax.ppermute(up, AXES, above)
    behind = lax.ppermute(down, AXES, below)

    def half_rows(half, places, after):
        rows = main_product(half, plan, a_tiles, p_tiles, places, after)
        return edge_product(half, plan, before, behind, up, down, p_tiles, rows)

    rows_b = half_rows(1, count_y, plan)
    rows_a = half_rows(0, coarse, rows_b)

    table = owner.reshape(count_x, count_y, coarse)
    order = jnp.arange(coarse)
    shift = table[0, 0] // count_y
    same = shift[None, :] == shift[:, None]
    rank = jnp.sum((same & (order[None, :] < order[:, None])).astype(jnp.int32), axis=1)
    slot = (shift * depth + rank).astype(jnp.int32)
    from_x = (index_x - shift) % count_x
    column = table[:, index_y] % count_y
    mid_a_target = jnp.sum(
        jnp.where(jnp.arange(count_x)[:, None] == from_x[None, :], column, 0), axis=0
    ).astype(jnp.int32)
    hit = (table[index_x] % count_y) == index_y
    mid_b_source = jnp.sum(jnp.where(hit, jnp.arange(count_y)[:, None], 0), axis=0).astype(jnp.int32)
    found = table.reshape(size, coarse) == device
    sender = jnp.sum(jnp.where(found, jnp.arange(size)[:, None], 0), axis=0)
    ids = sender * coarse + order
    spot = jnp.sum((ids[None, :] < ids[:, None]).astype(jnp.int32), axis=1)
    at = spot[None, :] == order[:, None]
    last_a = jnp.sum(jnp.where(at, (sender % count_y)[None, :], 0), axis=1).astype(jnp.int32)
    last_b = jnp.sum(jnp.where(at, slot[None, :], 0), axis=1).astype(jnp.int32)

    def over_y(x):
        return lax.all_to_all(x, "gy", split_axis=0, concat_axis=0, tiled=True)

    def along_x(x):
        parts = [x[:depth]]
        for k in range(1, count_x):
            pairs = [(i, (i + k) % count_x) for i in range(count_x)]
            parts.append(lax.ppermute(x[k * depth : (k + 1) * depth], "gx", pairs))
        return jnp.concatenate(parts, axis=0)

    got_b = over_y(rows_b)
    got_a = along_x(rows_a)
    end_a = over_y(move_rows(slot, mid_a_target, got_a, count_y))
    end_b = along_x(move_rows(mid_b_source, slot, got_b, coarse))
    return put_rows(0, last_a, end_a, put_rows(1, last_b, end_b))


def solution(mesh):
    in_specs = (
        P(("gx", "gy"), None, None, None),
        P(("gx", "gy"), None),
        P(("gx", "gy")),
        P(("gx", "gy"), None, None, None),
        P(),
        P(),
    )
    out_specs = P(("gx", "gy"), None, None, None)
    return jax.shard_map(shards, mesh=mesh, in_specs=in_specs, out_specs=out_specs, check_vma=False)
```
